256 devices in a mesh: ha: 8 (over y, x_lo), wa: 32 (over x_hi, z, core).
Axes of the slice: x: 4 (x_hi: 2, x_lo: 2; x = x_hi * 2 + x_lo), y: 4, z: 8, core: 2. Of those that a mesh axis runs over, the one named last changes fastest.
Arguments:
- query_field: float32 [2, 128, 128, 256], P(None, 'ha', 'wa'), may hold values from -150 to 150, as said below
- key_field: float32 [2, 128, 128, 256], P(None, 'ha', 'wa'), may hold values from -6 to 6
- value_field: float32 [2, 128, 128, 256], P(None, 'ha', 'wa'), may hold values from -6 to 6
- output_grad: float32 [2, 128, 128, 256], P(None, 'ha', 'wa'), may hold values from -6 to 6
Outputs:
- query_grad: float32 [2, 128, 128, 256], P(None, 'ha', 'wa')
- key_grad: float32 [2, 128, 128, 256], P(None, 'ha', 'wa')
- value_grad: float32 [2, 128, 128, 256], P(None, 'ha', 'wa')
The draws below stay inside these ranges and needn't reach their ends.
Inputs may be any that keep to these rules, and one draw needn't show every extreme that they name: `query_field`: queries and keys are real-valued with no structure promised.
All inputs are finite; a program needn't handle non-finite values.
Results may differ from the reference program's by a relative error of at most 0.0003.
Values sent between devices are 32-bit elements; how exact they have to be, the bound alone decides.
A program may use at most 128 MiB of HBM per device.

```python
import jax
import jax.numpy as jnp
from jax import lax

FRAMES = 2
HEADS = 2
HEAD_DIM = 128
TILE = 16
CHANNELS = 256
HEIGHT = 128
WIDTH = 128


def draw_common(base):
    shape = (FRAMES, HEIGHT, WIDTH, CHANNELS)
    key_base = jnp.clip(jax.random.normal(jax.random.fold_in(base, 11), shape, jnp.float32), -6.0, 6.0)
    query_base = jnp.clip(jax.random.normal(jax.random.fold_in(base, 12), shape, jnp.float32), -6.0, 6.0)
    return (query_base, key_base)


def draw_query_field(key, part):
    return draw_common(jax.random.fold_in(key, 5))[0]


def draw_key_field(key, part):
    return draw_common(jax.random.fold_in(key, 5))[1]


def shard_levels(own_key, extent, shards, least, largest):
    level, own = 1.0, jax.random.fold_in(own_key, 6)
    for position, parts in shards:
        draws = jnp.exp(jax.random.uniform(jax.random.fold_in(own, position), (parts,), jnp.float32, least / len(shards), largest / len(shards)))
        level = level * jnp.repeat(draws, extent[position] // parts).reshape([-1 if axis == position else 1 for axis in range(len(extent))])
    return level


def bell_draw(key, dims, scale, reach, shards=(), held_as=jnp.bfloat16):
    values = scale * jax.random.normal(key, dims, jnp.float32)
    if shards:
        values = values * shard_levels(key, dims, shards, -0.22, 0.18)
    return jnp.clip(values, -reach, reach).astype(held_as)


def setup_inputs(seed: int = 0) -> dict:
    seeds = jax.random.split(jax.random.key(seed), 5)
    return {
        "query_field": draw_query_field(jax.random.fold_in(seeds[4], 71), 0),
        "key_field": draw_key_field(jax.random.fold_in(seeds[4], 71), 0),
        "value_field": bell_draw(seeds[2], (FRAMES, HEIGHT, WIDTH, CHANNELS), 1.0, 6.0, ((1, 8), (2, 32)), jnp.float32),
        "output_grad": bell_draw(seeds[3], (FRAMES, HEIGHT, WIDTH, CHANNELS), 1.0, 6.0, ((1, 8), (2, 32)), jnp.float32),
    }


def tile_grads(query_rows, grad_rows, key_rows, value_rows, key_valid):
    score_scale = HEAD_DIM ** -0.5
    highest = lax.Precision.HIGHEST
    mask_bias = jnp.where(key_valid, jnp.float32(0.0), jnp.float32(-1e30))
    query_parts = []
    key_parts = []
    value_parts = []
    for head_index in range(HEADS):
        head_start = head_index * HEAD_DIM
        head_stop = head_start + HEAD_DIM
        query_scaled = query_rows[:, head_start:head_stop] * score_scale
        grad_head = grad_rows[:, head_start:head_stop]
        key_head = key_rows[:, head_start:head_stop]
        value_head = value_rows[:, head_start:head_stop]
        scores = jnp.dot(query_scaled, key_head.T, precision=highest) + mask_bias[None, :]
        row_peak = jnp.max(scores, axis=1, keepdims=True)
        weights = jnp.exp(scores - row_peak)
        inverse = 1.0 / jnp.sum(weights, axis=1, keepdims=True)
        probabilities = weights * inverse
        dprobs = jnp.dot(grad_head, value_head.T, precision=highest)
        center = jnp.sum(probabilities * dprobs, axis=1, keepdims=True)
        dscores = probabilities * (dprobs - center)
        query_parts.append(jnp.dot(dscores, key_head, precision=highest) * score_scale)
        key_parts.append(jnp.dot(dscores.T, query_scaled, precision=highest))
        value_parts.append(jnp.dot(probabilities.T, grad_head, precision=highest))
    return (jnp.concatenate(query_parts, axis=1), jnp.concatenate(key_parts, axis=1),
            jnp.concatenate(value_parts, axis=1))


def reference(query_field, key_field, value_field, output_grad):
    tiles_high = HEIGHT // TILE
    tiles_wide = WIDTH // TILE
    padding = ((0, 0), (TILE, TILE), (TILE, TILE), (0, 0))
    key_padded = jnp.pad(key_field, padding)
    value_padded = jnp.pad(value_field, padding)
    window_span = jnp.arange(3 * TILE, dtype=jnp.int32)
    window_shape = (FRAMES, 3 * TILE, 3 * TILE, CHANNELS)

    def visit(carry, tile_number):
        key_acc, value_acc = carry
        tile_row = tile_number // tiles_wide
        tile_col = tile_number % tiles_wide
        row_start = (tile_row * TILE).astype(jnp.int32)
        col_start = (tile_col * TILE).astype(jnp.int32)
        anchor = jnp.int32(0)
        where_tile = (anchor, row_start, col_start, anchor)
        query_rows = lax.dynamic_slice(query_field, where_tile, (FRAMES, TILE, TILE, CHANNELS)).reshape(-1, CHANNELS)
        grad_rows = lax.dynamic_slice(output_grad, where_tile, (FRAMES, TILE, TILE, CHANNELS)).reshape(-1, CHANNELS)
        key_rows = lax.dynamic_slice(key_padded, where_tile, window_shape).reshape(-1, CHANNELS)
        value_rows = lax.dynamic_slice(value_padded, where_tile, window_shape).reshape(-1, CHANNELS)
        rows_global = row_start - TILE + window_span
        cols_global = col_start - TILE + window_span
        row_ok = (rows_global >= 0) & (rows_global < HEIGHT)
        col_ok = (cols_global >= 0) & (cols_global < WIDTH)
        plane_ok = row_ok[:, None] & col_ok[None, :]
        key_valid = jnp.broadcast_to(plane_ok[None], (FRAMES, 3 * TILE, 3 * TILE)).reshape(-1)
        query_part, key_part, value_part = tile_grads(query_rows, grad_rows, key_rows, value_rows, key_valid)
        key_acc = lax.dynamic_update_slice(
            key_acc, lax.dynamic_slice(key_acc, where_tile, window_shape) + key_part.reshape(window_shape), where_tile)
        value_acc = lax.dynamic_update_slice(
            value_acc, lax.dynamic_slice(value_acc, where_tile, window_shape) + value_part.reshape(window_shape), where_tile)
        return (key_acc, value_acc), query_part.reshape(FRAMES, TILE, TILE, CHANNELS)

    empty = jnp.zeros(key_padded.shape, jnp.float32)
    numbers = jnp.arange(tiles_high * tiles_wide, dtype=jnp.int32)
    (key_acc, value_acc), query_tiles = lax.scan(visit, (empty, empty), numbers)
    query_grad = query_tiles.reshape(tiles_high, tiles_wide, FRAMES, TILE, TILE, CHANNELS)
    query_grad = query_grad.transpose(2, 0, 3, 1, 4, 5).reshape(FRAMES, HEIGHT, WIDTH, CHANNELS)
    key_grad = key_acc[:, TILE:TILE + HEIGHT, TILE:TILE + WIDTH]
    value_grad = value_acc[:, TILE:TILE + HEIGHT, TILE:TILE + WIDTH]
    return query_grad, key_grad, value_grad
```

```python
import jax
import jax.numpy as jnp
from jax import lax
from jax.experimental import pallas as pl
from jax.experimental.pallas import tpu as pltpu
from jax.sharding import PartitionSpec as P

MESH = pl.DeviceIdType.MESH
F32 = jnp.float32
BF16 = jnp.bfloat16
DIM = 128
SCALE = DIM ** -0.5
LOW = -1e30
CELLS = 128
UNIT = 2 * CELLS
HALF = 2 * UNIT


def halves(x):
    hi = x.astype(BF16)
    return hi, (x - hi.astype(F32)).astype(BF16)


def thirds(x):
    hi = x.astype(BF16)
    rest = x - hi.astype(F32)
    mid = rest.astype(BF16)
    return hi, mid, (rest - mid.astype(F32)).astype(BF16)


def dot(a, b, dims):
    return lax.dot_general(a, b, (dims, ((), ())), preferred_element_type=F32)


def kernel(
    x_ref, out_ref,
    sib, kvb, qb, kp, rq, ro, wbuf, dbuf, st, sall, gst, dqt, dqr, own, halo, yret, zret, fin, fout,
    core_sem, near_sem, far_sem, y_sem, zq_sem, xq_sem, stat_sem, yr_sem, zr_sem, dq_sem, fin_sem,
):
    ha, wa = lax.axis_index("ha"), lax.axis_index("wa")
    row, xl = ha // 2, ha % 2
    core = wa % 2
    chip = wa // 2
    zp = chip % 2
    tile = chip // 2
    side = 2 * zp - 1
    up = 2 * xl - 1

    sib_id = (ha, wa + 1 - 2 * core)
    near_id = (ha, (wa + 2 * side + 32) % 32)
    far_to = (ha, (wa - 4 * side + 32) % 32)
    far_from = (ha, (wa + 4 * side + 32) % 32)
    zpair = (ha, wa - 2 * side)
    xpair = (ha - up, wa)
    diag = (ha - up, wa - 2 * side)
    y_to = ((ha + 2 * up + 8) % 8, wa)
    y_from = ((ha - 2 * up + 8) % 8, wa)

    side_in = jnp.where(zp == 0, tile > 0, tile < 7)
    far_out = jnp.where(zp == 0, tile < 7, tile > 0)
    y_out = jnp.where(xl == 1, row < 3, row > 0)
    y_in = jnp.where(xl == 1, row > 0, row < 3)

    def remote(src, dst, sems, index, device):
        return pltpu.make_async_remote_copy(
            src_ref=src, dst_ref=dst, send_sem=sems.at[(0,) + index], recv_sem=sems.at[(1,) + index],
            device_id=device, device_id_type=MESH,
        )

    barrier = pltpu.get_barrier_semaphore()
    partners = (sib_id, near_id, far_to, far_from, zpair, xpair, diag, y_to, y_from)
    for device in partners:
        pl.semaphore_signal(barrier, inc=1, device_id=device, device_id_type=MESH)
    pl.semaphore_wait(barrier, len(partners))

    def core_copy():
        return remote(x_ref.at[1 - core], sib, core_sem, (0,), sib_id)

    def near_copy(src, blk):
        return remote(src, kvb.at[0, 1, blk], near_sem, (blk,), near_id)

    def far_copy(src, blk):
        return remote(src, kvb.at[0, 2, blk], far_sem, (blk,), far_to)

    def y_copy(src, unit, blk):
        return remote(src, kvb.at[1, unit, blk], y_sem, (unit, blk), y_to)

    def zq_copy(src, blk):
        return remote(src, qb.at[xl, zp, blk], zq_sem, (blk,), zpair)

    def xq_copy(src, which, blk):
        place = zp + which - 2 * zp * which
        return remote(src, qb.at[xl, place, blk], xq_sem, (which, blk), xpair)

    def first_sends(kv, q, blk):
        @pl.when(y_out)
        def _():
            y_copy(kv, 0, blk).start()

        @pl.when(side_in)
        def _():
            near_copy(kv, blk).start()

        @pl.when(far_out)
        def _():
            far_copy(kv, blk).start()

        zq_copy(q, blk).start()
        xq_copy(q, 0, blk).start()

    core_copy().start()
    first_sends(x_ref.at[core, pl.ds(0, 2)], x_ref.at[core, pl.ds(2, 2)], core)
    kvb[0, 0, core] = x_ref[core, 0:2]
    qb[xl, zp, core] = x_ref[core, 2:4]
    core_copy().wait_recv()
    first_sends(sib.at[pl.ds(0, 2)], sib.at[pl.ds(2, 2)], 1 - core)
    kvb[0, 0, 1 - core] = sib[0:2]
    qb[xl, zp, 1 - core] = sib[2:4]

    def prepare_queries(half, place):
        for blk in range(2):
            q1, q2, q3 = thirds(qb[half, place, blk, 0] * SCALE)
            o1, o2 = halves(qb[half, place, blk, 1])
            rows = pl.ds(pl.multiple_of(place * UNIT + blk * CELLS, CELLS), CELLS)
            for i, part in enumerate((q1, q1, q2, q2, q3, q1)):
                rq[half, rows, i * DIM:(i + 1) * DIM] = part
            for i, part in enumerate((o1, o1, o2, o2)):
                ro[half, rows, i * DIM:(i + 1) * DIM] = part

    prepare_queries(xl, zp)
    dqt[...] = jnp.zeros_like(dqt)

    for step in range(2):
        blk = core + step - 2 * core * step

        @pl.when(side_in)
        def _():
            near_copy(kvb.at[0, 1, blk], blk).wait_recv()

            @pl.when(y_out)
            def _():
                y_copy(kvb.at[0, 1, blk], 1, blk).start()

            far_copy(kvb.at[0, 2, blk], blk).wait_recv()

            @pl.when(y_out)
            def _():
                y_copy(kvb.at[0, 2, blk], 2, blk).start()

        zq_copy(qb.at[xl, 1 - zp, blk], blk).wait_recv()
        xq_copy(qb.at[xl, 1 - zp, blk], 1, blk).start()

    prepare_queries(xl, 1 - zp)
    for which in range(2):
        for blk in range(2):
            xq_copy(qb.at[xl, zp, blk], which, blk).wait_recv()
    prepare_queries(1 - xl, zp)
    prepare_queries(1 - xl, 1 - zp)

    def prepare_keys(line, unit):
        index = 3 * line + unit
        parts = []
        for blk in range(2):
            k1, k2, k3 = thirds(kvb[line, unit, blk, 0])
            v1, v2 = halves(kvb[line, unit, blk, 1])
            for i, part in enumerate((k1, k2, k1, k2, k1, k3)):
                kp[index, blk * CELLS:(blk + 1) * CELLS, i * DIM:(i + 1) * DIM] = part
            parts.append(jnp.concatenate([v1, v2, v1, v2], axis=1))
        return jnp.concatenate(parts, axis=0)

    def forward_block(index, values, line_index, half):
        scores = dot(kp[line_index], rq[half], ((1,), (1,)))
        dprobs = dot(values, ro[half], ((1,), (1,)))
        peak = jnp.max(scores, axis=0, keepdims=True)
        weights = jnp.exp(scores - peak)
        wbuf[index] = weights
        dbuf[index] = dprobs
        st[index, 0:1] = peak
        st[index, 1:2] = jnp.sum(weights, axis=0, keepdims=True)
        st[index, 2:3] = jnp.sum(weights * dprobs, axis=0, keepdims=True)

    def empty_stats(index):
        st[index, 0:1] = jnp.full((1, HALF), LOW, F32)
        st[index, 1:3] = jnp.zeros((2, HALF), F32)

    def own_unit(unit, carry):
        @pl.when((unit == 0) | side_in)
        def _():
            values = prepare_keys(0, unit)

            def one(half, c):
                forward_block(3 * unit + half, values, unit, half)
                return c

            lax.fori_loop(0, 2, one, 0)

        @pl.when((unit > 0) & jnp.logical_not(side_in))
        def _():
            empty_stats(3 * unit)
            empty_stats(3 * unit + 1)

        return carry

    lax.fori_loop(0, 3, own_unit, 0)

    def halo_unit(unit, carry):
        valid = y_in & ((unit == 0) | side_in)

        @pl.when(valid)
        def _():
            for blk in range(2):
                y_copy(kvb.at[1, unit, blk], unit, blk).wait_recv()
            values = prepare_keys(1, unit)
            forward_block(3 * unit + 2, values, 3 + unit, 1 - xl)

        @pl.when(jnp.logical_not(valid))
        def _():
            empty_stats(3 * unit + 2)

        return carry

    lax.fori_loop(0, 3, halo_unit, 0)

    me = 2 * xl + zp
    for half in range(2):
        mine = half == 1 - xl
        peaks, sums, centers = [], [], []
        for unit in range(3):
            peaks.append(st[3 * unit + half, 0:1])
            sums.append(st[3 * unit + half, 1:2])
            centers.append(st[3 * unit + half, 2:3])
            peaks.append(jnp.where(mine, st[3 * unit + 2, 0:1], LOW))
            sums.append(jnp.where(mine, st[3 * unit + 2, 1:2], 0.0))
            centers.append(jnp.where(mine, st[3 * unit + 2, 2:3], 0.0))
        peak = peaks[0]
        for p in peaks[1:]:
            peak = jnp.maximum(peak, p)
        total = jnp.zeros_like(peak)
        center = jnp.zeros_like(peak)
        for p, s, c in zip(peaks, sums, centers):
            factor = jnp.exp(p - peak)
            total += s * factor
            center += c * factor
        sall[me, 3 * half:3 * half + 1] = peak
        sall[me, 3 * half + 1:3 * half + 2] = total
        sall[me, 3 * half + 2:3 * half + 3] = center
    sall[me, 6:8] = jnp.zeros((2, HALF), F32)

    def stat_copy(which):
        device = (xpair, zpair, diag)[which]
        return remote(sall.at[me], sall.at[me], stat_sem, (which,), device)

    for which in range(3):
        stat_copy(which).start()
    for which in range(3):
        stat_copy(which).wait_recv()
    for half in range(2):
        peak = sall[0, 3 * half:3 * half + 1]
        for i in range(1, 4):
            peak = jnp.maximum(peak, sall[i, 3 * half:3 * half + 1])
        total = jnp.zeros_like(peak)
        center = jnp.zeros_like(peak)
        for i in range(4):
            factor = jnp.exp(sall[i, 3 * half:3 * half + 1] - peak)
            total += sall[i, 3 * half + 1:3 * half + 2] * factor
            center += sall[i, 3 * half + 2:3 * half + 3] * factor
        inverse = 1.0 / total
        gst[half, 0:1] = peak
        gst[half, 1:2] = inverse
        gst[half, 2:3] = center * inverse

    def backward_block(index, line_index, half):
        alpha = jnp.exp(st[index, 0:1] - gst[half, 0:1]) * gst[half, 1:2]
        probs = wbuf[index] * alpha
        dscores = probs * (dbuf[index] - gst[half, 2:3])
        p1, p2 = halves(probs)
        s1, s2 = halves(dscores)
        q12 = rq[half, :, DIM:3 * DIM]
        o12 = ro[half, :, DIM:3 * DIM]
        k12 = kp[line_index, :, 0:2 * DIM]
        dv = dot(p1, o12, ((1,), (0,))) + dot(p2, o12, ((1,), (0,)))
        dk = dot(s1, q12, ((1,), (0,))) + dot(s2, q12, ((1,), (0,)))
        dq = dot(k12, s1, ((0,), (0,))) + dot(k12, s2, ((0,), (0,)))
        dq = dq[:DIM] + dq[DIM:]
        dqt[half, 0] += dq[:, :UNIT]
        dqt[half, 1] += dq[:, UNIT:]
        return dk[:, :DIM] + dk[:, DIM:], dv[:, :DIM] + dv[:, DIM:]

    def yr_copy(unit):
        return remote(halo.at[unit], yret.at[unit], yr_sem, (unit,), y_from)

    def halo_back(step, carry):
        unit = 2 - step

        @pl.when(y_in & ((unit == 0) | side_in))
        def _():
            dk, dv = backward_block(3 * unit + 2, 3 + unit, 1 - xl)
            halo[unit, 0] = dk
            halo[unit, 1] = dv
            yr_copy(unit).start()

        return carry

    lax.fori_loop(0, 3, halo_back, 0)

    def own_back(step, carry):
        unit = 2 - step

        @pl.when((unit == 0) | side_in)
        def _():
            own[unit] = jnp.zeros((2, UNIT, DIM), F32)

            def one(half, c):
                dk, dv = backward_block(3 * unit + half, unit, half)
                own[unit, 0] += dk
                own[unit, 1] += dv
                return c

            lax.fori_loop(0, 2, one, 0)

        return carry

    lax.fori_loop(0, 3, own_back, 0)

    def dq_copy(which):
        device = (xpair, zpair, diag)[which]
        src = (dqt.at[1 - xl, zp], dqt.at[xl, 1 - zp], dqt.at[1 - xl, 1 - zp])[which]
        return remote(src, dqr.at[which], dq_sem, (which,), device)

    for which in range(3):
        dq_copy(which).start()

    def zr_copy(which):
        return remote(own.at[1 + which], zret.at[which], zr_sem, (which,), (near_id, far_from)[which])

    for which in (1, 0):
        @pl.when(side_in)
        def _():
            @pl.when(y_out)
            def _():
                yr_copy(1 + which).wait_recv()
                own[1 + which] += yret[1 + which]

            zr_copy(which).start()

    for which in range(3):
        dq_copy(which).wait_recv()
    dq = dqt[xl, zp] + dqr[0] + dqr[1] + dqr[2]
    dq = dq.T * SCALE
    fin[0, 0] = dq[:CELLS]
    fin[0, 1] = dq[CELLS:]

    @pl.when(y_out)
    def _():
        yr_copy(0).wait_recv()
        own[0] += yret[0]

    @pl.when(far_out)
    def _():
        zr_copy(1).wait_recv()
        own[0] += zret[1]

    @pl.when(side_in)
    def _():
        zr_copy(0).wait_recv()
        own[0] += zret[0]

    for i in range(2):
        for blk in range(2):
            fin[1 + i, blk] = own[0, i, blk * CELLS:(blk + 1) * CELLS]

    final = remote(fin.at[:, 1 - core], fout, fin_sem, (0,), sib_id)
    final.start()
    lanes = pl.ds(pl.multiple_of(core * DIM, DIM), DIM)
    other = pl.ds(pl.multiple_of((1 - core) * DIM, DIM), DIM)
    for i in range(3):
        out_ref[i, :, lanes] = fin[i, core]
    final.wait_recv()
    for i in range(3):
        out_ref[i, :, other] = fout[i]

    final.wait_send()
    core_copy().wait_send()
    for blk in range(2):
        @pl.when(y_out)
        def _():
            y_copy(sib.at[pl.ds(0, 2)], 0, blk).wait_send()

            @pl.when(side_in)
            def _():
                for unit in (1, 2):
                    y_copy(kvb.at[0, unit, blk], unit, blk).wait_send()

        @pl.when(side_in)
        def _():
            near_copy(sib.at[pl.ds(0, 2)], blk).wait_send()

        @pl.when(far_out)
        def _():
            far_copy(sib.at[pl.ds(0, 2)], blk).wait_send()

        zq_copy(sib.at[pl.ds(2, 2)], blk).wait_send()
        for which in range(2):
            xq_copy(sib.at[pl.ds(2, 2)], which, blk).wait_send()
    for which in range(3):
        stat_copy(which).wait_send()
        dq_copy(which).wait_send()

    @pl.when(y_in)
    def _():
        yr_copy(0).wait_send()

    @pl.when(side_in)
    def _():
        for which in range(2):
            zr_copy(which).wait_send()

            @pl.when(y_in)
            def _():
                yr_copy(1 + which).wait_send()


def body(query_field, key_field, value_field, output_grad):
    frames, rows, cols, channels = query_field.shape
    packed = jnp.stack([key_field, value_field, query_field, output_grad])
    packed = packed.reshape(4, CELLS, 2, DIM).transpose(2, 0, 1, 3)

    def sems(*shape):
        return pltpu.SemaphoreType.DMA((2,) + shape)

    out = pl.pallas_call(
        kernel,
        out_shape=jax.ShapeDtypeStruct((3, CELLS, channels), F32),
        in_specs=[pl.BlockSpec(memory_space=pltpu.VMEM)],
        out_specs=pl.BlockSpec(memory_space=pltpu.VMEM),
        scratch_shapes=[
            pltpu.VMEM((4, CELLS, DIM), F32),
            pltpu.VMEM((2, 3, 2, 2, CELLS, DIM), F32),
            pltpu.VMEM((2, 2, 2, 2, CELLS, DIM), F32),
            pltpu.VMEM((6, UNIT, 6 * DIM), BF16),
            pltpu.VMEM((2, HALF, 6 * DIM), BF16),
            pltpu.VMEM((2, HALF, 4 * DIM), BF16),
            pltpu.VMEM((9, UNIT, HALF), F32),
            pltpu.VMEM((9, UNIT, HALF), F32),
            pltpu.VMEM((9, 8, HALF), F32),
            pltpu.VMEM((4, 8, HALF), F32),
            pltpu.VMEM((2, 8, HALF), F32),
            pltpu.VMEM((2, 2, DIM, UNIT), F32),
            pltpu.VMEM((3, DIM, UNIT), F32),
            pltpu.VMEM((3, 2, UNIT, DIM), F32),
            pltpu.VMEM((3, 2, UNIT, DIM), F32),
            pltpu.VMEM((3, 2, UNIT, DIM), F32),
            pltpu.VMEM((2, 2, UNIT, DIM), F32),
            pltpu.VMEM((3, 2, CELLS, DIM), F32),
            pltpu.VMEM((3, CELLS, DIM), F32),
            sems(1), sems(2), sems(2), sems(3, 2), sems(2), sems(2, 2), sems(3), sems(3), sems(2), sems(3), sems(1),
        ],
        compiler_params=pltpu.CompilerParams(
            collective_id=0, has_side_effects=True, vmem_limit_bytes=56 * 1024 * 1024
        ),
    )(packed)
    out = out.reshape(3, frames, rows, cols, channels)
    return out[0], out[1], out[2]


def solution(mesh):
    spec = P(None, "ha", "wa", None)
    return jax.shard_map(
        body, mesh=mesh, in_specs=(spec,) * 4, out_specs=(spec,) * 3, check_vma=False,
    )
```

```python
import jax
import jax.numpy as jnp
from jax import lax
from jax.experimental import pallas as pl
from jax.experimental.pallas import tpu as pltpu
from jax.sharding import PartitionSpec as P

MESH = pl.DeviceIdType.MESH
F32 = jnp.float32
BF16 = jnp.bfloat16
DIM = 128
SCALE = DIM ** -0.5
LOW = -1e30
CELLS = 128
KEYS = 3 * CELLS
HALF = 4 * CELLS


def halves(x):
    hi = x.astype(BF16)
    return hi, (x - hi.astype(F32)).astype(BF16)


def thirds(x):
    hi = x.astype(BF16)
    rest = x - hi.astype(F32)
    mid = rest.astype(BF16)
    return hi, mid, (rest - mid.astype(F32)).astype(BF16)


def dot(a, b, dims):
    return lax.dot_general(a, b, (dims, ((), ())), preferred_element_type=F32)


def kernel(
    q_in, k_in, v_in, g_in, dq_out, dk_out, dv_out,
    raw, kvb, qb, kp, lv, rq, ro, wbuf, dbuf, st, sst, sall, gst, dqt, dqs, dqr, own, halo, yret, zret,
    in_sem, near_sem, far_sem, y_sem, zq_sem, xq_sem, diag_sem, sibq_sem, pair_sem, stat_sem,
    yr_sem, zr_sem, dqs_sem, dq_sem,
):
    ha, wa = lax.axis_index("ha"), lax.axis_index("wa")
    row, xl = ha // 2, ha % 2
    core = wa % 2
    chip = wa // 2
    zp = chip % 2
    tile = chip // 2
    side = 2 * zp - 1
    up = 2 * xl - 1

    sib_id = (ha, wa + 1 - 2 * core)
    near_id = (ha, (wa + 2 * side + 32) % 32)
    far_to = (ha, (wa - 4 * side + 32) % 32)
    far_from = (ha, (wa + 4 * side + 32) % 32)
    zpair = (ha, wa - 2 * side)
    xpair = (ha - up, wa)
    diag = (ha - up, wa - 2 * side)
    y_to = ((ha + 2 * up + 8) % 8, wa)
    y_from = ((ha - 2 * up + 8) % 8, wa)

    side_in = jnp.where(zp == 0, tile > 0, tile < 7)
    far_out = jnp.where(zp == 0, tile < 7, tile > 0)
    y_out = jnp.where(xl == 1, row < 3, row > 0)
    y_in = jnp.where(xl == 1, row > 0, row < 3)
    z_first = (tile > 0) & (tile < 7)

    barrier = pltpu.get_barrier_semaphore()
    partners = (sib_id, near_id, far_to, far_from, zpair, xpair, diag, y_to, y_from)
    for device in partners:
        pl.semaphore_signal(barrier, inc=1, device_id=device, device_id_type=MESH)
    loads = [
        pltpu.make_async_copy(ref, raw.at[i], in_sem.at[i]) for i, ref in enumerate((k_in, v_in, q_in, g_in))
    ]
    for load in loads:
        load.start()
    for load in loads:
        load.wait()
    for h in range(2):
        for i in range(4):
            part = raw[i, :, :, h * DIM:(h + 1) * DIM].reshape(CELLS, DIM)
            if i < 2:
                kvb[h, 0, 0, i] = part
            else:
                qb[h, xl, zp, core, i - 2] = part
    pl.semaphore_wait(barrier, len(partners))

    def remote(src, dst, sems, index, device):
        return pltpu.make_async_remote_copy(
            src_ref=src, dst_ref=dst, send_sem=sems.at[(0,) + index], recv_sem=sems.at[(1,) + index],
            device_id=device, device_id_type=MESH,
        )

    def near_copy(h):
        return remote(kvb.at[h, 0, 0], kvb.at[h, 0, 1], near_sem, (h,), near_id)

    def far_copy(h):
        return remote(kvb.at[h, 0, 0], kvb.at[h, 0, 2], far_sem, (h,), far_to)

    def y_copy(h, unit):
        return remote(kvb.at[h, 0, unit], kvb.at[h, 1, unit], y_sem, (h, unit), y_to)

    def q_copy(h, half, place, sems, device):
        return remote(qb.at[h, half, place, core], qb.at[h, half, place, core], sems, (h,), device)

    def zq_copy(h):
        return q_copy(h, xl, zp, zq_sem, zpair)

    def xq_copy(h):
        return q_copy(h, xl, zp, xq_sem, xpair)

    def diag_by_x(h):
        return q_copy(h, xl, 1 - zp, diag_sem, xpair)

    def diag_by_z(h):
        return q_copy(h, 1 - xl, zp, diag_sem, zpair)

    def sib_copy(h, slot):
        half, place = (
            (xl, zp), (xl, 1 - zp), (1 - xl, zp), (1 - xl, 1 - zp)
        )[slot]
        block = qb.at[h, half, place, core]
        return remote(block, block, sibq_sem, (h, slot), sib_id)

    def first_sends(h):
        @pl.when(y_out)
        def _():
            y_copy(h, 0).start()

        @pl.when(side_in)
        def _():
            near_copy(h).start()

        @pl.when(far_out)
        def _():
            far_copy(h).start()

        zq_copy(h).start()
        xq_copy(h).start()
        sib_copy(h, 0).start()

    def pass_on(h):
        @pl.when(side_in)
        def _():
            near_copy(h).wait_recv()

            @pl.when(y_out)
            def _():
                y_copy(h, 1).start()

            far_copy(h).wait_recv()

            @pl.when(y_out)
            def _():
                y_copy(h, 2).start()

        zq_copy(h).wait_recv()
        sib_copy(h, 1).start()

        @pl.when(z_first)
        def _():
            diag_by_x(h).start()

        xq_copy(h).wait_recv()
        sib_copy(h, 2).start()

        @pl.when(jnp.logical_not(z_first))
        def _():
            diag_by_z(h).start()

    def last_queries(h):
        diag_by_x(h).wait_recv()
        sib_copy(h, 3).start()

    def prepare_queries(h):
        for slot in range(4):
            sib_copy(h, slot).wait_recv()

        def one(index, c):
            half, place = index // 2, index % 2
            for blk in range(2):
                q1, q2, q3 = thirds(qb[h, half, place, blk, 0] * SCALE)
                o1, o2 = halves(qb[h, half, place, blk, 1])
                rows = pl.ds(pl.multiple_of(place * (2 * CELLS) + blk * CELLS, CELLS), CELLS)
                for i, part in enumerate((q1, q1, q2, q2, q3, q1)):
                    rq[h, half, rows, i * DIM:(i + 1) * DIM] = part
                for i, part in enumerate((o1, o1, o2, o2)):
                    ro[h, half, rows, i * DIM:(i + 1) * DIM] = part
            return c

        lax.fori_loop(0, 4, one, 0)

    def prepare_keys(h, line):
        for unit in range(3):
            rows = slice(unit * CELLS, (unit + 1) * CELLS)
            k1, k2, k3 = thirds(kvb[h, line, unit, 0])
            v1, v2 = halves(kvb[h, line, unit, 1])
            for i, part in enumerate((k1, k2, k1, k2, k1, k3)):
                kp[2 * h + line, rows, i * DIM:(i + 1) * DIM] = part
            for i, part in enumerate((v1, v2, v1, v2)):
                lv[rows, i * DIM:(i + 1) * DIM] = part

    far_keys = lax.broadcasted_iota(jnp.int32, (KEYS, 1), 0) >= CELLS
    bias = jnp.where(far_keys, jnp.where(side_in, 0.0, LOW), 0.0)

    def forward_block(h, k, line, half):
        index = 3 * h + k
        scores = dot(kp[2 * h + line], rq[h, half], ((1,), (1,))) + bias
        dprobs = dot(lv[...], ro[h, half], ((1,), (1,)))
        peak = jnp.max(scores, axis=0, keepdims=True)
        weights = jnp.exp(scores - peak)
        wbuf[index] = weights
        dbuf[index] = dprobs
        st[index, 0:1] = peak
        st[index, 1:2] = jnp.sum(weights, axis=0, keepdims=True)
        st[index, 2:3] = jnp.sum(weights * dprobs, axis=0, keepdims=True)

    def own_forward(h):
        prepare_keys(h, 0)

        def one(half, c):
            forward_block(h, half, 0, half)
            return c

        lax.fori_loop(0, 2, one, 0)

    def halo_forward(h):
        @pl.when(y_in)
        def _():
            y_copy(h, 0).wait_recv()

            @pl.when(side_in)
            def _():
                y_copy(h, 1).wait_recv()
                y_copy(h, 2).wait_recv()

            prepare_keys(h, 1)
            forward_block(h, 2, 1, 1 - xl)

        @pl.when(jnp.logical_not(y_in))
        def _():
            st[3 * h + 2, 0:1] = jnp.full((1, HALF), LOW, F32)
            st[3 * h + 2, 1:3] = jnp.zeros((2, HALF), F32)

    me = 2 * xl + zp

    def merge(triples):
        peak = triples[0][0]
        for p, _, _ in triples[1:]:
            peak = jnp.maximum(peak, p)
        total = jnp.zeros_like(peak)
        center = jnp.zeros_like(peak)
        for p, s, c in triples:
            factor = jnp.exp(p - peak)
            total += s * factor
            center += c * factor
        return peak, total, center

    def triple(ref, base):
        return tuple(ref[base + i:base + i + 1] for i in range(3))

    def pair_copy(h):
        return remote(sst.at[h, core], sst.at[h, core], pair_sem, (h,), sib_id)

    def stat_copy(h, which):
        device = (xpair, zpair, diag)[which]
        return remote(sall.at[h, me], sall.at[h, me], stat_sem, (h, which), device)

    def start_stats(h):
        for half in range(2):
            mine = half == 1 - xl
            extra = triple(st.at[3 * h + 2], 0)
            extra = (
                jnp.where(mine, extra[0], LOW), jnp.where(mine, extra[1], 0.0), jnp.where(mine, extra[2], 0.0)
            )
            merged = merge([triple(st.at[3 * h + half], 0), extra])
            for i in range(3):
                sst[h, core, 3 * half + i:3 * half + i + 1] = merged[i]
        sst[h, core, 6:8] = jnp.zeros((2, HALF), F32)
        pair_copy(h).start()

    def share_stats(h):
        pair_copy(h).wait_recv()
        for half in range(2):
            merged = merge([triple(sst.at[h, i], 3 * half) for i in range(2)])
            for i in range(3):
                sall[h, me, 3 * half + i:3 * half + i + 1] = merged[i]
        sall[h, me, 6:8] = jnp.zeros((2, HALF), F32)
        for which in range(3):
            stat_copy(h, which).start()

    def end_stats(h):
        for which in range(3):
            stat_copy(h, which).wait_recv()
        for half in range(2):
            peak, total, center = merge([triple(sall.at[h, i], 3 * half) for i in range(4)])
            inverse = 1.0 / total
            gst[h, half, 0:1] = peak
            gst[h, half, 1:2] = inverse
            gst[h, half, 2:3] = center * inverse

    def backward_block(h, k, line, half):
        index = 3 * h + k
        alpha = jnp.exp(st[index, 0:1] - gst[h, half, 0:1]) * gst[h, half, 1:2]
        probs = wbuf[index] * alpha
        dscores = probs * (dbuf[index] - gst[h, half, 2:3])
        p1, p2 = halves(probs)
        s1, s2 = halves(dscores)
        q12 = rq[h, half, :, DIM:3 * DIM]
        o12 = ro[h, half, :, DIM:3 * DIM]
        k12 = kp[2 * h + line, :, 0:2 * DIM]
        dv = dot(p1, o12, ((1,), (0,))) + dot(p2, o12, ((1,), (0,)))
        dk = dot(s1, q12, ((1,), (0,))) + dot(s2, q12, ((1,), (0,)))
        dq = dot(k12, s1, ((0,), (0,))) + dot(k12, s2, ((0,), (0,)))
        dq = dq[:DIM] + dq[DIM:]
        for place in range(2):
            for blk in range(2):
                at = (2 * place + blk) * CELLS
                dqt[h, half, place, blk] += dq[:, at:at + CELLS]
        return dk[:, :DIM] + dk[:, DIM:], dv[:, :DIM] + dv[:, DIM:]

    def yr_copy(h, unit):
        return remote(halo.at[h, unit], yret.at[h, unit], yr_sem, (h, unit), y_from)

    def dqs_copy(h):
        return remote(dqt.at[h, :, :, 1 - core], dqs.at[h], dqs_sem, (h,), sib_id)

    def backward(h):
        dqt[h] = jnp.zeros(dqt.shape[1:], F32)
        own[h] = jnp.zeros(own.shape[1:], F32)

        @pl.when(y_in)
        def _():
            dk, dv = backward_block(h, 2, 1, 1 - xl)
            for unit in range(3):
                halo[h, unit, 0] = dk[unit * CELLS:(unit + 1) * CELLS]
                halo[h, unit, 1] = dv[unit * CELLS:(unit + 1) * CELLS]

            @pl.when(side_in)
            def _():
                yr_copy(h, 2).start()
                yr_copy(h, 1).start()

            yr_copy(h, 0).start()

        def one(half, c):
            dk, dv = backward_block(h, half, 0, half)
            for unit in range(3):
                own[h, unit, 0] += dk[unit * CELLS:(unit + 1) * CELLS]
                own[h, unit, 1] += dv[unit * CELLS:(unit + 1) * CELLS]
            return c

        lax.fori_loop(0, 2, one, 0)
        dqs_copy(h).start()

    def dq_copy(h, which):
        device = (xpair, zpair, diag)[which]
        half, place = ((1 - xl, zp), (xl, 1 - zp), (1 - xl, 1 - zp))[which]
        return remote(dqt.at[h, half, place, core], dqr.at[h, which], dq_sem, (h, which), device)

    def share_dq(h):
        dqs_copy(h).wait_recv()
        for half in range(2):
            for place in range(2):
                dqt[h, half, place, core] += dqs[h, half, place]
        for which in range(3):
            dq_copy(h, which).start()

    def zr_copy(h, which):
        return remote(own.at[h, 1 + which], zret.at[h, which], zr_sem, (h, which), (near_id, far_from)[which])

    def pass_back(h):
        for which in (1, 0):
            @pl.when(side_in)
            def _():
                @pl.when(y_out)
                def _():
                    yr_copy(h, 1 + which).wait_recv()
                    own[h, 1 + which] += yret[h, 1 + which]

                zr_copy(h, which).start()

    def finish(h):
        lanes = slice(h * DIM, (h + 1) * DIM)
        for which in range(3):
            dq_copy(h, which).wait_recv()
        dq = dqt[h, xl, zp, core] + dqr[h, 0] + dqr[h, 1] + dqr[h, 2]
        dq_out[:, :, lanes] = (dq.T * SCALE).reshape(32, 4, DIM)

        @pl.when(y_out)
        def _():
            yr_copy(h, 0).wait_recv()
            own[h, 0] += yret[h, 0]

        @pl.when(far_out)
        def _():
            zr_copy(h, 1).wait_recv()
            own[h, 0] += zret[h, 1]

        @pl.when(side_in)
        def _():
            zr_copy(h, 0).wait_recv()
            own[h, 0] += zret[h, 0]

        dk_out[:, :, lanes] = own[h, 0, 0].reshape(32, 4, DIM)
        dv_out[:, :, lanes] = own[h, 0, 1].reshape(32, 4, DIM)

    def all_left(h):
        @pl.when(y_out)
        def _():
            y_copy(h, 0).wait_send()

            @pl.when(side_in)
            def _():
                y_copy(h, 1).wait_send()
                y_copy(h, 2).wait_send()

        @pl.when(side_in)
        def _():
            near_copy(h).wait_send()
            for which in range(2):
                zr_copy(h, which).wait_send()

        @pl.when(far_out)
        def _():
            far_copy(h).wait_send()

        @pl.when(y_in)
        def _():
            yr_copy(h, 0).wait_send()

            @pl.when(side_in)
            def _():
                yr_copy(h, 1).wait_send()
                yr_copy(h, 2).wait_send()

        zq_copy(h).wait_send()
        xq_copy(h).wait_send()
        diag_by_x(h).wait_send()
        for slot in range(4):
            sib_copy(h, slot).wait_send()
        pair_copy(h).wait_send()
        dqs_copy(h).wait_send()
        for which in range(3):
            stat_copy(h, which).wait_send()
            dq_copy(h, which).wait_send()

    first_sends(0)

    @pl.when(jnp.logical_not(side_in))
    def _():
        for h in range(2):
            for line in range(2):
                kvb[h, line, 1:3] = jnp.zeros((2, 2, CELLS, DIM), F32)

    pass_on(0)
    first_sends(1)
    last_queries(0)
    prepare_queries(0)
    own_forward(0)
    pass_on(1)
    halo_forward(0)
    start_stats(0)
    last_queries(1)
    share_stats(0)
    prepare_queries(1)
    own_forward(1)
    end_stats(0)
    backward(0)
    halo_forward(1)
    start_stats(1)
    share_dq(0)
    share_stats(1)
    pass_back(0)
    end_stats(1)
    backward(1)
    finish(0)
    share_dq(1)
    pass_back(1)
    finish(1)
    all_left(0)
    all_left(1)


def body(query_field, key_field, value_field, output_grad):
    frames, rows, cols, channels = query_field.shape
    flat = (frames * rows, cols, channels)

    def sems(*shape):
        return pltpu.SemaphoreType.DMA((2, 2) + shape)

    outs = pl.pallas_call(
        kernel,
        out_shape=[jax.ShapeDtypeStruct(flat, F32)] * 3,
        in_specs=[pl.BlockSpec(memory_space=pl.ANY)] * 4,
        out_specs=[pl.BlockSpec(memory_space=pltpu.VMEM)] * 3,
        scratch_shapes=[
            pltpu.VMEM((4,) + flat, F32),
            pltpu.VMEM((2, 2, 3, 2, CELLS, DIM), F32),
            pltpu.VMEM((2, 2, 2, 2, 2, CELLS, DIM), F32),
            pltpu.VMEM((4, KEYS, 6 * DIM), BF16),
            pltpu.VMEM((KEYS, 4 * DIM), BF16),
            pltpu.VMEM((2, 2, HALF, 6 * DIM), BF16),
            pltpu.VMEM((2, 2, HALF, 4 * DIM), BF16),
            pltpu.VMEM((6, KEYS, HALF), F32),
            pltpu.VMEM((6, KEYS, HALF), F32),
            pltpu.VMEM((6, 8, HALF), F32),
            pltpu.VMEM((2, 2, 8, HALF), F32),
            pltpu.VMEM((2, 4, 8, HALF), F32),
            pltpu.VMEM((2, 2, 8, HALF), F32),
            pltpu.VMEM((2, 2, 2, 2, DIM, CELLS), F32),
            pltpu.VMEM((2, 2, 2, DIM, CELLS), F32),
            pltpu.VMEM((2, 3, DIM, CELLS), F32),
            pltpu.VMEM((2, 3, 2, CELLS, DIM), F32),
            pltpu.VMEM((2, 3, 2, CELLS, DIM), F32),
            pltpu.VMEM((2, 3, 2, CELLS, DIM), F32),
            pltpu.VMEM((2, 2, 2, CELLS, DIM), F32),
            pltpu.SemaphoreType.DMA((4,)),
            sems(), sems(), sems(3), sems(), sems(), sems(), sems(4), sems(), sems(3),
            sems(3), sems(2), sems(), sems(3),
        ],
        compiler_params=pltpu.CompilerParams(
            collective_id=0, has_side_effects=True, vmem_limit_bytes=56 * 1024 * 1024
        ),
    )(*(x.reshape(flat) for x in (query_field, key_field, value_field, output_grad)))
    return tuple(x.reshape(frames, rows, cols, channels) for x in outs)


def solution(mesh):
    spec = P(None, "ha", "wa", None)
    return jax.shard_map(
        body, mesh=mesh, in_specs=(spec,) * 4, out_specs=(spec,) * 3, check_vma=False,
    )
```

```python
import jax
import jax.numpy as jnp
from jax import lax
from jax.experimental import pallas as pl
from jax.experimental.pallas import tpu as pltpu
from jax.sharding import PartitionSpec as P

MESH = pl.DeviceIdType.MESH
F32 = jnp.float32
BF16 = jnp.bfloat16
DIM = 128
SCALE = DIM ** -0.5
LOW = -1e30
CELLS = 128
KEYS = 3 * CELLS
HALF = 4 * CELLS


def halves(x):
    hi = x.astype(BF16)
    return hi, (x - hi.astype(F32)).astype(BF16)


def thirds(x):
    hi = x.astype(BF16)
    rest = x - hi.astype(F32)
    mid = rest.astype(BF16)
    return hi, mid, (rest - mid.astype(F32)).astype(BF16)


def dot(a, b, dims):
    return lax.dot_general(a, b, (dims, ((), ())), preferred_element_type=F32)


def kernel(
    q_in, k_in, v_in, g_in, dq_out, dk_out, dv_out,
    raw, kvb, qb, kp, lv, rq, ro, wbuf, dbuf, st, sst, sall, gst, dqt, dqs, dqr, own, halo, yret, zret,
    in_sem, near_sem, far_sem, y_sem, zq_sem, xq_sem, diag_sem, sibq_sem, pair_sem, stat_sem,
    yr_sem, zr_sem, dqs_sem, dq_sem,
):
    ha, wa = lax.axis_index("ha"), lax.axis_index("wa")
    row, xl = ha // 2, ha % 2
    core = wa % 2
    chip = wa // 2
    zp = chip % 2
    tile = chip // 2
    side = 2 * zp - 1
    up = 2 * xl - 1

    sib_id = (ha, wa + 1 - 2 * core)
    near_id = (ha, (wa + 2 * side + 32) % 32)
    far_to = (ha, (wa - 4 * side + 32) % 32)
    far_from = (ha, (wa + 4 * side + 32) % 32)
    zpair = (ha, wa - 2 * side)
    xpair = (ha - up, wa)
    diag = (ha - up, wa - 2 * side)
    y_to = ((ha + 2 * up + 8) % 8, wa)
    y_from = ((ha - 2 * up + 8) % 8, wa)

    side_in = jnp.where(zp == 0, tile > 0, tile < 7)
    far_out = jnp.where(zp == 0, tile < 7, tile > 0)
    y_out = jnp.where(xl == 1, row < 3, row > 0)
    y_in = jnp.where(xl == 1, row > 0, row < 3)
    z_first = (tile > 0) & (tile < 7)

    barrier = pltpu.get_barrier_semaphore()
    partners = (sib_id, near_id, far_to, far_from, zpair, xpair, diag, y_to, y_from)
    for device in partners:
        pl.semaphore_signal(barrier, inc=1, device_id=device, device_id_type=MESH)
    loads = [
        pltpu.make_async_copy(ref, raw.at[i], in_sem.at[i]) for i, ref in enumerate((k_in, v_in, q_in, g_in))
    ]
    for load in loads:
        load.start()
    for load in loads:
        load.wait()
    for h in range(2):
        for i in range(4):
            part = raw[i, :, :, h * DIM:(h + 1) * DIM].reshape(CELLS, DIM)
            if i < 2:
                kvb[h, 0, 0, i] = part
            else:
                qb[h, xl, zp, core, i - 2] = part
    pl.semaphore_wait(barrier, len(partners))

    def remote(src, dst, sems, index, device):
        return pltpu.make_async_remote_copy(
            src_ref=src, dst_ref=dst, send_sem=sems.at[(0,) + index], recv_sem=sems.at[(1,) + index],
            device_id=device, device_id_type=MESH,
        )

    def near_copy(h, kv):
        return remote(kvb.at[h, 0, 0, kv], kvb.at[h, 0, 1, kv], near_sem, (h, kv), near_id)

    def far_copy(h, kv):
        return remote(kvb.at[h, 0, 0, kv], kvb.at[h, 0, 2, kv], far_sem, (h, kv), far_to)

    def y_copy(h, unit, kv):
        return remote(kvb.at[h, 0, unit, kv], kvb.at[h, 1, unit, kv], y_sem, (h, unit, kv), y_to)

    def q_copy(h, half, place, part, sems, device):
        block = qb.at[h, half, place, core, part]
        return remote(block, block, sems, (h, part), device)

    def zq_copy(h, part):
        return q_copy(h, xl, zp, part, zq_sem, zpair)

    def xq_copy(h, part):
        return q_copy(h, xl, zp, part, xq_sem, xpair)

    def diag_by_x(h, part):
        return q_copy(h, xl, 1 - zp, part, diag_sem, xpair)

    def diag_by_z(h, part):
        return q_copy(h, 1 - xl, zp, part, diag_sem, zpair)

    def slot_place(slot):
        return xl + (slot // 2) * (1 - 2 * xl), zp + (slot % 2) * (1 - 2 * zp)

    def sib_copy(h, slot):
        half, place = slot_place(slot)
        block = qb.at[h, half, place, core]
        return remote(block, block, sibq_sem, (h, slot), sib_id)

    def first_sends(h):
        @pl.when(y_out)
        def _():
            y_copy(h, 0, 0).start()
            y_copy(h, 0, 1).start()

        for part in range(2):
            @pl.when(side_in)
            def _():
                near_copy(h, part).start()

            @pl.when(far_out)
            def _():
                far_copy(h, part).start()

            zq_copy(h, part).start()
            xq_copy(h, part).start()
        sib_copy(h, 0).start()

    def pass_keys(h, kv):
        @pl.when(side_in)
        def _():
            near_copy(h, kv).wait_recv()

            @pl.when(y_out)
            def _():
                y_copy(h, 1, kv).start()

            far_copy(h, kv).wait_recv()

            @pl.when(y_out)
            def _():
                y_copy(h, 2, kv).start()

    def pass_queries(h):
        xq_copy(h, 1).wait_recv()
        diag_by_z(h, 1).start()
        zq_copy(h, 0).wait_recv()

        @pl.when(z_first)
        def _():
            diag_by_x(h, 0).start()

        xq_copy(h, 0).wait_recv()
        sib_copy(h, 2).start()

        @pl.when(jnp.logical_not(z_first))
        def _():
            diag_by_z(h, 0).start()

        zq_copy(h, 1).wait_recv()
        sib_copy(h, 1).start()

    def last_queries(h):
        for part in range(2):
            diag_by_x(h, part).wait_recv()
        sib_copy(h, 3).start()

    def prepare_queries(h, low):
        def one(slot, c):
            sib_copy(h, slot).wait_recv()
            half, place = slot_place(slot)
            for blk in range(2):
                q1, q2, q3 = thirds(qb[h, half, place, blk, 0] * SCALE)
                o1, o2 = halves(qb[h, half, place, blk, 1])
                rows = pl.ds(pl.multiple_of(place * (2 * CELLS) + blk * CELLS, CELLS), CELLS)
                for i, part in enumerate((q1, q1, q2, q2, q3, q1)):
                    rq[h, half, rows, i * DIM:(i + 1) * DIM] = part
                for i, part in enumerate((o1, o1, o2, o2)):
                    ro[h, half, rows, i * DIM:(i + 1) * DIM] = part
            return c

        lax.fori_loop(low, low + 2, one, 0)

    def prepare_keys(h, line):
        for unit in range(3):
            rows = slice(unit * CELLS, (unit + 1) * CELLS)
            k1, k2, k3 = thirds(kvb[h, line, unit, 0])
            v1, v2 = halves(kvb[h, line, unit, 1])
            for i, part in enumerate((k1, k2, k1, k2, k1, k3)):
                kp[2 * h + line, rows, i * DIM:(i + 1) * DIM] = part
            for i, part in enumerate((v1, v2, v1, v2)):
                lv[rows, i * DIM:(i + 1) * DIM] = part

    far_keys = lax.broadcasted_iota(jnp.int32, (KEYS, 1), 0) >= CELLS
    bias = jnp.where(far_keys, jnp.where(side_in, 0.0, LOW), 0.0)

    def forward_block(h, k, line, half):
        index = 3 * h + k
        scores = dot(kp[2 * h + line], rq[h, half], ((1,), (1,))) + bias
        dprobs = dot(lv[...], ro[h, half], ((1,), (1,)))
        peak = jnp.max(scores, axis=0, keepdims=True)
        weights = jnp.exp(scores - peak)
        wbuf[index] = weights
        dbuf[index] = dprobs
        st[index, 0:1] = peak
        st[index, 1:2] = jnp.sum(weights, axis=0, keepdims=True)
        st[index, 2:3] = jnp.sum(weights * dprobs, axis=0, keepdims=True)

    def forward(h, before):
        def one(step, c):
            for i in range(3):
                @pl.when(step == i)
                def _():
                    before[i]()

            half = jnp.where(step == 0, xl, 1 - xl)
            line = step // 2
            here = (step < 2) | y_in

            @pl.when(here & (step != 1))
            def _():
                @pl.when(step == 2)
                def _():
                    for kv in range(2):
                        y_copy(h, 0, kv).wait_recv()

                        @pl.when(side_in)
                        def _():
                            y_copy(h, 1, kv).wait_recv()
                            y_copy(h, 2, kv).wait_recv()

                prepare_keys(h, line)

            @pl.when(here)
            def _():
                forward_block(h, step, line, half)

            @pl.when(jnp.logical_not(here))
            def _():
                st[3 * h + 2, 0:1] = jnp.full((1, HALF), LOW, F32)
                st[3 * h + 2, 1:3] = jnp.zeros((2, HALF), F32)

            return c

        lax.fori_loop(0, 3, one, 0)

    me = 2 * xl + zp

    def merge(triples):
        peak = triples[0][0]
        for p, _, _ in triples[1:]:
            peak = jnp.maximum(peak, p)
        total = jnp.zeros_like(peak)
        center = jnp.zeros_like(peak)
        for p, s, c in triples:
            factor = jnp.exp(p - peak)
            total += s * factor
            center += c * factor
        return peak, total, center

    def triple(ref, base):
        return tuple(ref[base + i:base + i + 1] for i in range(3))

    def pair_copy(h):
        return remote(sst.at[h, core], sst.at[h, core], pair_sem, (h,), sib_id)

    def stat_copy(h, which):
        device = (xpair, zpair, diag)[which]
        return remote(sall.at[h, me], sall.at[h, me], stat_sem, (h, which), device)

    def start_stats(h):
        merged = (triple(st.at[3 * h], 0), merge([triple(st.at[3 * h + 1], 0), triple(st.at[3 * h + 2], 0)]))
        for half in range(2):
            for i in range(3):
                value = jnp.where(half == xl, merged[0][i], merged[1][i])
                sst[h, core, 3 * half + i:3 * half + i + 1] = value
        sst[h, core, 6:8] = jnp.zeros((2, HALF), F32)
        pair_copy(h).start()

    def share_stats(h):
        pair_copy(h).wait_recv()
        for half in range(2):
            merged = merge([triple(sst.at[h, i], 3 * half) for i in range(2)])
            for i in range(3):
                sall[h, me, 3 * half + i:3 * half + i + 1] = merged[i]
        sall[h, me, 6:8] = jnp.zeros((2, HALF), F32)
        for which in range(3):
            stat_copy(h, which).start()

    def end_stats(h):
        for which in range(3):
            stat_copy(h, which).wait_recv()
        for half in range(2):
            peak, total, center = merge([triple(sall.at[h, i], 3 * half) for i in range(4)])
            inverse = 1.0 / total
            gst[h, half, 0:1] = peak
            gst[h, half, 1:2] = inverse
            gst[h, half, 2:3] = center * inverse

    def backward_block(h, k, line, half):
        index = 3 * h + k
        alpha = jnp.exp(st[index, 0:1] - gst[h, half, 0:1]) * gst[h, half, 1:2]
        probs = wbuf[index] * alpha
        dscores = probs * (dbuf[index] - gst[h, half, 2:3])
        p1, p2 = halves(probs)
        s1, s2 = halves(dscores)
        q12 = rq[h, half, :, DIM:3 * DIM]
        o12 = ro[h, half, :, DIM:3 * DIM]
        k12 = kp[2 * h + line, :, 0:2 * DIM]
        dv = dot(p1, o12, ((1,), (0,))) + dot(p2, o12, ((1,), (0,)))
        dk = dot(s1, q12, ((1,), (0,))) + dot(s2, q12, ((1,), (0,)))
        dq = dot(k12, s1, ((0,), (0,))) + dot(k12, s2, ((0,), (0,)))
        dq = dq[:DIM] + dq[DIM:]
        for place in range(2):
            for blk in range(2):
                at = (2 * place + blk) * CELLS
                dqt[h, half, place, blk] += dq[:, at:at + CELLS]
        return dk[:, :DIM] + dk[:, DIM:], dv[:, :DIM] + dv[:, DIM:]

    def yr_copy(h, unit):
        return remote(halo.at[h, unit], yret.at[h, unit], yr_sem, (h, unit), y_from)

    def dqs_copy(h):
        return remote(dqt.at[h, :, :, 1 - core], dqs.at[h], dqs_sem, (h,), sib_id)

    def backward(h):
        dqt[h] = jnp.zeros(dqt.shape[1:], F32)
        own[h] = jnp.zeros(own.shape[1:], F32)

        def one(turn, c):
            step = 2 - turn

            @pl.when((step < 2) | y_in)
            def _():
                half = jnp.where(step == 0, xl, 1 - xl)
                dk, dv = backward_block(h, step, step // 2, half)

                @pl.when(step == 2)
                def _():
                    for unit in range(3):
                        halo[h, unit, 0] = dk[unit * CELLS:(unit + 1) * CELLS]
                        halo[h, unit, 1] = dv[unit * CELLS:(unit + 1) * CELLS]

                    @pl.when(side_in)
                    def _():
                        yr_copy(h, 2).start()
                        yr_copy(h, 1).start()

                    yr_copy(h, 0).start()

                @pl.when(step < 2)
                def _():
                    for unit in range(3):
                        own[h, unit, 0] += dk[unit * CELLS:(unit + 1) * CELLS]
                        own[h, unit, 1] += dv[unit * CELLS:(unit + 1) * CELLS]

            return c

        lax.fori_loop(0, 3, one, 0)
        dqs_copy(h).start()

    def dq_copy(h, which):
        device = (xpair, zpair, diag)[which]
        half, place = ((1 - xl, zp), (xl, 1 - zp), (1 - xl, 1 - zp))[which]
        return remote(dqt.at[h, half, place, core], dqr.at[h, which], dq_sem, (h, which), device)

    def share_dq(h):
        dqs_copy(h).wait_recv()
        for half in range(2):
            for place in range(2):
                dqt[h, half, place, core] += dqs[h, half, place]
        for which in range(3):
            dq_copy(h, which).start()

    def zr_copy(h, which):
        return remote(own.at[h, 1 + which], zret.at[h, which], zr_sem, (h, which), (near_id, far_from)[which])

    def pass_back(h):
        for which in (1, 0):
            @pl.when(side_in)
            def _():
                @pl.when(y_out)
                def _():
                    yr_copy(h, 1 + which).wait_recv()
                    own[h, 1 + which] += yret[h, 1 + which]

                zr_copy(h, which).start()

    def finish(h):
        lanes = slice(h * DIM, (h + 1) * DIM)
        for which in range(3):
            dq_copy(h, which).wait_recv()
        dq = dqt[h, xl, zp, core] + dqr[h, 0] + dqr[h, 1] + dqr[h, 2]
        dq_out[:, :, lanes] = (dq.T * SCALE).reshape(32, 4, DIM)

        @pl.when(y_out)
        def _():
            yr_copy(h, 0).wait_recv()
            own[h, 0] += yret[h, 0]

        @pl.when(far_out)
        def _():
            zr_copy(h, 1).wait_recv()
            own[h, 0] += zret[h, 1]

        @pl.when(side_in)
        def _():
            zr_copy(h, 0).wait_recv()
            own[h, 0] += zret[h, 0]

        dk_out[:, :, lanes] = own[h, 0, 0].reshape(32, 4, DIM)
        dv_out[:, :, lanes] = own[h, 0, 1].reshape(32, 4, DIM)

    def all_left(h):
        for part in range(2):
            @pl.when(y_out)
            def _():
                y_copy(h, 0, part).wait_send()

                @pl.when(side_in)
                def _():
                    y_copy(h, 1, part).wait_send()
                    y_copy(h, 2, part).wait_send()

            @pl.when(side_in)
            def _():
                near_copy(h, part).wait_send()
                zr_copy(h, part).wait_send()

            @pl.when(far_out)
            def _():
                far_copy(h, part).wait_send()

            zq_copy(h, part).wait_send()
            xq_copy(h, part).wait_send()
            diag_by_x(h, part).wait_send()

        @pl.when(y_in)
        def _():
            yr_copy(h, 0).wait_send()

            @pl.when(side_in)
            def _():
                yr_copy(h, 1).wait_send()
                yr_copy(h, 2).wait_send()

        for slot in range(4):
            sib_copy(h, slot).wait_send()
        pair_copy(h).wait_send()
        dqs_copy(h).wait_send()
        for which in range(3):
            stat_copy(h, which).wait_send()
            dq_copy(h, which).wait_send()

    first_sends(0)
    first_sends(1)

    @pl.when(jnp.logical_not(side_in))
    def _():
        for h in range(2):
            for line in range(2):
                kvb[h, line, 1:3] = jnp.zeros((2, 2, CELLS, DIM), F32)

    def head0_start():
        pass_keys(0, 0)
        pass_keys(0, 1)
        pass_queries(0)
        prepare_queries(0, 0)

    def head0_other():
        last_queries(0)
        prepare_queries(0, 2)

    def head0_halo():
        pass_keys(1, 0)

    def head1_start():
        prepare_queries(1, 0)

    def head1_other():
        last_queries(1)
        prepare_queries(1, 2)

    def head1_halo():
        end_stats(0)
        backward(0)

    forward(0, (head0_start, head0_other, head0_halo))
    start_stats(0)
    pass_keys(1, 1)
    pass_queries(1)
    share_stats(0)
    forward(1, (head1_start, head1_other, head1_halo))
    start_stats(1)
    share_dq(0)
    share_stats(1)
    pass_back(0)
    end_stats(1)
    backward(1)
    finish(0)
    share_dq(1)
    pass_back(1)
    finish(1)
    all_left(0)
    all_left(1)


def copy_kernel(*refs):
    copies = [pltpu.make_async_copy(refs[i], refs[3 + i], refs[6].at[i]) for i in range(3)]
    for copy in copies:
        copy.start()
    for copy in copies:
        copy.wait()


def body(query_field, key_field, value_field, output_grad):
    frames, rows, cols, channels = query_field.shape
    flat = (frames * rows, cols, channels)

    def sems(*shape):
        return pltpu.SemaphoreType.DMA((2, 2) + shape)

    outs = pl.pallas_call(
        kernel,
        out_shape=[jax.ShapeDtypeStruct(flat, F32)] * 3,
        in_specs=[pl.BlockSpec(memory_space=pl.ANY)] * 4,
        out_specs=[pl.BlockSpec(memory_space=pltpu.VMEM)] * 3,
        scratch_shapes=[
            pltpu.VMEM((4,) + flat, F32),
            pltpu.VMEM((2, 2, 3, 2, CELLS, DIM), F32),
            pltpu.VMEM((2, 2, 2, 2, 2, CELLS, DIM), F32),
            pltpu.VMEM((4, KEYS, 6 * DIM), BF16),
            pltpu.VMEM((KEYS, 4 * DIM), BF16),
            pltpu.VMEM((2, 2, HALF, 6 * DIM), BF16),
            pltpu.VMEM((2, 2, HALF, 4 * DIM), BF16),
            pltpu.VMEM((6, KEYS, HALF), F32),
            pltpu.VMEM((6, KEYS, HALF), F32),
            pltpu.VMEM((6, 8, HALF), F32),
            pltpu.VMEM((2, 2, 8, HALF), F32),
            pltpu.VMEM((2, 4, 8, HALF), F32),
            pltpu.VMEM((2, 2, 8, HALF), F32),
            pltpu.VMEM((2, 2, 2, 2, DIM, CELLS), F32),
            pltpu.VMEM((2, 2, 2, DIM, CELLS), F32),
            pltpu.VMEM((2, 3, DIM, CELLS), F32),
            pltpu.VMEM((2, 3, 2, CELLS, DIM), F32),
            pltpu.VMEM((2, 3, 2, CELLS, DIM), F32),
            pltpu.VMEM((2, 3, 2, CELLS, DIM), F32),
            pltpu.VMEM((2, 2, 2, CELLS, DIM), F32),
            pltpu.SemaphoreType.DMA((4,)),
            sems(2), sems(2), sems(3, 2), sems(2), sems(2), sems(2), sems(4), sems(), sems(3),
            sems(3), sems(2), sems(), sems(3),
        ],
        compiler_params=pltpu.CompilerParams(
            collective_id=0, has_side_effects=True, vmem_limit_bytes=56 * 1024 * 1024
        ),
    )(*(x.reshape(flat) for x in (query_field, key_field, value_field, output_grad)))
    outs = pl.pallas_call(
        copy_kernel,
        out_shape=[jax.ShapeDtypeStruct(flat, F32)] * 3,
        in_specs=[pl.BlockSpec(memory_space=pl.ANY)] * 3,
        out_specs=[pl.BlockSpec(memory_space=pl.ANY)] * 3,
        scratch_shapes=[pltpu.SemaphoreType.DMA((3,))],
    )(*outs)
    return tuple(x.reshape(frames, rows, cols, channels) for x in outs)


def solution(mesh):
    spec = P(None, "ha", "wa", None)
    return jax.shard_map(
        body, mesh=mesh, in_specs=(spec,) * 4, out_specs=(spec,) * 3, check_vma=False,
    )
```

```python
import jax
import jax.numpy as jnp
from jax import lax
from jax.experimental import pallas as pl
from jax.experimental.pallas import tpu as pltpu
from jax.sharding import PartitionSpec as P

MESH = pl.DeviceIdType.MESH
F32 = jnp.float32
BF16 = jnp.bfloat16
DIM = 128
SCALE = DIM ** -0.5
LOW = -1e30
CELLS = 128
KEYS = 3 * CELLS
HALF = 4 * CELLS


def halves(x):
    hi = x.astype(BF16)
    return hi, (x - hi.astype(F32)).astype(BF16)


def thirds(x):
    hi = x.astype(BF16)
    rest = x - hi.astype(F32)
    mid = rest.astype(BF16)
    return hi, mid, (rest - mid.astype(F32)).astype(BF16)


def dot(a, b, dims):
    return lax.dot_general(a, b, (dims, ((), ())), preferred_element_type=F32)


def kernel(
    q_in, k_in, v_in, g_in, dq_out, dk_out, dv_out,
    raw, kvb, qb, kp, lv, rq, ro, wbuf, dbuf, rel, st, sst, sall, gst, dqt, dqs, dqr, own, halo, yret, zret,
    in_sem, near_sem, far_sem, y_sem, zq_sem, xq_sem, diag_sem, sibq_sem, rel_sem, pair_sem, stat_sem,
    yr_sem, zr_sem, dqs_sem, dq_sem,
):
    ha, wa = lax.axis_index("ha"), lax.axis_index("wa")
    row, xl = ha // 2, ha % 2
    core = wa % 2
    chip = wa // 2
    zp = chip % 2
    tile = chip // 2
    side = 2 * zp - 1
    up = 2 * xl - 1

    sib_id = (ha, wa + 1 - 2 * core)
    near_id = (ha, (wa + 2 * side + 32) % 32)
    far_to = (ha, (wa - 4 * side + 32) % 32)
    far_from = (ha, (wa + 4 * side + 32) % 32)
    zpair = (ha, wa - 2 * side)
    xpair = (ha - up, wa)
    diag = (ha - up, wa - 2 * side)
    y_to = ((ha + 2 * up + 8) % 8, wa)
    y_from = ((ha - 2 * up + 8) % 8, wa)

    side_in = jnp.where(zp == 0, tile > 0, tile < 7)
    far_out = jnp.where(zp == 0, tile < 7, tile > 0)
    y_out = jnp.where(xl == 1, row < 3, row > 0)
    y_in = jnp.where(xl == 1, row > 0, row < 3)
    z_first = (tile > 0) & (tile < 7)

    barrier = pltpu.get_barrier_semaphore()
    partners = (sib_id, near_id, far_to, far_from, zpair, xpair, diag, y_to, y_from)
    for device in partners:
        pl.semaphore_signal(barrier, inc=1, device_id=device, device_id_type=MESH)

    to_relay = (chip == 6) | (chip == 9)
    relay = (chip == 14) | (chip == 1)
    from_relay = (chip == 8) | (chip == 7)
    turn = jnp.where((chip == 6) | (chip == 1), 1, -1)
    jump = jnp.where((chip == 1) | (chip == 8), 1, -1)
    cross_id = (ha, (wa + 16 * turn + 32) % 32)
    jump_id = (ha, (wa + 12 * jump + 32) % 32)

    @pl.when(to_relay | relay)
    def _():
        pl.semaphore_signal(barrier, inc=1, device_id=cross_id, device_id_type=MESH)

    @pl.when(relay | from_relay)
    def _():
        pl.semaphore_signal(barrier, inc=1, device_id=jump_id, device_id_type=MESH)

    loads = [
        pltpu.make_async_copy(ref, raw.at[i], in_sem.at[i]) for i, ref in enumerate((k_in, v_in, q_in, g_in))
    ]
    for load in loads:
        load.start()
    for load in loads:
        load.wait()
    for h in range(2):
        for i in range(4):
            part = raw[i, :, :, h * DIM:(h + 1) * DIM].reshape(CELLS, DIM)
            if i < 2:
                kvb[h, 0, 0, i] = part
            else:
                qb[h, xl, zp, core, i - 2] = part
    extra = jnp.where(relay, 2, jnp.where(to_relay | from_relay, 1, 0))
    pl.semaphore_wait(barrier, len(partners) + extra)

    def remote(src, dst, sems, index, device):
        return pltpu.make_async_remote_copy(
            src_ref=src, dst_ref=dst, send_sem=sems.at[(0,) + index], recv_sem=sems.at[(1,) + index],
            device_id=device, device_id_type=MESH,
        )

    def near_copy(h, kv):
        return remote(kvb.at[h, 0, 0, kv], kvb.at[h, 0, 1, kv], near_sem, (h, kv), near_id)

    def far_copy(h, kv):
        return remote(kvb.at[h, 0, 0, kv], kvb.at[h, 0, 2, kv], far_sem, (h, kv), far_to)

    def relay_copy(h, kv):
        return remote(kvb.at[h, 0, 0, kv], rel.at[h, kv], rel_sem, (h, kv), cross_id)

    def jump_copy(h, kv):
        return remote(rel.at[h, kv], kvb.at[h, 0, 2, kv], far_sem, (h, kv), jump_id)

    def y_copy(h, unit, kv):
        return remote(kvb.at[h, 0, unit, kv], kvb.at[h, 1, unit, kv], y_sem, (h, unit, kv), y_to)

    def q_copy(h, half, place, part, sems, device):
        block = qb.at[h, half, place, core, part]
        return remote(block, block, sems, (h, part), device)

    def zq_copy(h, part):
        return q_copy(h, xl, zp, part, zq_sem, zpair)

    def xq_copy(h, part):
        return q_copy(h, xl, zp, part, xq_sem, xpair)

    def diag_by_x(h, part):
        return q_copy(h, xl, 1 - zp, part, diag_sem, xpair)

    def diag_by_z(h, part):
        return q_copy(h, 1 - xl, zp, part, diag_sem, zpair)

    def slot_place(slot):
        return xl + (slot // 2) * (1 - 2 * xl), zp + (slot % 2) * (1 - 2 * zp)

    def sib_copy(h, slot):
        half, place = slot_place(slot)
        block = qb.at[h, half, place, core]
        return remote(block, block, sibq_sem, (h, slot), sib_id)

    def first_sends(h):
        @pl.when(y_out)
        def _():
            y_copy(h, 0, 0).start()
            y_copy(h, 0, 1).start()

        for part in range(2):
            @pl.when(side_in)
            def _():
                near_copy(h, part).start()

            @pl.when(to_relay)
            def _():
                relay_copy(h, part).start()

            @pl.when(far_out & jnp.logical_not(to_relay))
            def _():
                far_copy(h, part).start()

            zq_copy(h, part).start()
            xq_copy(h, part).start()
        sib_copy(h, 0).start()

    def pass_keys(h, kv):
        @pl.when(relay)
        def _():
            relay_copy(h, kv).wait_recv()
            jump_copy(h, kv).start()

        @pl.when(side_in)
        def _():
            near_copy(h, kv).wait_recv()

            @pl.when(y_out)
            def _():
                y_copy(h, 1, kv).start()

            far_copy(h, kv).wait_recv()

            @pl.when(y_out)
            def _():
                y_copy(h, 2, kv).start()

    def pass_queries(h):
        xq_copy(h, 1).wait_recv()
        diag_by_z(h, 1).start()
        zq_copy(h, 0).wait_recv()

        @pl.when(z_first)
        def _():
            diag_by_x(h, 0).start()

        xq_copy(h, 0).wait_recv()
        sib_copy(h, 2).start()

        @pl.when(jnp.logical_not(z_first))
        def _():
            diag_by_z(h, 0).start()

    def last_pass(h):
        pass_keys(h, 1)
        zq_copy(h, 1).wait_recv()
        sib_copy(h, 1).start()

    def last_queries(h):
        for part in range(2):
            diag_by_x(h, part).wait_recv()
        sib_copy(h, 3).start()

    def prepare_queries(h, low):
        def one(slot, c):
            sib_copy(h, slot).wait_recv()
            half, place = slot_place(slot)
            for blk in range(2):
                q1, q2, q3 = thirds(qb[h, half, place, blk, 0] * SCALE)
                o1, o2 = halves(qb[h, half, place, blk, 1])
                rows = pl.ds(pl.multiple_of(place * (2 * CELLS) + blk * CELLS, CELLS), CELLS)
                for i, part in enumerate((q1, q1, q2, q2, q3, q1)):
                    rq[h, half, rows, i * DIM:(i + 1) * DIM] = part
                for i, part in enumerate((o1, o1, o2, o2)):
                    ro[h, half, rows, i * DIM:(i + 1) * DIM] = part
            return c

        lax.fori_loop(low, low + 2, one, 0)

    def prepare_keys(h, line):
        for unit in range(3):
            rows = slice(unit * CELLS, (unit + 1) * CELLS)
            k1, k2, k3 = thirds(kvb[h, line, unit, 0])
            v1, v2 = halves(kvb[h, line, unit, 1])
            for i, part in enumerate((k1, k2, k1, k2, k1, k3)):
                kp[2 * h + line, rows, i * DIM:(i + 1) * DIM] = part
            for i, part in enumerate((v1, v2, v1, v2)):
                lv[rows, i * DIM:(i + 1) * DIM] = part

    far_keys = lax.broadcasted_iota(jnp.int32, (KEYS, 1), 0) >= CELLS
    bias = jnp.where(far_keys, jnp.where(side_in, 0.0, LOW), 0.0)

    def forward_block(h, k, line, half):
        index = 3 * h + k
        scores = dot(kp[2 * h + line], rq[h, half], ((1,), (1,))) + bias
        dprobs = dot(lv[...], ro[h, half], ((1,), (1,)))
        peak = jnp.max(scores, axis=0, keepdims=True)
        weights = jnp.exp(scores - peak)
        wbuf[index] = weights
        dbuf[index] = dprobs
        st[index, 0:1] = peak
        st[index, 1:2] = jnp.sum(weights, axis=0, keepdims=True)
        st[index, 2:3] = jnp.sum(weights * dprobs, axis=0, keepdims=True)

    def forward(h, before):
        def one(step, c):
            for i in range(3):
                @pl.when(step == i)
                def _():
                    before[i]()

            half = jnp.where(step == 0, xl, 1 - xl)
            line = step // 2
            here = (step < 2) | y_in

            @pl.when(here & (step != 1))
            def _():
                @pl.when(step == 2)
                def _():
                    for kv in range(2):
                        y_copy(h, 0, kv).wait_recv()

                        @pl.when(side_in)
                        def _():
                            y_copy(h, 1, kv).wait_recv()
                            y_copy(h, 2, kv).wait_recv()

                prepare_keys(h, line)

            @pl.when(here)
            def _():
                forward_block(h, step, line, half)

            @pl.when(jnp.logical_not(here))
            def _():
                st[3 * h + 2, 0:1] = jnp.full((1, HALF), LOW, F32)
                st[3 * h + 2, 1:3] = jnp.zeros((2, HALF), F32)

            return c

        lax.fori_loop(0, 3, one, 0)

    me = 2 * xl + zp

    def merge(triples):
        peak = triples[0][0]
        for p, _, _ in triples[1:]:
            peak = jnp.maximum(peak, p)
        total = jnp.zeros_like(peak)
        center = jnp.zeros_like(peak)
        for p, s, c in triples:
            factor = jnp.exp(p - peak)
            total += s * factor
            center += c * factor
        return peak, total, center

    def triple(ref, base):
        return tuple(ref[base + i:base + i + 1] for i in range(3))

    def pair_copy(h):
        return remote(sst.at[h, core], sst.at[h, core], pair_sem, (h,), sib_id)

    def stat_copy(h, which):
        device = (xpair, zpair, diag)[which]
        return remote(sall.at[h, me], sall.at[h, me], stat_sem, (h, which), device)

    def start_stats(h):
        merged = (triple(st.at[3 * h], 0), merge([triple(st.at[3 * h + 1], 0), triple(st.at[3 * h + 2], 0)]))
        for half in range(2):
            for i in range(3):
                value = jnp.where(half == xl, merged[0][i], merged[1][i])
                sst[h, core, 3 * half + i:3 * half + i + 1] = value
        sst[h, core, 6:8] = jnp.zeros((2, HALF), F32)
        pair_copy(h).start()

    def share_stats(h):
        pair_copy(h).wait_recv()
        for half in range(2):
            merged = merge([triple(sst.at[h, i], 3 * half) for i in range(2)])
            for i in range(3):
                sall[h, me, 3 * half + i:3 * half + i + 1] = merged[i]
        sall[h, me, 6:8] = jnp.zeros((2, HALF), F32)
        for which in range(3):
            stat_copy(h, which).start()

    def end_stats(h):
        for which in range(3):
            stat_copy(h, which).wait_recv()
        for half in range(2):
            peak, total, center = merge([triple(sall.at[h, i], 3 * half) for i in range(4)])
            inverse = 1.0 / total
            gst[h, half, 0:1] = peak
            gst[h, half, 1:2] = inverse
            gst[h, half, 2:3] = center * inverse

    def backward_block(h, k, line, half):
        index = 3 * h + k
        alpha = jnp.exp(st[index, 0:1] - gst[h, half, 0:1]) * gst[h, half, 1:2]
        probs = wbuf[index] * alpha
        dscores = probs * (dbuf[index] - gst[h, half, 2:3])
        p1, p2 = halves(probs)
        s1, s2 = halves(dscores)
        q12 = rq[h, half, :, DIM:3 * DIM]
        o12 = ro[h, half, :, DIM:3 * DIM]
        k12 = kp[2 * h + line, :, 0:2 * DIM]
        dv = dot(p1, o12, ((1,), (0,))) + dot(p2, o12, ((1,), (0,)))
        dk = dot(s1, q12, ((1,), (0,))) + dot(s2, q12, ((1,), (0,)))
        dq = dot(k12, s1, ((0,), (0,))) + dot(k12, s2, ((0,), (0,)))
        dq = dq[:DIM] + dq[DIM:]
        for place in range(2):
            for blk in range(2):
                at = (2 * place + blk) * CELLS
                dqt[h, half, place, blk] += dq[:, at:at + CELLS]
        return dk[:, :DIM] + dk[:, DIM:], dv[:, :DIM] + dv[:, DIM:]

    def yr_copy(h, unit, kind):
        return remote(halo.at[h, unit, kind], yret.at[h, unit, kind], yr_sem, (h, unit, kind), y_from)

    def dqs_copy(h):
        return remote(dqt.at[h, :, :, 1 - core], dqs.at[h], dqs_sem, (h,), sib_id)

    def backward(h):
        dqt[h] = jnp.zeros(dqt.shape[1:], F32)
        own[h] = jnp.zeros(own.shape[1:], F32)

        def one(turn, c):
            step = 2 - turn

            @pl.when((step < 2) | y_in)
            def _():
                half = jnp.where(step == 0, xl, 1 - xl)
                dk, dv = backward_block(h, step, step // 2, half)

                @pl.when(step == 2)
                def _():
                    for unit in range(3):
                        halo[h, unit, 0] = dk[unit * CELLS:(unit + 1) * CELLS]
                        halo[h, unit, 1] = dv[unit * CELLS:(unit + 1) * CELLS]

                    @pl.when(side_in)
                    def _():
                        for unit in (2, 1):
                            for kind in range(2):
                                yr_copy(h, unit, kind).start()

                    for kind in range(2):
                        yr_copy(h, 0, kind).start()

                @pl.when(step < 2)
                def _():
                    for unit in range(3):
                        own[h, unit, 0] += dk[unit * CELLS:(unit + 1) * CELLS]
                        own[h, unit, 1] += dv[unit * CELLS:(unit + 1) * CELLS]

            return c

        lax.fori_loop(0, 3, one, 0)
        dqs_copy(h).start()

    def dq_copy(h, which):
        device = (xpair, zpair, diag)[which]
        half, place = ((1 - xl, zp), (xl, 1 - zp), (1 - xl, 1 - zp))[which]
        return remote(dqt.at[h, half, place, core], dqr.at[h, which], dq_sem, (h, which), device)

    def share_dq(h):
        dqs_copy(h).wait_recv()
        for half in range(2):
            for place in range(2):
                dqt[h, half, place, core] += dqs[h, half, place]
        for which in range(3):
            dq_copy(h, which).start()

    def zr_copy(h, which, kind):
        device = (near_id, far_from)[which]
        return remote(own.at[h, 1 + which, kind], zret.at[h, which, kind], zr_sem, (h, which, kind), device)

    def pass_back(h):
        for which in (1, 0):
            for kind in range(2):
                @pl.when(side_in)
                def _():
                    @pl.when(y_out)
                    def _():
                        yr_copy(h, 1 + which, kind).wait_recv()
                        own[h, 1 + which, kind] += yret[h, 1 + which, kind]

                    zr_copy(h, which, kind).start()

    def finish(h):
        lanes = slice(h * DIM, (h + 1) * DIM)
        for which in range(3):
            dq_copy(h, which).wait_recv()
        dq = dqt[h, xl, zp, core] + dqr[h, 0] + dqr[h, 1] + dqr[h, 2]
        dq_out[:, :, lanes] = (dq.T * SCALE).reshape(32, 4, DIM)

        @pl.when(y_out)
        def _():
            yr_copy(h, 0, 0).wait_recv()
            yr_copy(h, 0, 1).wait_recv()
            own[h, 0] += yret[h, 0]

        @pl.when(far_out)
        def _():
            zr_copy(h, 1, 0).wait_recv()
            zr_copy(h, 1, 1).wait_recv()
            own[h, 0] += zret[h, 1]

        @pl.when(side_in)
        def _():
            zr_copy(h, 0, 0).wait_recv()
            zr_copy(h, 0, 1).wait_recv()
            own[h, 0] += zret[h, 0]

        dk_out[:, :, lanes] = own[h, 0, 0].reshape(32, 4, DIM)
        dv_out[:, :, lanes] = own[h, 0, 1].reshape(32, 4, DIM)

    def all_left(h):
        for part in range(2):
            @pl.when(y_out)
            def _():
                y_copy(h, 0, part).wait_send()

                @pl.when(side_in)
                def _():
                    y_copy(h, 1, part).wait_send()
                    y_copy(h, 2, part).wait_send()

            @pl.when(side_in)
            def _():
                near_copy(h, part).wait_send()
                zr_copy(h, 0, part).wait_send()
                zr_copy(h, 1, part).wait_send()

            @pl.when(to_relay)
            def _():
                relay_copy(h, part).wait_send()

            @pl.when((far_out & jnp.logical_not(to_relay)) | relay)
            def _():
                far_copy(h, part).wait_send()

            zq_copy(h, part).wait_send()
            xq_copy(h, part).wait_send()
            diag_by_x(h, part).wait_send()

        @pl.when(y_in)
        def _():
            for kind in range(2):
                yr_copy(h, 0, kind).wait_send()

                @pl.when(side_in)
                def _():
                    yr_copy(h, 1, kind).wait_send()
                    yr_copy(h, 2, kind).wait_send()

        for slot in range(4):
            sib_copy(h, slot).wait_send()
        pair_copy(h).wait_send()
        dqs_copy(h).wait_send()
        for which in range(3):
            stat_copy(h, which).wait_send()
            dq_copy(h, which).wait_send()

    first_sends(0)
    first_sends(1)

    @pl.when(jnp.logical_not(side_in))
    def _():
        for h in range(2):
            for line in range(2):
                kvb[h, line, 1:3] = jnp.zeros((2, 2, CELLS, DIM), F32)

    def head0_start():
        pass_keys(0, 0)
        pass_queries(0)
        last_pass(0)
        prepare_queries(0, 0)

    def head0_other():
        last_queries(0)
        prepare_queries(0, 2)

    def head0_halo():
        pass_keys(1, 0)

    def head1_start():
        prepare_queries(1, 0)

    def head1_other():
        last_queries(1)
        prepare_queries(1, 2)

    def head1_halo():
        end_stats(0)
        backward(0)

    forward(0, (head0_start, head0_other, head0_halo))
    start_stats(0)
    pass_queries(1)
    last_pass(1)
    share_stats(0)
    forward(1, (head1_start, head1_other, head1_halo))
    start_stats(1)
    share_dq(0)
    share_stats(1)
    pass_back(0)
    end_stats(1)
    backward(1)
    share_dq(1)
    finish(0)
    pass_back(1)
    finish(1)
    all_left(0)
    all_left(1)


def copy_kernel(*refs):
    for i in range(3):
        refs[3 + i][...] = refs[i][...]


def body(query_field, key_field, value_field, output_grad):
    frames, rows, cols, channels = query_field.shape
    flat = (frames * rows, cols, channels)

    def sems(*shape):
        return pltpu.SemaphoreType.DMA((2, 2) + shape)

    outs = pl.pallas_call(
        kernel,
        out_shape=[jax.ShapeDtypeStruct(flat, F32)] * 3,
        in_specs=[pl.BlockSpec(memory_space=pl.ANY)] * 4,
        out_specs=[pl.BlockSpec(memory_space=pltpu.VMEM)] * 3,
        scratch_shapes=[
            pltpu.VMEM((4,) + flat, F32),
            pltpu.VMEM((2, 2, 3, 2, CELLS, DIM), F32),
            pltpu.VMEM((2, 2, 2, 2, 2, CELLS, DIM), F32),
            pltpu.VMEM((4, KEYS, 6 * DIM), BF16),
            pltpu.VMEM((KEYS, 4 * DIM), BF16),
            pltpu.VMEM((2, 2, HALF, 6 * DIM), BF16),
            pltpu.VMEM((2, 2, HALF, 4 * DIM), BF16),
            pltpu.VMEM((6, KEYS, HALF), F32),
            pltpu.VMEM((6, KEYS, HALF), F32),
            pltpu.VMEM((2, 2, CELLS, DIM), F32),
            pltpu.VMEM((6, 8, HALF), F32),
            pltpu.VMEM((2, 2, 8, HALF), F32),
            pltpu.VMEM((2, 4, 8, HALF), F32),
            pltpu.VMEM((2, 2, 8, HALF), F32),
            pltpu.VMEM((2, 2, 2, 2, DIM, CELLS), F32),
            pltpu.VMEM((2, 2, 2, DIM, CELLS), F32),
            pltpu.VMEM((2, 3, DIM, CELLS), F32),
            pltpu.VMEM((2, 3, 2, CELLS, DIM), F32),
            pltpu.VMEM((2, 3, 2, CELLS, DIM), F32),
            pltpu.VMEM((2, 3, 2, CELLS, DIM), F32),
            pltpu.VMEM((2, 2, 2, CELLS, DIM), F32),
            pltpu.SemaphoreType.DMA((4,)),
            sems(2), sems(2), sems(3, 2), sems(2), sems(2), sems(2), sems(4), sems(2), sems(), sems(3),
            sems(3, 2), sems(2, 2), sems(), sems(3),
        ],
        compiler_params=pltpu.CompilerParams(
            collective_id=0, has_side_effects=True, vmem_limit_bytes=56 * 1024 * 1024
        ),
    )(*(x.reshape(flat) for x in (query_field, key_field, value_field, output_grad)))
    outs = pl.pallas_call(
        copy_kernel,
        out_shape=[jax.ShapeDtypeStruct(flat, F32)] * 3,
        in_specs=[pl.BlockSpec(memory_space=pltpu.VMEM)] * 3,
        out_specs=[pl.BlockSpec(memory_space=pltpu.VMEM)] * 3,
    )(*outs)
    return tuple(x.reshape(frames, rows, cols, channels) for x in outs)


def solution(mesh):
    spec = P(None, "ha", "wa", None)
    return jax.shard_map(
        body, mesh=mesh, in_specs=(spec,) * 4, out_specs=(spec,) * 3, check_vma=False,
    )
```

```python
import jax
import jax.numpy as jnp
from jax import lax
from jax.experimental import pallas as pl
from jax.experimental.pallas import tpu as pltpu
from jax.sharding import PartitionSpec as P

MESH = pl.DeviceIdType.MESH
F32 = jnp.float32
BF16 = jnp.bfloat16
DIM = 128
SCALE = DIM ** -0.5
LOW = -1e30
CELLS = 128
KEYS = 3 * CELLS
HALF = 4 * CELLS


def halves(x):
    hi = x.astype(BF16)
    return hi, (x - hi.astype(F32)).astype(BF16)


def thirds(x):
    hi = x.astype(BF16)
    rest = x - hi.astype(F32)
    mid = rest.astype(BF16)
    return hi, mid, (rest - mid.astype(F32)).astype(BF16)


def dot(a, b, dims):
    return lax.dot_general(a, b, (dims, ((), ())), preferred_element_type=F32)


def kernel(
    q_in, k_in, v_in, g_in, dq_out, dk_out, dv_out,
    raw, kvb, qb, kp, lv, rq, ro, wbuf, dbuf, rel, st, sall, gst, dqt, dqs, dqr, own, halo, yret, zret,
    in_sem, near_sem, far_sem, y_sem, zq_sem, xq_sem, diag_sem, sibq_sem, rel_sem, stat_sem,
    yr_sem, zr_sem, dqs_sem, dq_sem,
):
    ha, wa = lax.axis_index("ha"), lax.axis_index("wa")
    row, xl = ha // 2, ha % 2
    core = wa % 2
    chip = wa // 2
    zp = chip % 2
    tile = chip // 2
    side = 2 * zp - 1
    up = 2 * xl - 1

    sib_id = (ha, wa + 1 - 2 * core)
    near_id = (ha, (wa + 2 * side + 32) % 32)
    far_to = (ha, (wa - 4 * side + 32) % 32)
    far_from = (ha, (wa + 4 * side + 32) % 32)
    zpair = (ha, wa - 2 * side)
    xpair = (ha - up, wa)
    diag = (ha - up, wa - 2 * side)
    y_to = ((ha + 2 * up + 8) % 8, wa)
    y_from = ((ha - 2 * up + 8) % 8, wa)

    side_in = jnp.where(zp == 0, tile > 0, tile < 7)
    far_out = jnp.where(zp == 0, tile < 7, tile > 0)
    y_out = jnp.where(xl == 1, row < 3, row > 0)
    y_in = jnp.where(xl == 1, row > 0, row < 3)
    z_first = (tile > 0) & (tile < 7)

    barrier = pltpu.get_barrier_semaphore()
    flip = 1 - 2 * core
    group = (diag, zpair, xpair, (ha - up, wa - 2 * side + flip), (ha, wa - 2 * side + flip), (ha - up, wa + flip), sib_id)
    partners = group + (near_id, far_to, far_from, y_to, y_from)
    for device in partners:
        pl.semaphore_signal(barrier, inc=1, device_id=device, device_id_type=MESH)

    to_relay = (chip == 6) | (chip == 9)
    relay = (chip == 14) | (chip == 1)
    from_relay = (chip == 8) | (chip == 7)
    turn = jnp.where((chip == 6) | (chip == 1), 1, -1)
    jump = jnp.where((chip == 1) | (chip == 8), 1, -1)
    cross_id = (ha, (wa + 16 * turn + 32) % 32)
    jump_id = (ha, (wa + 12 * jump + 32) % 32)

    @pl.when(to_relay | relay)
    def _():
        pl.semaphore_signal(barrier, inc=1, device_id=cross_id, device_id_type=MESH)

    @pl.when(relay | from_relay)
    def _():
        pl.semaphore_signal(barrier, inc=1, device_id=jump_id, device_id_type=MESH)

    loads = [
        pltpu.make_async_copy(ref, raw.at[i], in_sem.at[i]) for i, ref in enumerate((k_in, v_in, q_in, g_in))
    ]
    for load in loads:
        load.start()
    for load in loads:
        load.wait()
    for h in range(2):
        for i in range(4):
            part = raw[i, :, :, h * DIM:(h + 1) * DIM].reshape(CELLS, DIM)
            if i < 2:
                kvb[h, 0, 0, i] = part
            else:
                qb[h, xl, zp, core, i - 2] = part
    extra = jnp.where(relay, 2, jnp.where(to_relay | from_relay, 1, 0))
    pl.semaphore_wait(barrier, len(partners) + extra)

    def remote(src, dst, sems, index, device):
        return pltpu.make_async_remote_copy(
            src_ref=src, dst_ref=dst, send_sem=sems.at[(0,) + index], recv_sem=sems.at[(1,) + index],
            device_id=device, device_id_type=MESH,
        )

    def near_copy(h, kv):
        return remote(kvb.at[h, 0, 0, kv], kvb.at[h, 0, 1, kv], near_sem, (h, kv), near_id)

    def far_copy(h, kv):
        return remote(kvb.at[h, 0, 0, kv], kvb.at[h, 0, 2, kv], far_sem, (h, kv), far_to)

    def relay_copy(h, kv):
        return remote(kvb.at[h, 0, 0, kv], rel.at[h, kv], rel_sem, (h, kv), cross_id)

    def jump_copy(h, kv):
        return remote(rel.at[h, kv], kvb.at[h, 0, 2, kv], far_sem, (h, kv), jump_id)

    def y_copy(h, unit, kv):
        return remote(kvb.at[h, 0, unit, kv], kvb.at[h, 1, unit, kv], y_sem, (h, unit, kv), y_to)

    def q_copy(h, half, place, part, sems, device):
        block = qb.at[h, half, place, core, part]
        return remote(block, block, sems, (h, part), device)

    def zq_copy(h, part):
        return q_copy(h, xl, zp, part, zq_sem, zpair)

    def xq_copy(h, part):
        return q_copy(h, xl, zp, part, xq_sem, xpair)

    def diag_by_x(h, part):
        return q_copy(h, xl, 1 - zp, part, diag_sem, xpair)

    def diag_by_z(h, part):
        return q_copy(h, 1 - xl, zp, part, diag_sem, zpair)

    def slot_place(slot):
        return xl + (slot // 2) * (1 - 2 * xl), zp + (slot % 2) * (1 - 2 * zp)

    def sib_copy(h, slot):
        half, place = slot_place(slot)
        block = qb.at[h, half, place, core]
        return remote(block, block, sibq_sem, (h, slot), sib_id)

    def y_sends(h):
        @pl.when(y_out)
        def _():
            y_copy(h, 0, 0).start()
            y_copy(h, 0, 1).start()

    def x_sends(h):
        for part in (1, 0):
            xq_copy(h, part).start()
        sib_copy(h, 0).start()

    def z_sends(h):
        for part in range(2):
            @pl.when(side_in)
            def _():
                near_copy(h, part).start()

            @pl.when(to_relay)
            def _():
                relay_copy(h, part).start()

            @pl.when(far_out & jnp.logical_not(to_relay))
            def _():
                far_copy(h, part).start()

            zq_copy(h, part).start()

    def pass_keys(h, kv):
        @pl.when(relay)
        def _():
            relay_copy(h, kv).wait_recv()
            jump_copy(h, kv).start()

        @pl.when(side_in)
        def _():
            near_copy(h, kv).wait_recv()

            @pl.when(y_out)
            def _():
                y_copy(h, 1, kv).start()

            far_copy(h, kv).wait_recv()

            @pl.when(y_out)
            def _():
                y_copy(h, 2, kv).start()

    def pass_queries(h):
        xq_copy(h, 1).wait_recv()
        diag_by_z(h, 1).start()
        zq_copy(h, 0).wait_recv()

        @pl.when(z_first)
        def _():
            diag_by_x(h, 0).start()

        xq_copy(h, 0).wait_recv()
        sib_copy(h, 2).start()

        @pl.when(jnp.logical_not(z_first))
        def _():
            diag_by_z(h, 0).start()

    def last_pass(h):
        pass_keys(h, 1)
        zq_copy(h, 1).wait_recv()
        sib_copy(h, 1).start()

    def last_queries(h):
        for part in range(2):
            diag_by_x(h, part).wait_recv()
        sib_copy(h, 3).start()

    def prepare_queries(h, low):
        def one(slot, c):
            sib_copy(h, slot).wait_recv()
            half, place = slot_place(slot)
            for blk in range(2):
                q1, q2, q3 = thirds(qb[h, half, place, blk, 0] * SCALE)
                o1, o2 = halves(qb[h, half, place, blk, 1])
                rows = pl.ds(pl.multiple_of(place * (2 * CELLS) + blk * CELLS, CELLS), CELLS)
                for i, part in enumerate((q1, q1, q2, q2, q3, q1)):
                    rq[h, half, rows, i * DIM:(i + 1) * DIM] = part
                for i, part in enumerate((o1, o1, o2, o2)):
                    ro[h, half, rows, i * DIM:(i + 1) * DIM] = part
            return c

        lax.fori_loop(low, low + 2, one, 0)

    def prepare_keys(h, line):
        for unit in range(3):
            rows = slice(unit * CELLS, (unit + 1) * CELLS)
            k1, k2, k3 = thirds(kvb[h, line, unit, 0])
            v1, v2 = halves(kvb[h, line, unit, 1])
            for i, part in enumerate((k1, k2, k1, k2, k1, k3)):
                kp[2 * h + line, rows, i * DIM:(i + 1) * DIM] = part
            for i, part in enumerate((v1, v2, v1, v2)):
                lv[rows, i * DIM:(i + 1) * DIM] = part

    far_keys = lax.broadcasted_iota(jnp.int32, (KEYS, 1), 0) >= CELLS
    bias = jnp.where(far_keys, jnp.where(side_in, 0.0, LOW), 0.0)

    def forward_block(h, k, line, half):
        index = 3 * h + k
        scores = dot(kp[2 * h + line], rq[h, half], ((1,), (1,))) + bias
        dprobs = dot(lv[...], ro[h, half], ((1,), (1,)))
        peak = jnp.max(scores, axis=0, keepdims=True)
        weights = jnp.exp(scores - peak)
        wbuf[index] = weights
        dbuf[index] = dprobs
        st[index, 0:1] = peak
        st[index, 1:2] = jnp.sum(weights, axis=0, keepdims=True)
        st[index, 2:3] = jnp.sum(weights * dprobs, axis=0, keepdims=True)

    def forward(h, before):
        def one(step, c):
            for i in range(3):
                @pl.when(step == i)
                def _():
                    before[i]()

            half = jnp.where(step == 0, xl, 1 - xl)
            line = step // 2
            here = (step < 2) | y_in

            @pl.when(here & (step != 1))
            def _():
                @pl.when(step == 2)
                def _():
                    for kv in range(2):
                        y_copy(h, 0, kv).wait_recv()

                        @pl.when(side_in)
                        def _():
                            y_copy(h, 1, kv).wait_recv()
                            y_copy(h, 2, kv).wait_recv()

                prepare_keys(h, line)

            @pl.when(here)
            def _():
                forward_block(h, step, line, half)

            @pl.when(jnp.logical_not(here))
            def _():
                st[3 * h + 2, 0:1] = jnp.full((1, HALF), LOW, F32)
                st[3 * h + 2, 1:3] = jnp.zeros((2, HALF), F32)

            return c

        lax.fori_loop(0, 3, one, 0)

    me = 4 * xl + 2 * zp + core

    def merge(triples):
        peak = triples[0][0]
        for p, _, _ in triples[1:]:
            peak = jnp.maximum(peak, p)
        total = jnp.zeros_like(peak)
        center = jnp.zeros_like(peak)
        for p, s, c in triples:
            factor = jnp.exp(p - peak)
            total += s * factor
            center += c * factor
        return peak, total, center

    def triple(ref, base):
        return tuple(ref[base + i:base + i + 1] for i in range(3))

    def stat_copy(h, which):
        place = sall.at[h, me]
        return remote(place, place, stat_sem, (h, which), group[which])

    def start_stats(h):
        merged = (triple(st.at[3 * h], 0), merge([triple(st.at[3 * h + 1], 0), triple(st.at[3 * h + 2], 0)]))
        for half in range(2):
            for i in range(3):
                value = jnp.where(half == xl, merged[0][i], merged[1][i])
                sall[h, me, 3 * half + i:3 * half + i + 1] = value
        sall[h, me, 6:8] = jnp.zeros((2, HALF), F32)
        for which in range(7):
            stat_copy(h, which).start()

    def end_stats(h):
        for which in range(7):
            stat_copy(h, which).wait_recv()
        for half in range(2):
            peak, total, center = merge([triple(sall.at[h, i], 3 * half) for i in range(8)])
            inverse = 1.0 / total
            gst[h, half, 0:1] = peak
            gst[h, half, 1:2] = inverse
            gst[h, half, 2:3] = center * inverse

    def backward_block(h, k, line, half, give):
        index = 3 * h + k
        alpha = jnp.exp(st[index, 0:1] - gst[h, half, 0:1]) * gst[h, half, 1:2]
        probs = wbuf[index] * alpha
        dscores = probs * (dbuf[index] - gst[h, half, 2:3])
        p1, p2 = halves(probs)
        o12 = ro[h, half, :, DIM:3 * DIM]
        dv = dot(p1, o12, ((1,), (0,))) + dot(p2, o12, ((1,), (0,)))
        give(1, dv[:, :DIM] + dv[:, DIM:])
        s1, s2 = halves(dscores)
        q12 = rq[h, half, :, DIM:3 * DIM]
        dk = dot(s1, q12, ((1,), (0,))) + dot(s2, q12, ((1,), (0,)))
        give(0, dk[:, :DIM] + dk[:, DIM:])
        k12 = kp[2 * h + line, :, 0:2 * DIM]
        dq = dot(k12, s1, ((0,), (0,))) + dot(k12, s2, ((0,), (0,)))
        dq = dq[:DIM] + dq[DIM:]
        for place in range(2):
            for blk in range(2):
                at = (2 * place + blk) * CELLS
                dqt[h, half, place, blk] += dq[:, at:at + CELLS]

    def yr_copy(h, unit, kind):
        return remote(halo.at[h, unit, kind], yret.at[h, unit, kind], yr_sem, (h, unit, kind), y_from)

    def dqs_copy(h):
        return remote(dqt.at[h, :, :, 1 - core], dqs.at[h], dqs_sem, (h,), sib_id)

    def backward(h):
        dqt[h] = jnp.zeros(dqt.shape[1:], F32)
        own[h] = jnp.zeros(own.shape[1:], F32)

        def one(turn, c):
            step = 2 - turn

            @pl.when((step < 2) | y_in)
            def _():
                half = jnp.where(step == 0, xl, 1 - xl)

                def give(kind, value):
                    @pl.when(step == 2)
                    def _():
                        for unit in range(3):
                            halo[h, unit, kind] = value[unit * CELLS:(unit + 1) * CELLS]

                        @pl.when(side_in)
                        def _():
                            yr_copy(h, 2, kind).start()
                            yr_copy(h, 1, kind).start()

                        if kind == 0:
                            yr_copy(h, 0, 0).start()
                            yr_copy(h, 0, 1).start()

                    @pl.when(step < 2)
                    def _():
                        for unit in range(3):
                            own[h, unit, kind] += value[unit * CELLS:(unit + 1) * CELLS]

                backward_block(h, step, step // 2, half, give)

            return c

        lax.fori_loop(0, 3, one, 0)
        dqs_copy(h).start()

    def dq_copy(h, which):
        device = (xpair, zpair, diag)[which]
        half, place = ((1 - xl, zp), (xl, 1 - zp), (1 - xl, 1 - zp))[which]
        return remote(dqt.at[h, half, place, core], dqr.at[h, which], dq_sem, (h, which), device)

    def share_dq(h):
        dqs_copy(h).wait_recv()
        for half in range(2):
            for place in range(2):
                dqt[h, half, place, core] += dqs[h, half, place]
        for which in range(3):
            dq_copy(h, which).start()

    def zr_copy(h, which, kind):
        device = (near_id, far_from)[which]
        return remote(own.at[h, 1 + which, kind], zret.at[h, which, kind], zr_sem, (h, which, kind), device)

    def pass_back(h):
        for kind in (1, 0):
            for which in (1, 0):
                @pl.when(side_in)
                def _():
                    @pl.when(y_out)
                    def _():
                        yr_copy(h, 1 + which, kind).wait_recv()
                        own[h, 1 + which, kind] += yret[h, 1 + which, kind]

                    zr_copy(h, which, kind).start()

    def finish(h):
        lanes = slice(h * DIM, (h + 1) * DIM)
        for which in range(3):
            dq_copy(h, which).wait_recv()
        dq = dqt[h, xl, zp, core] + dqr[h, 0] + dqr[h, 1] + dqr[h, 2]
        dq_out[:, :, lanes] = (dq.T * SCALE).reshape(32, 4, DIM)

        @pl.when(y_out)
        def _():
            yr_copy(h, 0, 0).wait_recv()
            yr_copy(h, 0, 1).wait_recv()
            own[h, 0] += yret[h, 0]

        @pl.when(far_out)
        def _():
            zr_copy(h, 1, 0).wait_recv()
            zr_copy(h, 1, 1).wait_recv()
            own[h, 0] += zret[h, 1]

        @pl.when(side_in)
        def _():
            zr_copy(h, 0, 0).wait_recv()
            zr_copy(h, 0, 1).wait_recv()
            own[h, 0] += zret[h, 0]

        dk_out[:, :, lanes] = own[h, 0, 0].reshape(32, 4, DIM)
        dv_out[:, :, lanes] = own[h, 0, 1].reshape(32, 4, DIM)

    def all_left(h):
        for part in range(2):
            @pl.when(y_out)
            def _():
                y_copy(h, 0, part).wait_send()

                @pl.when(side_in)
                def _():
                    y_copy(h, 1, part).wait_send()
                    y_copy(h, 2, part).wait_send()

            @pl.when(side_in)
            def _():
                near_copy(h, part).wait_send()
                zr_copy(h, 0, part).wait_send()
                zr_copy(h, 1, part).wait_send()

            @pl.when(to_relay)
            def _():
                relay_copy(h, part).wait_send()

            @pl.when((far_out & jnp.logical_not(to_relay)) | relay)
            def _():
                far_copy(h, part).wait_send()

            zq_copy(h, part).wait_send()
            xq_copy(h, part).wait_send()
            diag_by_x(h, part).wait_send()

        @pl.when(y_in)
        def _():
            for kind in range(2):
                yr_copy(h, 0, kind).wait_send()

                @pl.when(side_in)
                def _():
                    yr_copy(h, 1, kind).wait_send()
                    yr_copy(h, 2, kind).wait_send()

        for slot in range(4):
            sib_copy(h, slot).wait_send()
        dqs_copy(h).wait_send()
        for which in range(3):
            dq_copy(h, which).wait_send()
        for which in range(7):
            stat_copy(h, which).wait_send()

    y_sends(0)
    z_sends(0)
    x_sends(0)

    @pl.when(jnp.logical_not(side_in))
    def _():
        for h in range(2):
            for line in range(2):
                kvb[h, line, 1:3] = jnp.zeros((2, 2, CELLS, DIM), F32)

    def head0_start():
        pass_keys(0, 0)
        pass_queries(0)
        z_sends(1)
        x_sends(1)
        last_pass(0)
        y_sends(1)
        prepare_queries(0, 0)

    def head0_other():
        last_queries(0)
        prepare_queries(0, 2)

    def head0_halo():
        pass_keys(1, 0)

    def head1_start():
        prepare_queries(1, 0)

    def head1_other():
        end_stats(0)
        backward(0)
        last_queries(1)
        prepare_queries(1, 2)

    def head1_halo():
        share_dq(0)

    forward(0, (head0_start, head0_other, head0_halo))
    start_stats(0)
    pass_queries(1)
    last_pass(1)
    forward(1, (head1_start, head1_other, head1_halo))
    start_stats(1)
    pass_back(0)
    end_stats(1)
    backward(1)
    share_dq(1)
    finish(0)
    pass_back(1)
    finish(1)
    all_left(0)
    all_left(1)


def copy_kernel(*refs):
    for i in range(3):
        refs[3 + i][...] = refs[i][...]


def body(query_field, key_field, value_field, output_grad):
    frames, rows, cols, channels = query_field.shape
    flat = (frames * rows, cols, channels)

    def sems(*shape):
        return pltpu.SemaphoreType.DMA((2, 2) + shape)

    outs = pl.pallas_call(
        kernel,
        out_shape=[jax.ShapeDtypeStruct(flat, F32)] * 3,
        in_specs=[pl.BlockSpec(memory_space=pl.ANY)] * 4,
        out_specs=[pl.BlockSpec(memory_space=pltpu.VMEM)] * 3,
        scratch_shapes=[
            pltpu.VMEM((4,) + flat, F32),
            pltpu.VMEM((2, 2, 3, 2, CELLS, DIM), F32),
            pltpu.VMEM((2, 2, 2, 2, 2, CELLS, DIM), F32),
            pltpu.VMEM((4, KEYS, 6 * DIM), BF16),
            pltpu.VMEM((KEYS, 4 * DIM), BF16),
            pltpu.VMEM((2, 2, HALF, 6 * DIM), BF16),
            pltpu.VMEM((2, 2, HALF, 4 * DIM), BF16),
            pltpu.VMEM((6, KEYS, HALF), F32),
            pltpu.VMEM((6, KEYS, HALF), F32),
            pltpu.VMEM((2, 2, CELLS, DIM), F32),
            pltpu.VMEM((6, 8, HALF), F32),
            pltpu.VMEM((2, 8, 8, HALF), F32),
            pltpu.VMEM((2, 2, 8, HALF), F32),
            pltpu.VMEM((2, 2, 2, 2, DIM, CELLS), F32),
            pltpu.VMEM((2, 2, 2, DIM, CELLS), F32),
            pltpu.VMEM((2, 3, DIM, CELLS), F32),
            pltpu.VMEM((2, 3, 2, CELLS, DIM), F32),
            pltpu.VMEM((2, 3, 2, CELLS, DIM), F32),
            pltpu.VMEM((2, 3, 2, CELLS, DIM), F32),
            pltpu.VMEM((2, 2, 2, CELLS, DIM), F32),
            pltpu.SemaphoreType.DMA((4,)),
            sems(2), sems(2), sems(3, 2), sems(2), sems(2), sems(2), sems(4), sems(2), sems(7),
            sems(3, 2), sems(2, 2), sems(), sems(3),
        ],
        compiler_params=pltpu.CompilerParams(
            collective_id=0, has_side_effects=True, vmem_limit_bytes=56 * 1024 * 1024
        ),
    )(*(x.reshape(flat) for x in (query_field, key_field, value_field, output_grad)))
    outs = pl.pallas_call(
        copy_kernel,
        out_shape=[jax.ShapeDtypeStruct(flat, F32)] * 3,
        in_specs=[pl.BlockSpec(memory_space=pltpu.VMEM)] * 3,
        out_specs=[pl.BlockSpec(memory_space=pltpu.VMEM)] * 3,
    )(*outs)
    return tuple(x.reshape(frames, rows, cols, channels) for x in outs)


def solution(mesh):
    spec = P(None, "ha", "wa", None)
    return jax.shard_map(
        body, mesh=mesh, in_specs=(spec,) * 4, out_specs=(spec,) * 3, check_vma=False,
    )
```

```python
import jax
import jax.numpy as jnp
from jax import lax
from jax.experimental import pallas as pl
from jax.experimental.pallas import tpu as pltpu
from jax.sharding import PartitionSpec as P

MESH = pl.DeviceIdType.MESH
F32 = jnp.float32
BF16 = jnp.bfloat16
DIM = 128
SCALE = DIM ** -0.5
LOW = -1e30
CELLS = 128
KEYS = 3 * CELLS
HALF = 4 * CELLS


def halves(x):
    hi = x.astype(BF16)
    return hi, (x - hi.astype(F32)).astype(BF16)


def thirds(x):
    hi = x.astype(BF16)
    rest = x - hi.astype(F32)
    mid = rest.astype(BF16)
    return hi, mid, (rest - mid.astype(F32)).astype(BF16)


def dot(a, b, dims):
    return lax.dot_general(a, b, (dims, ((), ())), preferred_element_type=F32)


def kernel(
    q_in, k_in, v_in, g_in, dq_out, dk_out, dv_out,
    raw, kvb, qb, kp, lv, rq, ro, wbuf, dbuf, rel, st, sall, gst, dqt, dqs, dqr, own, halo, yret, zret,
    in_sem, near_sem, far_sem, y_sem, zq_sem, xq_sem, diag_sem, sibq_sem, rel_sem, stat_sem,
    yr_sem, zr_sem, dqs_sem, dq_sem,
):
    ha, wa = lax.axis_index("ha"), lax.axis_index("wa")
    row, xl = ha // 2, ha % 2
    core = wa % 2
    chip = wa // 2
    zp = chip % 2
    tile = chip // 2
    side = 2 * zp - 1
    up = 2 * xl - 1

    sib_id = (ha, wa + 1 - 2 * core)
    near_id = (ha, (wa + 2 * side + 32) % 32)
    far_to = (ha, (wa - 4 * side + 32) % 32)
    far_from = (ha, (wa + 4 * side + 32) % 32)
    zpair = (ha, wa - 2 * side)
    xpair = (ha - up, wa)
    diag = (ha - up, wa - 2 * side)
    y_to = ((ha + 2 * up + 8) % 8, wa)
    y_from = ((ha - 2 * up + 8) % 8, wa)

    side_in = jnp.where(zp == 0, tile > 0, tile < 7)
    far_out = jnp.where(zp == 0, tile < 7, tile > 0)
    y_out = jnp.where(xl == 1, row < 3, row > 0)
    y_in = jnp.where(xl == 1, row > 0, row < 3)
    z_first = (tile > 0) & (tile < 7)

    barrier = pltpu.get_barrier_semaphore()
    flip = 1 - 2 * core
    group = (diag, zpair, xpair, (ha - up, wa - 2 * side + flip), (ha, wa - 2 * side + flip), (ha - up, wa + flip), sib_id)
    partners = group + (near_id, far_to, far_from, y_to, y_from)
    for device in partners:
        pl.semaphore_signal(barrier, inc=1, device_id=device, device_id_type=MESH)

    to_relay = (chip == 6) | (chip == 9)
    relay = (chip == 14) | (chip == 1)
    from_relay = (chip == 8) | (chip == 7)
    turn = jnp.where((chip == 6) | (chip == 1), 1, -1)
    jump = jnp.where((chip == 1) | (chip == 8), 1, -1)
    cross_id = (ha, (wa + 16 * turn + 32) % 32)
    jump_id = (ha, (wa + 12 * jump + 32) % 32)

    @pl.when(to_relay | relay)
    def _():
        pl.semaphore_signal(barrier, inc=1, device_id=cross_id, device_id_type=MESH)

    @pl.when(relay | from_relay)
    def _():
        pl.semaphore_signal(barrier, inc=1, device_id=jump_id, device_id_type=MESH)

    loads = [
        pltpu.make_async_copy(ref, raw.at[i], in_sem.at[i]) for i, ref in enumerate((k_in, v_in, q_in, g_in))
    ]
    for load in loads:
        load.start()

    def arrange(h, arrays):
        for i in arrays:
            part = raw[i, :, :, h * DIM:(h + 1) * DIM].reshape(CELLS, DIM)
            if i < 2:
                kvb[h, 0, 0, i] = part
            else:
                qb[h, xl, zp, core, i - 2] = part

    for load in loads:
        load.wait()
    arrange(0, range(4))
    extra = jnp.where(relay, 2, jnp.where(to_relay | from_relay, 1, 0))
    pl.semaphore_wait(barrier, len(partners) + extra)

    def remote(src, dst, sems, index, device):
        return pltpu.make_async_remote_copy(
            src_ref=src, dst_ref=dst, send_sem=sems.at[(0,) + index], recv_sem=sems.at[(1,) + index],
            device_id=device, device_id_type=MESH,
        )

    def near_copy(h, kv):
        return remote(kvb.at[h, 0, 0, kv], kvb.at[h, 0, 1, kv], near_sem, (h, kv), near_id)

    def far_copy(h, kv):
        return remote(kvb.at[h, 0, 0, kv], kvb.at[h, 0, 2, kv], far_sem, (h, kv), far_to)

    def relay_copy(h, kv):
        return remote(kvb.at[h, 0, 0, kv], rel.at[h, kv], rel_sem, (h, kv), cross_id)

    def jump_copy(h, kv):
        return remote(rel.at[h, kv], kvb.at[h, 0, 2, kv], far_sem, (h, kv), jump_id)

    def y_copy(h, unit, kv):
        return remote(kvb.at[h, 0, unit, kv], kvb.at[h, 1, unit, kv], y_sem, (h, unit, kv), y_to)

    def q_copy(h, half, place, part, sems, device):
        block = qb.at[h, half, place, core, part]
        return remote(block, block, sems, (h, part), device)

    def zq_copy(h, part):
        return q_copy(h, xl, zp, part, zq_sem, zpair)

    def xq_copy(h, part):
        return q_copy(h, xl, zp, part, xq_sem, xpair)

    def diag_by_x(h, part):
        return q_copy(h, xl, 1 - zp, part, diag_sem, xpair)

    def diag_by_z(h, part):
        return q_copy(h, 1 - xl, zp, part, diag_sem, zpair)

    def slot_place(slot):
        return xl + (slot // 2) * (1 - 2 * xl), zp + (slot % 2) * (1 - 2 * zp)

    def sib_copy(h, slot):
        half, place = slot_place(slot)
        block = qb.at[h, half, place, core]
        return remote(block, block, sibq_sem, (h, slot), sib_id)

    def y_sends(h):
        @pl.when(y_out)
        def _():
            y_copy(h, 0, 0).start()
            y_copy(h, 0, 1).start()

    def x_sends(h):
        for part in (1, 0):
            xq_copy(h, part).start()
        sib_copy(h, 0).start()

    def z_sends(h):
        for part in range(2):
            @pl.when(side_in)
            def _():
                near_copy(h, part).start()

            @pl.when(to_relay)
            def _():
                relay_copy(h, part).start()

            @pl.when(far_out & jnp.logical_not(to_relay))
            def _():
                far_copy(h, part).start()

            zq_copy(h, part).start()

    def pass_keys(h, kv):
        @pl.when(relay)
        def _():
            relay_copy(h, kv).wait_recv()
            jump_copy(h, kv).start()

        @pl.when(side_in)
        def _():
            near_copy(h, kv).wait_recv()

            @pl.when(y_out)
            def _():
                y_copy(h, 1, kv).start()

            far_copy(h, kv).wait_recv()

            @pl.when(y_out)
            def _():
                y_copy(h, 2, kv).start()

    def pass_queries(h):
        xq_copy(h, 1).wait_recv()
        diag_by_z(h, 1).start()
        zq_copy(h, 0).wait_recv()

        @pl.when(z_first)
        def _():
            diag_by_x(h, 0).start()

        xq_copy(h, 0).wait_recv()
        sib_copy(h, 2).start()

        @pl.when(jnp.logical_not(z_first))
        def _():
            diag_by_z(h, 0).start()

    def last_pass(h):
        pass_keys(h, 1)
        zq_copy(h, 1).wait_recv()
        sib_copy(h, 1).start()

    def last_queries(h):
        for part in range(2):
            diag_by_x(h, part).wait_recv()
        sib_copy(h, 3).start()

    def prepare_queries(h, low):
        def one(slot, c):
            sib_copy(h, slot).wait_recv()
            half, place = slot_place(slot)
            for blk in range(2):
                q1, q2, q3 = thirds(qb[h, half, place, blk, 0] * SCALE)
                o1, o2 = halves(qb[h, half, place, blk, 1])
                rows = pl.ds(pl.multiple_of(place * (2 * CELLS) + blk * CELLS, CELLS), CELLS)
                for i, part in enumerate((q1, q1, q2, q2, q3, q1)):
                    rq[h, half, rows, i * DIM:(i + 1) * DIM] = part
                for i, part in enumerate((o1, o1, o2, o2)):
                    ro[h, half, rows, i * DIM:(i + 1) * DIM] = part
            return c

        lax.fori_loop(low, low + 2, one, 0)

    def prepare_keys(h, line):
        for unit in range(3):
            rows = slice(unit * CELLS, (unit + 1) * CELLS)
            k1, k2, k3 = thirds(kvb[h, line, unit, 0])
            v1, v2 = halves(kvb[h, line, unit, 1])
            for i, part in enumerate((k1, k2, k1, k2, k1, k3)):
                kp[2 * h + line, rows, i * DIM:(i + 1) * DIM] = part
            for i, part in enumerate((v1, v2, v1, v2)):
                lv[rows, i * DIM:(i + 1) * DIM] = part

    far_keys = lax.broadcasted_iota(jnp.int32, (KEYS, 1), 0) >= CELLS
    bias = jnp.where(far_keys, jnp.where(side_in, 0.0, LOW), 0.0)

    def forward_block(h, k, line, half):
        index = 3 * h + k
        scores = dot(kp[2 * h + line], rq[h, half], ((1,), (1,))) + bias
        dprobs = dot(lv[...], ro[h, half], ((1,), (1,)))
        peak = jnp.max(scores, axis=0, keepdims=True)
        weights = jnp.exp(scores - peak)
        wbuf[index] = weights
        dbuf[index] = dprobs
        st[index, 0:1] = peak
        st[index, 1:2] = jnp.sum(weights, axis=0, keepdims=True)
        st[index, 2:3] = jnp.sum(weights * dprobs, axis=0, keepdims=True)

    def forward(h, before):
        def one(step, c):
            for i in range(3):
                @pl.when(step == i)
                def _():
                    before[i]()

            half = jnp.where(step == 0, xl, 1 - xl)
            line = step // 2
            here = (step < 2) | y_in

            @pl.when(here & (step != 1))
            def _():
                @pl.when(step == 2)
                def _():
                    for kv in range(2):
                        y_copy(h, 0, kv).wait_recv()

                        @pl.when(side_in)
                        def _():
                            y_copy(h, 1, kv).wait_recv()
                            y_copy(h, 2, kv).wait_recv()

                prepare_keys(h, line)

            @pl.when(here)
            def _():
                forward_block(h, step, line, half)

            @pl.when(jnp.logical_not(here))
            def _():
                st[3 * h + 2, 0:1] = jnp.full((1, HALF), LOW, F32)
                st[3 * h + 2, 1:3] = jnp.zeros((2, HALF), F32)

            return c

        lax.fori_loop(0, 3, one, 0)

    me = 4 * xl + 2 * zp + core

    def merge(triples):
        peak = triples[0][0]
        for p, _, _ in triples[1:]:
            peak = jnp.maximum(peak, p)
        total = jnp.zeros_like(peak)
        center = jnp.zeros_like(peak)
        for p, s, c in triples:
            factor = jnp.exp(p - peak)
            total += s * factor
            center += c * factor
        return peak, total, center

    def triple(ref, base):
        return tuple(ref[base + i:base + i + 1] for i in range(3))

    def stat_copy(h, which):
        place = sall.at[h, me]
        return remote(place, place, stat_sem, (h, which), group[which])

    def start_stats(h):
        merged = (triple(st.at[3 * h], 0), merge([triple(st.at[3 * h + 1], 0), triple(st.at[3 * h + 2], 0)]))
        for half in range(2):
            for i in range(3):
                value = jnp.where(half == xl, merged[0][i], merged[1][i])
                sall[h, me, 3 * half + i:3 * half + i + 1] = value
        sall[h, me, 6:8] = jnp.zeros((2, HALF), F32)
        for which in range(7):
            stat_copy(h, which).start()

    def end_stats(h):
        for which in range(7):
            stat_copy(h, which).wait_recv()
        for half in range(2):
            peak, total, center = merge([triple(sall.at[h, i], 3 * half) for i in range(8)])
            inverse = 1.0 / total
            gst[h, half, 0:1] = peak
            gst[h, half, 1:2] = inverse
            gst[h, half, 2:3] = center * inverse

    def backward_block(h, k, line, half, give):
        index = 3 * h + k
        alpha = jnp.exp(st[index, 0:1] - gst[h, half, 0:1]) * gst[h, half, 1:2]
        probs = wbuf[index] * alpha
        dscores = probs * (dbuf[index] - gst[h, half, 2:3])
        p1, p2 = halves(probs)
        s1, s2 = halves(dscores)
        o12 = ro[h, half, :, DIM:3 * DIM]
        q12 = rq[h, half, :, DIM:3 * DIM]
        k12 = kp[2 * h + line, :, 0:2 * DIM].T
        dv = dot(p1, o12, ((1,), (0,))) + dot(p2, o12, ((1,), (0,)))
        dk = dot(s1, q12, ((1,), (0,))) + dot(s2, q12, ((1,), (0,)))
        dq = dot(jnp.concatenate([k12, k12], axis=1), jnp.concatenate([s1, s2], axis=0), ((1,), (0,)))
        dq = dq[:DIM] + dq[DIM:]
        for place in range(2):
            for blk in range(2):
                at = (2 * place + blk) * CELLS
                dqt[h, half, place, blk] += dq[:, at:at + CELLS]
        give(1, dv[:, :DIM] + dv[:, DIM:])
        give(0, dk[:, :DIM] + dk[:, DIM:])

    def yr_copy(h, unit, kind):
        return remote(halo.at[h, unit, kind], yret.at[h, unit, kind], yr_sem, (h, unit, kind), y_from)

    def dqs_copy(h):
        return remote(dqt.at[h, :, :, 1 - core], dqs.at[h], dqs_sem, (h,), sib_id)

    def backward(h):
        dqt[h] = jnp.zeros(dqt.shape[1:], F32)
        own[h] = jnp.zeros(own.shape[1:], F32)

        def one(turn, c):
            step = 2 - turn

            @pl.when((step < 2) | y_in)
            def _():
                half = jnp.where(step == 0, xl, 1 - xl)

                def give(kind, value):
                    @pl.when(step == 2)
                    def _():
                        for unit in range(3):
                            halo[h, unit, kind] = value[unit * CELLS:(unit + 1) * CELLS]

                        @pl.when(side_in)
                        def _():
                            yr_copy(h, 2, kind).start()
                            yr_copy(h, 1, kind).start()

                        if kind == 0:
                            yr_copy(h, 0, 0).start()
                            yr_copy(h, 0, 1).start()

                    @pl.when(step < 2)
                    def _():
                        for unit in range(3):
                            own[h, unit, kind] += value[unit * CELLS:(unit + 1) * CELLS]

                backward_block(h, step, step // 2, half, give)

            return c

        lax.fori_loop(0, 3, one, 0)
        dqs_copy(h).start()

    def dq_copy(h, which):
        device = (xpair, zpair, diag)[which]
        half, place = ((1 - xl, zp), (xl, 1 - zp), (1 - xl, 1 - zp))[which]
        return remote(dqt.at[h, half, place, core], dqr.at[h, which], dq_sem, (h, which), device)

    def share_dq(h):
        dqs_copy(h).wait_recv()
        for half in range(2):
            for place in range(2):
                dqt[h, half, place, core] += dqs[h, half, place]
        for which in range(3):
            dq_copy(h, which).start()

    def zr_copy(h, which, kind):
        device = (near_id, far_from)[which]
        return remote(own.at[h, 1 + which, kind], zret.at[h, which, kind], zr_sem, (h, which, kind), device)

    def pass_back(h):
        for kind in (1, 0):
            for which in (1, 0):
                @pl.when(side_in)
                def _():
                    @pl.when(y_out)
                    def _():
                        yr_copy(h, 1 + which, kind).wait_recv()
                        own[h, 1 + which, kind] += yret[h, 1 + which, kind]

                    zr_copy(h, which, kind).start()

    def finish(h):
        lanes = slice(h * DIM, (h + 1) * DIM)
        for which in range(3):
            dq_copy(h, which).wait_recv()
        dq = dqt[h, xl, zp, core] + dqr[h, 0] + dqr[h, 1] + dqr[h, 2]
        dq_out[:, :, lanes] = (dq.T * SCALE).reshape(32, 4, DIM)

        @pl.when(y_out)
        def _():
            yr_copy(h, 0, 0).wait_recv()
            yr_copy(h, 0, 1).wait_recv()
            own[h, 0] += yret[h, 0]

        @pl.when(far_out)
        def _():
            zr_copy(h, 1, 0).wait_recv()
            zr_copy(h, 1, 1).wait_recv()
            own[h, 0] += zret[h, 1]

        @pl.when(side_in)
        def _():
            zr_copy(h, 0, 0).wait_recv()
            zr_copy(h, 0, 1).wait_recv()
            own[h, 0] += zret[h, 0]

        dk_out[:, :, lanes] = own[h, 0, 0].reshape(32, 4, DIM)
        dv_out[:, :, lanes] = own[h, 0, 1].reshape(32, 4, DIM)

    def all_left(h):
        for part in range(2):
            @pl.when(y_out)
            def _():
                y_copy(h, 0, part).wait_send()

                @pl.when(side_in)
                def _():
                    y_copy(h, 1, part).wait_send()
                    y_copy(h, 2, part).wait_send()

            @pl.when(side_in)
            def _():
                near_copy(h, part).wait_send()
                zr_copy(h, 0, part).wait_send()
                zr_copy(h, 1, part).wait_send()

            @pl.when(to_relay)
            def _():
                relay_copy(h, part).wait_send()

            @pl.when((far_out & jnp.logical_not(to_relay)) | relay)
            def _():
                far_copy(h, part).wait_send()

            zq_copy(h, part).wait_send()
            xq_copy(h, part).wait_send()
            diag_by_x(h, part).wait_send()

        @pl.when(y_in)
        def _():
            for kind in range(2):
                yr_copy(h, 0, kind).wait_send()

                @pl.when(side_in)
                def _():
                    yr_copy(h, 1, kind).wait_send()
                    yr_copy(h, 2, kind).wait_send()

        for slot in range(4):
            sib_copy(h, slot).wait_send()
        dqs_copy(h).wait_send()
        for which in range(3):
            dq_copy(h, which).wait_send()
        for which in range(7):
            stat_copy(h, which).wait_send()

    y_sends(0)
    z_sends(0)
    x_sends(0)
    arrange(1, range(4))

    @pl.when(jnp.logical_not(side_in))
    def _():
        for h in range(2):
            for line in range(2):
                kvb[h, line, 1:3] = jnp.zeros((2, 2, CELLS, DIM), F32)

    def head0_start():
        pass_keys(0, 0)
        pass_queries(0)
        z_sends(1)
        x_sends(1)
        last_pass(0)
        y_sends(1)
        prepare_queries(0, 0)

    def head0_other():
        last_queries(0)
        prepare_queries(0, 2)

    def head0_halo():
        pass_keys(1, 0)

    def head1_start():
        prepare_queries(1, 0)

    def head1_other():
        end_stats(0)
        backward(0)
        last_queries(1)
        prepare_queries(1, 2)

    def head1_halo():
        share_dq(0)

    forward(0, (head0_start, head0_other, head0_halo))
    start_stats(0)
    pass_queries(1)
    last_pass(1)
    forward(1, (head1_start, head1_other, head1_halo))
    start_stats(1)
    pass_back(0)
    end_stats(1)
    backward(1)
    share_dq(1)
    finish(0)
    pass_back(1)
    finish(1)
    all_left(0)
    all_left(1)


def copy_kernel(*refs):
    for i in range(3):
        refs[3 + i][...] = refs[i][...]


def body(query_field, key_field, value_field, output_grad):
    frames, rows, cols, channels = query_field.shape
    flat = (frames * rows, cols, channels)

    def sems(*shape):
        return pltpu.SemaphoreType.DMA((2, 2) + shape)

    outs = pl.pallas_call(
        kernel,
        out_shape=[jax.ShapeDtypeStruct(flat, F32)] * 3,
        in_specs=[pl.BlockSpec(memory_space=pl.ANY)] * 4,
        out_specs=[pl.BlockSpec(memory_space=pltpu.VMEM)] * 3,
        scratch_shapes=[
            pltpu.VMEM((4,) + flat, F32),
            pltpu.VMEM((2, 2, 3, 2, CELLS, DIM), F32),
            pltpu.VMEM((2, 2, 2, 2, 2, CELLS, DIM), F32),
            pltpu.VMEM((4, KEYS, 6 * DIM), BF16),
            pltpu.VMEM((KEYS, 4 * DIM), BF16),
            pltpu.VMEM((2, 2, HALF, 6 * DIM), BF16),
            pltpu.VMEM((2, 2, HALF, 4 * DIM), BF16),
            pltpu.VMEM((6, KEYS, HALF), F32),
            pltpu.VMEM((6, KEYS, HALF), F32),
            pltpu.VMEM((2, 2, CELLS, DIM), F32),
            pltpu.VMEM((6, 8, HALF), F32),
            pltpu.VMEM((2, 8, 8, HALF), F32),
            pltpu.VMEM((2, 2, 8, HALF), F32),
            pltpu.VMEM((2, 2, 2, 2, DIM, CELLS), F32),
            pltpu.VMEM((2, 2, 2, DIM, CELLS), F32),
            pltpu.VMEM((2, 3, DIM, CELLS), F32),
            pltpu.VMEM((2, 3, 2, CELLS, DIM), F32),
            pltpu.VMEM((2, 3, 2, CELLS, DIM), F32),
            pltpu.VMEM((2, 3, 2, CELLS, DIM), F32),
            pltpu.VMEM((2, 2, 2, CELLS, DIM), F32),
            pltpu.SemaphoreType.DMA((4,)),
            sems(2), sems(2), sems(3, 2), sems(2), sems(2), sems(2), sems(4), sems(2), sems(7),
            sems(3, 2), sems(2, 2), sems(), sems(3),
        ],
        compiler_params=pltpu.CompilerParams(
            collective_id=0, has_side_effects=True, vmem_limit_bytes=56 * 1024 * 1024
        ),
    )(*(x.reshape(flat) for x in (query_field, key_field, value_field, output_grad)))
    outs = pl.pallas_call(
        copy_kernel,
        out_shape=[jax.ShapeDtypeStruct(flat, F32)] * 3,
        in_specs=[pl.BlockSpec(memory_space=pltpu.VMEM)] * 3,
        out_specs=[pl.BlockSpec(memory_space=pltpu.VMEM)] * 3,
    )(*outs)
    return tuple(x.reshape(frames, rows, cols, channels) for x in outs)


def solution(mesh):
    spec = P(None, "ha", "wa", None)
    return jax.shard_map(
        body, mesh=mesh, in_specs=(spec,) * 4, out_specs=(spec,) * 3, check_vma=False,
    )
```

```python
import jax
import jax.numpy as jnp
from jax import lax
from jax.experimental import pallas as pl
from jax.experimental.pallas import tpu as pltpu
from jax.sharding import PartitionSpec as P

MESH = pl.DeviceIdType.MESH
F32 = jnp.float32
BF16 = jnp.bfloat16
DIM = 128
SCALE = DIM ** -0.5
LOW = -1e30
CELLS = 128
KEYS = 3 * CELLS
HALF = 4 * CELLS


def halves(x):
    hi = x.astype(BF16)
    return hi, (x - hi.astype(F32)).astype(BF16)


def thirds(x):
    hi = x.astype(BF16)
    rest = x - hi.astype(F32)
    mid = rest.astype(BF16)
    return hi, mid, (rest - mid.astype(F32)).astype(BF16)


def dot(a, b, dims):
    return lax.dot_general(a, b, (dims, ((), ())), preferred_element_type=F32)


def kernel(
    q_in, k_in, v_in, g_in, dq_out, dk_out, dv_out,
    raw, kvb, qb, kp, lv, rq, ro, wbuf, dbuf, rel, st, sall, gst, dqt, dqs, dqr, own, halo, yret, zret,
    in_sem, near_sem, far_sem, y_sem, zq_sem, xq_sem, diag_sem, sibq_sem, rel_sem, stat_sem,
    yr_sem, zr_sem, dqs_sem, dq_sem,
):
    ha, wa = lax.axis_index("ha"), lax.axis_index("wa")
    row, xl = ha // 2, ha % 2
    core = wa % 2
    chip = wa // 2
    zp = chip % 2
    tile = chip // 2
    side = 2 * zp - 1
    up = 2 * xl - 1

    sib_id = (ha, wa + 1 - 2 * core)
    near_id = (ha, (wa + 2 * side + 32) % 32)
    far_to = (ha, (wa - 4 * side + 32) % 32)
    far_from = (ha, (wa + 4 * side + 32) % 32)
    zpair = (ha, wa - 2 * side)
    xpair = (ha - up, wa)
    diag = (ha - up, wa - 2 * side)
    y_to = ((ha + 2 * up + 8) % 8, wa)
    y_from = ((ha - 2 * up + 8) % 8, wa)

    side_in = jnp.where(zp == 0, tile > 0, tile < 7)
    far_out = jnp.where(zp == 0, tile < 7, tile > 0)
    y_out = jnp.where(xl == 1, row < 3, row > 0)
    y_in = jnp.where(xl == 1, row > 0, row < 3)

    barrier = pltpu.get_barrier_semaphore()
    flip = 1 - 2 * core
    group = (diag, zpair, xpair, (ha - up, wa - 2 * side + flip), (ha, wa - 2 * side + flip), (ha - up, wa + flip), sib_id)
    partners = group + (near_id, far_to, far_from, y_to, y_from)
    for device in partners:
        pl.semaphore_signal(barrier, inc=1, device_id=device, device_id_type=MESH)

    to_relay = (chip == 6) | (chip == 9)
    relay = (chip == 14) | (chip == 1)
    from_relay = (chip == 8) | (chip == 7)
    turn = jnp.where((chip == 6) | (chip == 1), 1, -1)
    jump = jnp.where((chip == 1) | (chip == 8), 1, -1)
    cross_id = (ha, (wa + 16 * turn + 32) % 32)
    jump_id = (ha, (wa + 12 * jump + 32) % 32)

    @pl.when(to_relay | relay)
    def _():
        pl.semaphore_signal(barrier, inc=1, device_id=cross_id, device_id_type=MESH)

    @pl.when(relay | from_relay)
    def _():
        pl.semaphore_signal(barrier, inc=1, device_id=jump_id, device_id_type=MESH)

    loads = [
        pltpu.make_async_copy(ref, raw.at[i], in_sem.at[i]) for i, ref in enumerate((k_in, v_in, q_in, g_in))
    ]
    for load in loads:
        load.start()

    def arrange(h, arrays):
        for i in arrays:
            part = raw[i, :, :, h * DIM:(h + 1) * DIM].reshape(CELLS, DIM)
            if i < 2:
                kvb[h, 0, 0, i] = part
            else:
                qb[h, xl, zp, core, i - 2] = part

    for load in loads:
        load.wait()
    arrange(0, range(4))
    extra = jnp.where(relay, 2, jnp.where(to_relay | from_relay, 1, 0))
    pl.semaphore_wait(barrier, len(partners) + extra)

    def remote(src, dst, sems, index, device):
        return pltpu.make_async_remote_copy(
            src_ref=src, dst_ref=dst, send_sem=sems.at[(0,) + index], recv_sem=sems.at[(1,) + index],
            device_id=device, device_id_type=MESH,
        )

    def near_copy(h, kv):
        return remote(kvb.at[h, 0, 0, kv], kvb.at[h, 0, 1, kv], near_sem, (h, kv), near_id)

    def far_copy(h, kv):
        return remote(kvb.at[h, 0, 0, kv], kvb.at[h, 0, 2, kv], far_sem, (h, kv), far_to)

    def relay_copy(h, kv):
        return remote(kvb.at[h, 0, 0, kv], rel.at[h, kv], rel_sem, (h, kv), cross_id)

    def jump_copy(h, kv):
        return remote(rel.at[h, kv], kvb.at[h, 0, 2, kv], far_sem, (h, kv), jump_id)

    def y_copy(h, unit, kv):
        return remote(kvb.at[h, 0, unit, kv], kvb.at[h, 1, unit, kv], y_sem, (h, unit, kv), y_to)

    def q_copy(h, half, place, part, sems, device):
        block = qb.at[h, half, place, core, part]
        return remote(block, block, sems, (h, part), device)

    def zq_copy(h, part):
        return q_copy(h, xl, zp, part, zq_sem, zpair)

    def xq_copy(h, part):
        return q_copy(h, xl, zp, part, xq_sem, xpair)

    def diag_by_z(h, part):
        return q_copy(h, 1 - xl, zp, part, diag_sem, zpair)

    def slot_place(slot):
        return xl + (slot // 2) * (1 - 2 * xl), zp + (slot % 2) * (1 - 2 * zp)

    def sib_copy(h, slot):
        half, place = slot_place(slot)
        block = qb.at[h, half, place, core]
        return remote(block, block, sibq_sem, (h, slot), sib_id)

    def y_sends(h):
        @pl.when(y_out)
        def _():
            y_copy(h, 0, 0).start()
            y_copy(h, 0, 1).start()

    def x_sends(h):
        for part in (1, 0):
            xq_copy(h, part).start()
        sib_copy(h, 0).start()

    def z_sends(h):
        for part in range(2):
            @pl.when(side_in)
            def _():
                near_copy(h, part).start()

            @pl.when(to_relay)
            def _():
                relay_copy(h, part).start()

            @pl.when(far_out & jnp.logical_not(to_relay))
            def _():
                far_copy(h, part).start()

            zq_copy(h, part).start()

    def pass_keys(h, kv):
        @pl.when(relay)
        def _():
            relay_copy(h, kv).wait_recv()
            jump_copy(h, kv).start()

        @pl.when(side_in)
        def _():
            near_copy(h, kv).wait_recv()

            @pl.when(y_out)
            def _():
                y_copy(h, 1, kv).start()

            far_copy(h, kv).wait_recv()

            @pl.when(y_out)
            def _():
                y_copy(h, 2, kv).start()

    def pass_queries(h):
        xq_copy(h, 1).wait_recv()
        diag_by_z(h, 1).start()
        zq_copy(h, 0).wait_recv()
        xq_copy(h, 0).wait_recv()
        sib_copy(h, 2).start()
        diag_by_z(h, 0).start()

    def last_pass(h):
        pass_keys(h, 1)
        zq_copy(h, 1).wait_recv()
        sib_copy(h, 1).start()

    def last_queries(h):
        for part in range(2):
            diag_by_z(h, part).wait_recv()
        sib_copy(h, 3).start()

    def prepare_queries(h, low):
        def one(slot, c):
            sib_copy(h, slot).wait_recv()
            half, place = slot_place(slot)
            for blk in range(2):
                q1, q2, q3 = thirds(qb[h, half, place, blk, 0] * SCALE)
                o1, o2 = halves(qb[h, half, place, blk, 1])
                rows = pl.ds(pl.multiple_of(place * (2 * CELLS) + blk * CELLS, CELLS), CELLS)
                for i, part in enumerate((q1, q1, q2, q2, q3, q1)):
                    rq[h, half, rows, i * DIM:(i + 1) * DIM] = part
                for i, part in enumerate((o1, o1, o2, o2)):
                    ro[h, half, rows, i * DIM:(i + 1) * DIM] = part
            return c

        lax.fori_loop(low, low + 2, one, 0)

    def prepare_keys(h, line):
        for unit in range(3):
            rows = slice(unit * CELLS, (unit + 1) * CELLS)
            k1, k2, k3 = thirds(kvb[h, line, unit, 0])
            v1, v2 = halves(kvb[h, line, unit, 1])
            for i, part in enumerate((k1, k2, k1, k2, k1, k3)):
                kp[2 * h + line, rows, i * DIM:(i + 1) * DIM] = part
            for i, part in enumerate((v1, v2, v1, v2)):
                lv[rows, i * DIM:(i + 1) * DIM] = part

    far_keys = lax.broadcasted_iota(jnp.int32, (KEYS, 1), 0) >= CELLS
    bias = jnp.where(far_keys, jnp.where(side_in, 0.0, LOW), 0.0)

    def forward_block(h, k, line, half):
        index = 3 * h + k
        scores = dot(kp[2 * h + line], rq[h, half], ((1,), (1,))) + bias
        dprobs = dot(lv[...], ro[h, half], ((1,), (1,)))
        peak = jnp.max(scores, axis=0, keepdims=True)
        weights = jnp.exp(scores - peak)
        wbuf[index] = weights
        dbuf[index] = dprobs
        st[index, 0:1] = peak
        st[index, 1:2] = jnp.sum(weights, axis=0, keepdims=True)
        st[index, 2:3] = jnp.sum(weights * dprobs, axis=0, keepdims=True)

    def forward(h, before):
        def one(step, c):
            for i in range(3):
                @pl.when(step == i)
                def _():
                    before[i]()

            half = jnp.where(step == 0, xl, 1 - xl)
            line = step // 2
            here = (step < 2) | y_in

            @pl.when(here & (step != 1))
            def _():
                @pl.when(step == 2)
                def _():
                    for kv in range(2):
                        y_copy(h, 0, kv).wait_recv()

                        @pl.when(side_in)
                        def _():
                            y_copy(h, 1, kv).wait_recv()
                            y_copy(h, 2, kv).wait_recv()

                prepare_keys(h, line)

            @pl.when(here)
            def _():
                forward_block(h, step, line, half)

            @pl.when(jnp.logical_not(here))
            def _():
                st[3 * h + 2, 0:1] = jnp.full((1, HALF), LOW, F32)
                st[3 * h + 2, 1:3] = jnp.zeros((2, HALF), F32)

            return c

        lax.fori_loop(0, 3, one, 0)

    me = 4 * xl + 2 * zp + core

    def merge(triples):
        peak = triples[0][0]
        for p, _, _ in triples[1:]:
            peak = jnp.maximum(peak, p)
        total = jnp.zeros_like(peak)
        center = jnp.zeros_like(peak)
        for p, s, c in triples:
            factor = jnp.exp(p - peak)
            total += s * factor
            center += c * factor
        return peak, total, center

    def triple(ref, base):
        return tuple(ref[base + i:base + i + 1] for i in range(3))

    def stat_copy(h, which):
        place = sall.at[h, me]
        return remote(place, place, stat_sem, (h, which), group[which])

    def start_stats(h):
        merged = (triple(st.at[3 * h], 0), merge([triple(st.at[3 * h + 1], 0), triple(st.at[3 * h + 2], 0)]))
        for half in range(2):
            for i in range(3):
                value = jnp.where(half == xl, merged[0][i], merged[1][i])
                sall[h, me, 3 * half + i:3 * half + i + 1] = value
        sall[h, me, 6:8] = jnp.zeros((2, HALF), F32)
        for which in range(7):
            stat_copy(h, which).start()

    def end_stats(h):
        for which in range(7):
            stat_copy(h, which).wait_recv()
        for half in range(2):
            peak, total, center = merge([triple(sall.at[h, i], 3 * half) for i in range(8)])
            inverse = 1.0 / total
            gst[h, half, 0:1] = peak
            gst[h, half, 1:2] = inverse
            gst[h, half, 2:3] = center * inverse

    def backward_block(h, k, line, half, give):
        index = 3 * h + k
        alpha = jnp.exp(st[index, 0:1] - gst[h, half, 0:1]) * gst[h, half, 1:2]
        probs = wbuf[index] * alpha
        dscores = probs * (dbuf[index] - gst[h, half, 2:3])
        p1, p2 = halves(probs)
        s1, s2 = halves(dscores)
        o12 = ro[h, half, :, DIM:3 * DIM]
        q12 = rq[h, half, :, DIM:3 * DIM]
        k12 = kp[2 * h + line, :, 0:2 * DIM].T
        dv = dot(p1, o12, ((1,), (0,))) + dot(p2, o12, ((1,), (0,)))
        dk = dot(s1, q12, ((1,), (0,))) + dot(s2, q12, ((1,), (0,)))
        dq = dot(jnp.concatenate([k12, k12], axis=1), jnp.concatenate([s1, s2], axis=0), ((1,), (0,)))
        dq = dq[:DIM] + dq[DIM:]
        for place in range(2):
            for blk in range(2):
                at = (2 * place + blk) * CELLS
                dqt[h, half, place, blk] += dq[:, at:at + CELLS]
        give(1, dv[:, :DIM] + dv[:, DIM:])
        give(0, dk[:, :DIM] + dk[:, DIM:])

    def yr_copy(h, unit, kind):
        return remote(halo.at[h, unit, kind], yret.at[h, unit, kind], yr_sem, (h, unit, kind), y_from)

    def dqs_copy(h):
        return remote(dqt.at[h, :, :, 1 - core], dqs.at[h], dqs_sem, (h,), sib_id)

    def backward(h):
        dqt[h] = jnp.zeros(dqt.shape[1:], F32)
        own[h] = jnp.zeros(own.shape[1:], F32)

        def one(turn, c):
            step = 2 - turn

            @pl.when((step < 2) | y_in)
            def _():
                half = jnp.where(step == 0, xl, 1 - xl)

                def give(kind, value):
                    @pl.when(step == 2)
                    def _():
                        for unit in range(3):
                            halo[h, unit, kind] = value[unit * CELLS:(unit + 1) * CELLS]

                        @pl.when(side_in)
                        def _():
                            yr_copy(h, 2, kind).start()
                            yr_copy(h, 1, kind).start()

                        if kind == 0:
                            yr_copy(h, 0, 0).start()
                            yr_copy(h, 0, 1).start()

                    @pl.when(step < 2)
                    def _():
                        for unit in range(3):
                            own[h, unit, kind] += value[unit * CELLS:(unit + 1) * CELLS]

                backward_block(h, step, step // 2, half, give)

            return c

        lax.fori_loop(0, 3, one, 0)
        dqs_copy(h).start()

    def dq_copy(h, which):
        device = (xpair, zpair, diag)[which]
        half, place = ((1 - xl, zp), (xl, 1 - zp), (1 - xl, 1 - zp))[which]
        return remote(dqt.at[h, half, place, core], dqr.at[h, which], dq_sem, (h, which), device)

    def share_dq(h):
        dqs_copy(h).wait_recv()
        for half in range(2):
            for place in range(2):
                dqt[h, half, place, core] += dqs[h, half, place]
        for which in range(3):
            dq_copy(h, which).start()

    def zr_copy(h, which, kind):
        device = (near_id, far_from)[which]
        return remote(own.at[h, 1 + which, kind], zret.at[h, which, kind], zr_sem, (h, which, kind), device)

    def pass_back(h):
        for kind in (1, 0):
            for which in (1, 0):
                @pl.when(side_in)
                def _():
                    @pl.when(y_out)
                    def _():
                        yr_copy(h, 1 + which, kind).wait_recv()
                        own[h, 1 + which, kind] += yret[h, 1 + which, kind]

                    zr_copy(h, which, kind).start()

    def finish(h):
        lanes = slice(h * DIM, (h + 1) * DIM)
        for which in range(3):
            dq_copy(h, which).wait_recv()
        dq = dqt[h, xl, zp, core] + dqr[h, 0] + dqr[h, 1] + dqr[h, 2]
        dq_out[:, :, lanes] = (dq.T * SCALE).reshape(32, 4, DIM)

        @pl.when(y_out)
        def _():
            yr_copy(h, 0, 0).wait_recv()
            yr_copy(h, 0, 1).wait_recv()
            own[h, 0] += yret[h, 0]

        @pl.when(far_out)
        def _():
            zr_copy(h, 1, 0).wait_recv()
            zr_copy(h, 1, 1).wait_recv()
            own[h, 0] += zret[h, 1]

        @pl.when(side_in)
        def _():
            zr_copy(h, 0, 0).wait_recv()
            zr_copy(h, 0, 1).wait_recv()
            own[h, 0] += zret[h, 0]

        dk_out[:, :, lanes] = own[h, 0, 0].reshape(32, 4, DIM)
        dv_out[:, :, lanes] = own[h, 0, 1].reshape(32, 4, DIM)

    def all_left(h):
        for part in range(2):
            @pl.when(y_out)
            def _():
                y_copy(h, 0, part).wait_send()

                @pl.when(side_in)
                def _():
                    y_copy(h, 1, part).wait_send()
                    y_copy(h, 2, part).wait_send()

            @pl.when(side_in)
            def _():
                near_copy(h, part).wait_send()
                zr_copy(h, 0, part).wait_send()
                zr_copy(h, 1, part).wait_send()

            @pl.when(to_relay)
            def _():
                relay_copy(h, part).wait_send()

            @pl.when((far_out & jnp.logical_not(to_relay)) | relay)
            def _():
                far_copy(h, part).wait_send()

            zq_copy(h, part).wait_send()
            xq_copy(h, part).wait_send()
            diag_by_z(h, part).wait_send()

        @pl.when(y_in)
        def _():
            for kind in range(2):
                yr_copy(h, 0, kind).wait_send()

                @pl.when(side_in)
                def _():
                    yr_copy(h, 1, kind).wait_send()
                    yr_copy(h, 2, kind).wait_send()

        for slot in range(4):
            sib_copy(h, slot).wait_send()
        dqs_copy(h).wait_send()
        for which in range(3):
            dq_copy(h, which).wait_send()
        for which in range(7):
            stat_copy(h, which).wait_send()

    y_sends(0)
    z_sends(0)
    x_sends(0)
    arrange(1, range(4))

    @pl.when(jnp.logical_not(side_in))
    def _():
        for h in range(2):
            for line in range(2):
                kvb[h, line, 1:3] = jnp.zeros((2, 2, CELLS, DIM), F32)

    def head0_start():
        pass_keys(0, 0)
        pass_queries(0)
        last_pass(0)
        z_sends(1)
        prepare_queries(0, 0)

    def head0_other():
        y_sends(1)
        x_sends(1)
        last_queries(0)
        prepare_queries(0, 2)

    def head0_halo():
        pass_keys(1, 0)

    def head1_start():
        prepare_queries(1, 0)

    def head1_other():
        end_stats(0)
        backward(0)
        last_queries(1)
        share_dq(0)
        prepare_queries(1, 2)

    def head1_halo():
        pass

    forward(0, (head0_start, head0_other, head0_halo))
    start_stats(0)
    pass_queries(1)
    last_pass(1)
    forward(1, (head1_start, head1_other, head1_halo))
    start_stats(1)
    pass_back(0)
    end_stats(1)
    backward(1)
    share_dq(1)
    finish(0)
    pass_back(1)
    finish(1)
    all_left(0)
    all_left(1)


def copy_kernel(*refs):
    for i in range(3):
        refs[3 + i][...] = refs[i][...]


def body(query_field, key_field, value_field, output_grad):
    frames, rows, cols, channels = query_field.shape
    flat = (frames * rows, cols, channels)

    def sems(*shape):
        return pltpu.SemaphoreType.DMA((2, 2) + shape)

    outs = pl.pallas_call(
        kernel,
        out_shape=[jax.ShapeDtypeStruct(flat, F32)] * 3,
        in_specs=[pl.BlockSpec(memory_space=pl.ANY)] * 4,
        out_specs=[pl.BlockSpec(memory_space=pltpu.VMEM)] * 3,
        scratch_shapes=[
            pltpu.VMEM((4,) + flat, F32),
            pltpu.VMEM((2, 2, 3, 2, CELLS, DIM), F32),
            pltpu.VMEM((2, 2, 2, 2, 2, CELLS, DIM), F32),
            pltpu.VMEM((4, KEYS, 6 * DIM), BF16),
            pltpu.VMEM((KEYS, 4 * DIM), BF16),
            pltpu.VMEM((2, 2, HALF, 6 * DIM), BF16),
            pltpu.VMEM((2, 2, HALF, 4 * DIM), BF16),
            pltpu.VMEM((6, KEYS, HALF), F32),
            pltpu.VMEM((6, KEYS, HALF), F32),
            pltpu.VMEM((2, 2, CELLS, DIM), F32),
            pltpu.VMEM((6, 8, HALF), F32),
            pltpu.VMEM((2, 8, 8, HALF), F32),
            pltpu.VMEM((2, 2, 8, HALF), F32),
            pltpu.VMEM((2, 2, 2, 2, DIM, CELLS), F32),
            pltpu.VMEM((2, 2, 2, DIM, CELLS), F32),
            pltpu.VMEM((2, 3, DIM, CELLS), F32),
            pltpu.VMEM((2, 3, 2, CELLS, DIM), F32),
            pltpu.VMEM((2, 3, 2, CELLS, DIM), F32),
            pltpu.VMEM((2, 3, 2, CELLS, DIM), F32),
            pltpu.VMEM((2, 2, 2, CELLS, DIM), F32),
            pltpu.SemaphoreType.DMA((4,)),
            sems(2), sems(2), sems(3, 2), sems(2), sems(2), sems(2), sems(4), sems(2), sems(7),
            sems(3, 2), sems(2, 2), sems(), sems(3),
        ],
        compiler_params=pltpu.CompilerParams(
            collective_id=0, has_side_effects=True, vmem_limit_bytes=56 * 1024 * 1024
        ),
    )(*(x.reshape(flat) for x in (query_field, key_field, value_field, output_grad)))
    outs = pl.pallas_call(
        copy_kernel,
        out_shape=[jax.ShapeDtypeStruct(flat, F32)] * 3,
        in_specs=[pl.BlockSpec(memory_space=pltpu.VMEM)] * 3,
        out_specs=[pl.BlockSpec(memory_space=pltpu.VMEM)] * 3,
    )(*outs)
    return tuple(x.reshape(frames, rows, cols, channels) for x in outs)


def solution(mesh):
    spec = P(None, "ha", "wa", None)
    return jax.shard_map(
        body, mesh=mesh, in_specs=(spec,) * 4, out_specs=(spec,) * 3, check_vma=False,
    )
```

```python
import jax
import jax.numpy as jnp
from jax import lax
from jax.experimental import pallas as pl
from jax.experimental.pallas import tpu as pltpu
from jax.sharding import PartitionSpec as P

MESH = pl.DeviceIdType.MESH
F32 = jnp.float32
BF16 = jnp.bfloat16
DIM = 128
SCALE = DIM ** -0.5
LOW = -1e30
CELLS = 128
KEYS = 3 * CELLS
HALF = 4 * CELLS


def halves(x):
    hi = x.astype(BF16)
    return hi, (x - hi.astype(F32)).astype(BF16)


def thirds(x):
    hi = x.astype(BF16)
    rest = x - hi.astype(F32)
    mid = rest.astype(BF16)
    return hi, mid, (rest - mid.astype(F32)).astype(BF16)


def dot(a, b, dims):
    return lax.dot_general(a, b, (dims, ((), ())), preferred_element_type=F32)


def kernel(
    q_in, k_in, v_in, g_in, dq_out, dk_out, dv_out,
    raw, kvb, qb, kp, lv, rq, ro, wbuf, dbuf, rel, st, sall, gst, dqt, dqs, dqr, own, halo, yret, zret,
    in_sem, near_sem, far_sem, y_sem, zq_sem, xq_sem, diag_sem, sibq_sem, rel_sem, stat_sem,
    yr_sem, zr_sem, dqs_sem, dq_sem,
):
    ha, wa = lax.axis_index("ha"), lax.axis_index("wa")
    row, xl = ha // 2, ha % 2
    core = wa % 2
    chip = wa // 2
    zp = chip % 2
    tile = chip // 2
    side = 2 * zp - 1
    up = 2 * xl - 1

    sib_id = (ha, wa + 1 - 2 * core)
    near_id = (ha, (wa + 2 * side + 32) % 32)
    far_to = (ha, (wa - 4 * side + 32) % 32)
    far_from = (ha, (wa + 4 * side + 32) % 32)
    zpair = (ha, wa - 2 * side)
    xpair = (ha - up, wa)
    diag = (ha - up, wa - 2 * side)
    y_to = ((ha + 2 * up + 8) % 8, wa)
    y_from = ((ha - 2 * up + 8) % 8, wa)

    side_in = jnp.where(zp == 0, tile > 0, tile < 7)
    far_out = jnp.where(zp == 0, tile < 7, tile > 0)
    y_out = jnp.where(xl == 1, row < 3, row > 0)
    y_in = jnp.where(xl == 1, row > 0, row < 3)

    barrier = pltpu.get_barrier_semaphore()
    flip = 1 - 2 * core
    group = (diag, zpair, xpair, (ha - up, wa - 2 * side + flip), (ha, wa - 2 * side + flip), (ha - up, wa + flip), sib_id)
    partners = group + (near_id, far_to, far_from, y_to, y_from)
    for device in partners:
        pl.semaphore_signal(barrier, inc=1, device_id=device, device_id_type=MESH)

    place8 = chip % 8
    crossing = (place8 < 2) | (place8 > 5)
    to_relay = (chip == 6) | (chip == 9)
    relay = (chip == 14) | (chip == 1)
    back_to = (chip == 8) | (chip == 7)
    back_relay = (chip == 0) | (chip == 15)
    cross_id = (ha, (wa + 16) % 32)
    jump_id = (ha, (wa + 12 * jnp.where(place8 < 4, 1, -1) + 32) % 32)

    @pl.when(crossing)
    def _():
        pl.semaphore_signal(barrier, inc=1, device_id=cross_id, device_id_type=MESH)
        pl.semaphore_signal(barrier, inc=1, device_id=jump_id, device_id_type=MESH)

    loads = [
        pltpu.make_async_copy(ref, raw.at[i], in_sem.at[i]) for i, ref in enumerate((k_in, v_in, q_in, g_in))
    ]
    for load in loads:
        load.start()

    def arrange(h, arrays):
        for i in arrays:
            part = raw[i, :, :, h * DIM:(h + 1) * DIM].reshape(CELLS, DIM)
            if i < 2:
                kvb[h, 0, 0, i] = part
            else:
                qb[h, xl, zp, core, i - 2] = part

    for load in loads:
        load.wait()
    arrange(0, range(4))
    extra = jnp.where(crossing, 2, 0)
    pl.semaphore_wait(barrier, len(partners) + extra)

    def remote(src, dst, sems, index, device):
        return pltpu.make_async_remote_copy(
            src_ref=src, dst_ref=dst, send_sem=sems.at[(0,) + index], recv_sem=sems.at[(1,) + index],
            device_id=device, device_id_type=MESH,
        )

    def near_copy(h, kv):
        return remote(kvb.at[h, 0, 0, kv], kvb.at[h, 0, 1, kv], near_sem, (h, kv), near_id)

    def far_copy(h, kv):
        return remote(kvb.at[h, 0, 0, kv], kvb.at[h, 0, 2, kv], far_sem, (h, kv), far_to)

    def relay_copy(h, kv):
        return remote(kvb.at[h, 0, 0, kv], rel.at[h, kv], rel_sem, (h, kv), cross_id)

    def jump_copy(h, kv):
        return remote(rel.at[h, kv], kvb.at[h, 0, 2, kv], far_sem, (h, kv), jump_id)

    def y_copy(h, unit, kv):
        return remote(kvb.at[h, 0, unit, kv], kvb.at[h, 1, unit, kv], y_sem, (h, unit, kv), y_to)

    def q_copy(h, half, place, part, sems, device):
        block = qb.at[h, half, place, core, part]
        return remote(block, block, sems, (h, part), device)

    def zq_copy(h, part):
        return q_copy(h, xl, zp, part, zq_sem, zpair)

    def xq_copy(h, part):
        return q_copy(h, xl, zp, part, xq_sem, xpair)

    def diag_by_z(h, part):
        return q_copy(h, 1 - xl, zp, part, diag_sem, zpair)

    def slot_place(slot):
        return xl + (slot // 2) * (1 - 2 * xl), zp + (slot % 2) * (1 - 2 * zp)

    def sib_copy(h, slot):
        half, place = slot_place(slot)
        block = qb.at[h, half, place, core]
        return remote(block, block, sibq_sem, (h, slot), sib_id)

    def y_sends(h):
        @pl.when(y_out)
        def _():
            y_copy(h, 0, 0).start()
            y_copy(h, 0, 1).start()

    def x_sends(h):
        for part in (1, 0):
            xq_copy(h, part).start()
        sib_copy(h, 0).start()

    def z_sends(h):
        for part in range(2):
            @pl.when(side_in)
            def _():
                near_copy(h, part).start()

            @pl.when(to_relay)
            def _():
                relay_copy(h, part).start()

            @pl.when(far_out & jnp.logical_not(to_relay))
            def _():
                far_copy(h, part).start()

            zq_copy(h, part).start()

    def pass_keys(h, kv):
        @pl.when(relay)
        def _():
            relay_copy(h, kv).wait_recv()
            jump_copy(h, kv).start()

        @pl.when(side_in)
        def _():
            near_copy(h, kv).wait_recv()

            @pl.when(y_out)
            def _():
                y_copy(h, 1, kv).start()

            far_copy(h, kv).wait_recv()

            @pl.when(y_out)
            def _():
                y_copy(h, 2, kv).start()

    def pass_queries(h):
        xq_copy(h, 1).wait_recv()
        diag_by_z(h, 1).start()
        zq_copy(h, 0).wait_recv()
        xq_copy(h, 0).wait_recv()
        sib_copy(h, 2).start()
        diag_by_z(h, 0).start()

    def last_pass(h):
        pass_keys(h, 1)
        zq_copy(h, 1).wait_recv()
        sib_copy(h, 1).start()

    def last_queries(h):
        for part in range(2):
            diag_by_z(h, part).wait_recv()
        sib_copy(h, 3).start()

    def prepare_queries(h, low):
        def one(slot, c):
            sib_copy(h, slot).wait_recv()
            half, place = slot_place(slot)
            for blk in range(2):
                q1, q2, q3 = thirds(qb[h, half, place, blk, 0] * SCALE)
                o1, o2 = halves(qb[h, half, place, blk, 1])
                rows = pl.ds(pl.multiple_of(place * (2 * CELLS) + blk * CELLS, CELLS), CELLS)
                for i, part in enumerate((q1, q1, q2, q2, q3, q1)):
                    rq[h, half, rows, i * DIM:(i + 1) * DIM] = part
                for i, part in enumerate((o1, o1, o2, o2)):
                    ro[h, half, rows, i * DIM:(i + 1) * DIM] = part
            return c

        lax.fori_loop(low, low + 2, one, 0)

    def prepare_keys(h, line):
        for unit in range(3):
            rows = slice(unit * CELLS, (unit + 1) * CELLS)
            k1, k2, k3 = thirds(kvb[h, line, unit, 0])
            v1, v2 = halves(kvb[h, line, unit, 1])
            for i, part in enumerate((k1, k2, k1, k2, k1, k3)):
                kp[2 * h + line, rows, i * DIM:(i + 1) * DIM] = part
            for i, part in enumerate((v1, v2, v1, v2)):
                lv[rows, i * DIM:(i + 1) * DIM] = part

    far_keys = lax.broadcasted_iota(jnp.int32, (KEYS, 1), 0) >= CELLS
    bias = jnp.where(far_keys, jnp.where(side_in, 0.0, LOW), 0.0)

    def forward_block(h, k, line, half):
        index = 3 * h + k
        scores = dot(kp[2 * h + line], rq[h, half], ((1,), (1,))) + bias
        dprobs = dot(lv[...], ro[h, half], ((1,), (1,)))
        peak = jnp.max(scores, axis=0, keepdims=True)
        weights = jnp.exp(scores - peak)
        wbuf[index] = weights
        dbuf[index] = dprobs
        st[index, 0:1] = peak
        st[index, 1:2] = jnp.sum(weights, axis=0, keepdims=True)
        st[index, 2:3] = jnp.sum(weights * dprobs, axis=0, keepdims=True)

    def forward(h, before):
        def one(step, c):
            for i in range(3):
                @pl.when(step == i)
                def _():
                    before[i]()

            half = jnp.where(step == 0, xl, 1 - xl)
            line = step // 2
            here = (step < 2) | y_in

            @pl.when(here & (step != 1))
            def _():
                @pl.when(step == 2)
                def _():
                    for kv in range(2):
                        y_copy(h, 0, kv).wait_recv()

                        @pl.when(side_in)
                        def _():
                            y_copy(h, 1, kv).wait_recv()
                            y_copy(h, 2, kv).wait_recv()

                prepare_keys(h, line)

            @pl.when(here)
            def _():
                forward_block(h, step, line, half)

            @pl.when(jnp.logical_not(here))
            def _():
                st[3 * h + 2, 0:1] = jnp.full((1, HALF), LOW, F32)
                st[3 * h + 2, 1:3] = jnp.zeros((2, HALF), F32)

            return c

        lax.fori_loop(0, 3, one, 0)

    me = 4 * xl + 2 * zp + core

    def merge(triples):
        peak = triples[0][0]
        for p, _, _ in triples[1:]:
            peak = jnp.maximum(peak, p)
        total = jnp.zeros_like(peak)
        center = jnp.zeros_like(peak)
        for p, s, c in triples:
            factor = jnp.exp(p - peak)
            total += s * factor
            center += c * factor
        return peak, total, center

    def triple(ref, base):
        return tuple(ref[base + i:base + i + 1] for i in range(3))

    def stat_copy(h, which):
        place = sall.at[h, me]
        return remote(place, place, stat_sem, (h, which), group[which])

    def start_stats(h):
        merged = (triple(st.at[3 * h], 0), merge([triple(st.at[3 * h + 1], 0), triple(st.at[3 * h + 2], 0)]))
        for half in range(2):
            for i in range(3):
                value = jnp.where(half == xl, merged[0][i], merged[1][i])
                sall[h, me, 3 * half + i:3 * half + i + 1] = value
        sall[h, me, 6:8] = jnp.zeros((2, HALF), F32)
        for which in range(7):
            stat_copy(h, which).start()

    def end_stats(h):
        for which in range(7):
            stat_copy(h, which).wait_recv()
        for half in range(2):
            peak, total, center = merge([triple(sall.at[h, i], 3 * half) for i in range(8)])
            inverse = 1.0 / total
            gst[h, half, 0:1] = peak
            gst[h, half, 1:2] = inverse
            gst[h, half, 2:3] = center * inverse

    def backward_block(h, k, line, half, give):
        index = 3 * h + k
        alpha = jnp.exp(st[index, 0:1] - gst[h, half, 0:1]) * gst[h, half, 1:2]
        probs = wbuf[index] * alpha
        dscores = probs * (dbuf[index] - gst[h, half, 2:3])
        p1, p2 = halves(probs)
        s1, s2 = halves(dscores)
        o12 = ro[h, half, :, DIM:3 * DIM]
        q12 = rq[h, half, :, DIM:3 * DIM]
        k12 = kp[2 * h + line, :, 0:2 * DIM].T
        dv = dot(p1, o12, ((1,), (0,))) + dot(p2, o12, ((1,), (0,)))
        dk = dot(s1, q12, ((1,), (0,))) + dot(s2, q12, ((1,), (0,)))
        dq = dot(jnp.concatenate([k12, k12], axis=1), jnp.concatenate([s1, s2], axis=0), ((1,), (0,)))
        dq = dq[:DIM] + dq[DIM:]
        for place in range(2):
            for blk in range(2):
                at = (2 * place + blk) * CELLS
                dqt[h, half, place, blk] += dq[:, at:at + CELLS]
        give(1, dv[:, :DIM] + dv[:, DIM:])
        give(0, dk[:, :DIM] + dk[:, DIM:])

    def yr_copy(h, unit, kind):
        return remote(halo.at[h, unit, kind], yret.at[h, unit, kind], yr_sem, (h, unit, kind), y_from)

    def dqs_copy(h):
        return remote(dqt.at[h, :, :, 1 - core], dqs.at[h], dqs_sem, (h,), sib_id)

    def backward(h):
        dqt[h] = jnp.zeros(dqt.shape[1:], F32)
        own[h] = jnp.zeros(own.shape[1:], F32)

        def one(turn, c):
            step = 2 - turn

            @pl.when((step < 2) | y_in)
            def _():
                half = jnp.where(step == 0, xl, 1 - xl)

                def give(kind, value):
                    @pl.when(step == 2)
                    def _():
                        for unit in range(3):
                            halo[h, unit, kind] = value[unit * CELLS:(unit + 1) * CELLS]

                        @pl.when(side_in)
                        def _():
                            yr_copy(h, 2, kind).start()
                            yr_copy(h, 1, kind).start()

                        if kind == 0:
                            yr_copy(h, 0, 0).start()
                            yr_copy(h, 0, 1).start()

                    @pl.when(step < 2)
                    def _():
                        for unit in range(3):
                            own[h, unit, kind] += value[unit * CELLS:(unit + 1) * CELLS]

                backward_block(h, step, step // 2, half, give)

            return c

        lax.fori_loop(0, 3, one, 0)
        dqs_copy(h).start()

    def dq_copy(h, which):
        device = (xpair, zpair, diag)[which]
        half, place = ((1 - xl, zp), (xl, 1 - zp), (1 - xl, 1 - zp))[which]
        return remote(dqt.at[h, half, place, core], dqr.at[h, which], dq_sem, (h, which), device)

    def share_dq(h):
        dqs_copy(h).wait_recv()
        for half in range(2):
            for place in range(2):
                dqt[h, half, place, core] += dqs[h, half, place]
        for which in range(3):
            dq_copy(h, which).start()

    def zr_copy(h, which, kind):
        device = (near_id, far_from)[which]
        return remote(own.at[h, 1 + which, kind], zret.at[h, which, kind], zr_sem, (h, which, kind), device)

    def back_copy(h, kind):
        return remote(own.at[h, 2, kind], rel.at[h, kind], rel_sem, (h, kind), cross_id)

    def back_jump(h, kind):
        return remote(rel.at[h, kind], zret.at[h, 1, kind], zr_sem, (h, 1, kind), jump_id)

    def relay_back(h):
        @pl.when(back_relay)
        def _():
            for kind in (1, 0):
                back_copy(h, kind).wait_recv()
                back_jump(h, kind).start()

    def pass_back(h):
        for kind in (1, 0):
            for which in (1, 0):
                @pl.when(side_in)
                def _():
                    @pl.when(y_out)
                    def _():
                        yr_copy(h, 1 + which, kind).wait_recv()
                        own[h, 1 + which, kind] += yret[h, 1 + which, kind]

                    if which == 0:
                        zr_copy(h, 0, kind).start()
                    else:
                        @pl.when(back_to)
                        def _():
                            back_copy(h, kind).start()

                        @pl.when(jnp.logical_not(back_to))
                        def _():
                            zr_copy(h, 1, kind).start()

    def finish(h):
        lanes = slice(h * DIM, (h + 1) * DIM)
        for which in range(3):
            dq_copy(h, which).wait_recv()
        dq = dqt[h, xl, zp, core] + dqr[h, 0] + dqr[h, 1] + dqr[h, 2]
        dq_out[:, :, lanes] = (dq.T * SCALE).reshape(32, 4, DIM)

        @pl.when(y_out)
        def _():
            yr_copy(h, 0, 0).wait_recv()
            yr_copy(h, 0, 1).wait_recv()
            own[h, 0] += yret[h, 0]

        @pl.when(far_out)
        def _():
            zr_copy(h, 1, 0).wait_recv()
            zr_copy(h, 1, 1).wait_recv()
            own[h, 0] += zret[h, 1]

        @pl.when(side_in)
        def _():
            zr_copy(h, 0, 0).wait_recv()
            zr_copy(h, 0, 1).wait_recv()
            own[h, 0] += zret[h, 0]

        dk_out[:, :, lanes] = own[h, 0, 0].reshape(32, 4, DIM)
        dv_out[:, :, lanes] = own[h, 0, 1].reshape(32, 4, DIM)

    def all_left(h):
        for part in range(2):
            @pl.when(y_out)
            def _():
                y_copy(h, 0, part).wait_send()

                @pl.when(side_in)
                def _():
                    y_copy(h, 1, part).wait_send()
                    y_copy(h, 2, part).wait_send()

            @pl.when(side_in)
            def _():
                near_copy(h, part).wait_send()
                zr_copy(h, 0, part).wait_send()

            @pl.when((side_in & jnp.logical_not(back_to)) | back_relay)
            def _():
                zr_copy(h, 1, part).wait_send()

            @pl.when(to_relay | back_to)
            def _():
                relay_copy(h, part).wait_send()

            @pl.when((far_out & jnp.logical_not(to_relay)) | relay)
            def _():
                far_copy(h, part).wait_send()

            zq_copy(h, part).wait_send()
            xq_copy(h, part).wait_send()
            diag_by_z(h, part).wait_send()

        @pl.when(y_in)
        def _():
            for kind in range(2):
                yr_copy(h, 0, kind).wait_send()

                @pl.when(side_in)
                def _():
                    yr_copy(h, 1, kind).wait_send()
                    yr_copy(h, 2, kind).wait_send()

        for slot in range(4):
            sib_copy(h, slot).wait_send()
        dqs_copy(h).wait_send()
        for which in range(3):
            dq_copy(h, which).wait_send()
        for which in range(7):
            stat_copy(h, which).wait_send()

    y_sends(0)
    z_sends(0)
    x_sends(0)
    arrange(1, range(4))

    @pl.when(jnp.logical_not(side_in))
    def _():
        for h in range(2):
            for line in range(2):
                kvb[h, line, 1:3] = jnp.zeros((2, 2, CELLS, DIM), F32)

    def head0_start():
        pass_keys(0, 0)
        pass_queries(0)
        last_pass(0)
        z_sends(1)
        prepare_queries(0, 0)

    def head0_other():
        y_sends(1)
        x_sends(1)
        last_queries(0)
        prepare_queries(0, 2)

    def head0_halo():
        pass_keys(1, 0)

    def head1_start():
        prepare_queries(1, 0)

    def head1_other():
        end_stats(0)
        backward(0)
        last_queries(1)
        share_dq(0)
        prepare_queries(1, 2)

    def head1_halo():
        pass

    forward(0, (head0_start, head0_other, head0_halo))
    start_stats(0)
    pass_queries(1)
    last_pass(1)
    forward(1, (head1_start, head1_other, head1_halo))
    start_stats(1)
    pass_back(0)
    end_stats(1)
    backward(1)
    relay_back(0)
    share_dq(1)
    finish(0)
    pass_back(1)
    relay_back(1)
    finish(1)
    all_left(0)
    all_left(1)


def copy_kernel(*refs):
    for i in range(3):
        refs[3 + i][...] = refs[i][...]


def body(query_field, key_field, value_field, output_grad):
    frames, rows, cols, channels = query_field.shape
    flat = (frames * rows, cols, channels)

    def sems(*shape):
        return pltpu.SemaphoreType.DMA((2, 2) + shape)

    outs = pl.pallas_call(
        kernel,
        out_shape=[jax.ShapeDtypeStruct(flat, F32)] * 3,
        in_specs=[pl.BlockSpec(memory_space=pl.ANY)] * 4,
        out_specs=[pl.BlockSpec(memory_space=pltpu.VMEM)] * 3,
        scratch_shapes=[
            pltpu.VMEM((4,) + flat, F32),
            pltpu.VMEM((2, 2, 3, 2, CELLS, DIM), F32),
            pltpu.VMEM((2, 2, 2, 2, 2, CELLS, DIM), F32),
            pltpu.VMEM((4, KEYS, 6 * DIM), BF16),
            pltpu.VMEM((KEYS, 4 * DIM), BF16),
            pltpu.VMEM((2, 2, HALF, 6 * DIM), BF16),
            pltpu.VMEM((2, 2, HALF, 4 * DIM), BF16),
            pltpu.VMEM((6, KEYS, HALF), F32),
            pltpu.VMEM((6, KEYS, HALF), F32),
            pltpu.VMEM((2, 2, CELLS, DIM), F32),
            pltpu.VMEM((6, 8, HALF), F32),
            pltpu.VMEM((2, 8, 8, HALF), F32),
            pltpu.VMEM((2, 2, 8, HALF), F32),
            pltpu.VMEM((2, 2, 2, 2, DIM, CELLS), F32),
            pltpu.VMEM((2, 2, 2, DIM, CELLS), F32),
            pltpu.VMEM((2, 3, DIM, CELLS), F32),
            pltpu.VMEM((2, 3, 2, CELLS, DIM), F32),
            pltpu.VMEM((2, 3, 2, CELLS, DIM), F32),
            pltpu.VMEM((2, 3, 2, CELLS, DIM), F32),
            pltpu.VMEM((2, 2, 2, CELLS, DIM), F32),
            pltpu.SemaphoreType.DMA((4,)),
            sems(2), sems(2), sems(3, 2), sems(2), sems(2), sems(2), sems(4), sems(2), sems(7),
            sems(3, 2), sems(2, 2), sems(), sems(3),
        ],
        compiler_params=pltpu.CompilerParams(
            collective_id=0, has_side_effects=True, vmem_limit_bytes=56 * 1024 * 1024
        ),
    )(*(x.reshape(flat) for x in (query_field, key_field, value_field, output_grad)))
    outs = pl.pallas_call(
        copy_kernel,
        out_shape=[jax.ShapeDtypeStruct(flat, F32)] * 3,
        in_specs=[pl.BlockSpec(memory_space=pltpu.VMEM)] * 3,
        out_specs=[pl.BlockSpec(memory_space=pltpu.VMEM)] * 3,
    )(*outs)
    return tuple(x.reshape(frames, rows, cols, channels) for x in outs)


def solution(mesh):
    spec = P(None, "ha", "wa", None)
    return jax.shard_map(
        body, mesh=mesh, in_specs=(spec,) * 4, out_specs=(spec,) * 3, check_vma=False,
    )
```

```python
import jax
import jax.numpy as jnp
from jax import lax
from jax.experimental import pallas as pl
from jax.experimental.pallas import tpu as pltpu
from jax.sharding import PartitionSpec as P

MESH = pl.DeviceIdType.MESH
F32 = jnp.float32
BF16 = jnp.bfloat16
DIM = 128
SCALE = DIM ** -0.5
LOW = -1e30
CELLS = 128
KEYS = 3 * CELLS
HALF = 4 * CELLS


def halves(x):
    hi = x.astype(BF16)
    return hi, (x - hi.astype(F32)).astype(BF16)


def thirds(x):
    hi = x.astype(BF16)
    rest = x - hi.astype(F32)
    mid = rest.astype(BF16)
    return hi, mid, (rest - mid.astype(F32)).astype(BF16)


def dot(a, b, dims):
    return lax.dot_general(a, b, (dims, ((), ())), preferred_element_type=F32)


def kernel(
    q_in, k_in, v_in, g_in, dq_out, dk_out, dv_out,
    raw, kvb, qb, kp, lv, rq, ro, wbuf, dbuf, rel, st, sall, gst, dqt, dqs, dqr, own, halo, yret, zret,
    in_sem, near_sem, far_sem, y_sem, zq_sem, xq_sem, diag_sem, sibq_sem, rel_sem, stat_sem,
    yr_sem, zr_sem, dqs_sem, dq_sem,
):
    ha, wa = lax.axis_index("ha"), lax.axis_index("wa")
    row, xl = ha // 2, ha % 2
    core = wa % 2
    chip = wa // 2
    zp = chip % 2
    tile = chip // 2
    side = 2 * zp - 1
    up = 2 * xl - 1

    sib_id = (ha, wa + 1 - 2 * core)
    near_id = (ha, (wa + 2 * side + 32) % 32)
    far_to = (ha, (wa - 4 * side + 32) % 32)
    far_from = (ha, (wa + 4 * side + 32) % 32)
    zpair = (ha, wa - 2 * side)
    xpair = (ha - up, wa)
    diag = (ha - up, wa - 2 * side)
    y_to = ((ha + 2 * up + 8) % 8, wa)
    y_from = ((ha - 2 * up + 8) % 8, wa)

    side_in = jnp.where(zp == 0, tile > 0, tile < 7)
    far_out = jnp.where(zp == 0, tile < 7, tile > 0)
    y_out = jnp.where(xl == 1, row < 3, row > 0)
    y_in = jnp.where(xl == 1, row > 0, row < 3)

    barrier = pltpu.get_barrier_semaphore()
    flip = 1 - 2 * core
    group = (diag, zpair, xpair, (ha - up, wa - 2 * side + flip), (ha, wa - 2 * side + flip), (ha - up, wa + flip), sib_id)
    partners = group + (near_id, far_to, far_from, y_to, y_from)
    for device in partners:
        pl.semaphore_signal(barrier, inc=1, device_id=device, device_id_type=MESH)

    to_relay = (chip == 6) | (chip == 9)
    relay = (chip == 14) | (chip == 1)
    from_relay = (chip == 8) | (chip == 7)
    turn = jnp.where((chip == 6) | (chip == 1), 1, -1)
    jump = jnp.where((chip == 1) | (chip == 8), 1, -1)
    cross_id = (ha, (wa + 16 * turn + 32) % 32)
    jump_id = (ha, (wa + 12 * jump + 32) % 32)

    @pl.when(to_relay | relay)
    def _():
        pl.semaphore_signal(barrier, inc=1, device_id=cross_id, device_id_type=MESH)

    @pl.when(relay | from_relay)
    def _():
        pl.semaphore_signal(barrier, inc=1, device_id=jump_id, device_id_type=MESH)

    loads = [
        pltpu.make_async_copy(ref, raw.at[i], in_sem.at[i]) for i, ref in enumerate((k_in, v_in, q_in, g_in))
    ]
    for load in loads:
        load.start()

    def arrange(h, arrays):
        for i in arrays:
            part = raw[i, :, :, h * DIM:(h + 1) * DIM].reshape(CELLS, DIM)
            if i < 2:
                kvb[h, 0, 0, i] = part
            else:
                qb[h, xl, zp, core, i - 2] = part

    for load in loads:
        load.wait()
    arrange(0, range(4))
    extra = jnp.where(relay, 2, jnp.where(to_relay | from_relay, 1, 0))
    pl.semaphore_wait(barrier, len(partners) + extra)

    def remote(src, dst, sems, index, device):
        return pltpu.make_async_remote_copy(
            src_ref=src, dst_ref=dst, send_sem=sems.at[(0,) + index], recv_sem=sems.at[(1,) + index],
            device_id=device, device_id_type=MESH,
        )

    def near_copy(h, kv):
        return remote(kvb.at[h, 0, 0, kv], kvb.at[h, 0, 1, kv], near_sem, (h, kv), near_id)

    def far_copy(h, kv):
        return remote(kvb.at[h, 0, 0, kv], kvb.at[h, 0, 2, kv], far_sem, (h, kv), far_to)

    def relay_copy(h, kv):
        return remote(kvb.at[h, 0, 0, kv], rel.at[h, kv], rel_sem, (h, kv), cross_id)

    def jump_copy(h, kv):
        return remote(rel.at[h, kv], kvb.at[h, 0, 2, kv], far_sem, (h, kv), jump_id)

    def y_copy(h, unit, kv):
        return remote(kvb.at[h, 0, unit, kv], kvb.at[h, 1, unit, kv], y_sem, (h, unit, kv), y_to)

    def q_copy(h, half, place, part, sems, device):
        block = qb.at[h, half, place, core, part]
        return remote(block, block, sems, (h, part), device)

    def zq_copy(h, part):
        return q_copy(h, xl, zp, part, zq_sem, zpair)

    def xq_copy(h, part):
        return q_copy(h, xl, zp, part, xq_sem, xpair)

    def diag_by_z(h, part):
        return q_copy(h, 1 - xl, zp, part, diag_sem, zpair)

    def slot_place(slot):
        return xl + (slot // 2) * (1 - 2 * xl), zp + (slot % 2) * (1 - 2 * zp)

    def sib_copy(h, slot):
        half, place = slot_place(slot)
        block = qb.at[h, half, place, core]
        return remote(block, block, sibq_sem, (h, slot), sib_id)

    def y_sends(h):
        @pl.when(y_out)
        def _():
            y_copy(h, 0, 0).start()
            y_copy(h, 0, 1).start()

    def x_sends(h):
        for part in (1, 0):
            xq_copy(h, part).start()
        sib_copy(h, 0).start()

    def z_sends(h):
        for part in range(2):
            @pl.when(side_in)
            def _():
                near_copy(h, part).start()

            @pl.when(to_relay)
            def _():
                relay_copy(h, part).start()

            @pl.when(far_out & jnp.logical_not(to_relay))
            def _():
                far_copy(h, part).start()

            zq_copy(h, part).start()

    def pass_keys(h, kv):
        @pl.when(relay)
        def _():
            relay_copy(h, kv).wait_recv()
            jump_copy(h, kv).start()

        @pl.when(side_in)
        def _():
            near_copy(h, kv).wait_recv()

            @pl.when(y_out)
            def _():
                y_copy(h, 1, kv).start()

            far_copy(h, kv).wait_recv()

            @pl.when(y_out)
            def _():
                y_copy(h, 2, kv).start()

    def pass_queries(h):
        xq_copy(h, 1).wait_recv()
        diag_by_z(h, 1).start()
        zq_copy(h, 0).wait_recv()
        xq_copy(h, 0).wait_recv()
        sib_copy(h, 2).start()
        diag_by_z(h, 0).start()

    def last_pass(h):
        pass_keys(h, 1)
        zq_copy(h, 1).wait_recv()
        sib_copy(h, 1).start()

    def last_queries(h):
        for part in range(2):
            diag_by_z(h, part).wait_recv()
        sib_copy(h, 3).start()

    def prepare_queries(h, low):
        def one(slot, c):
            sib_copy(h, slot).wait_recv()
            half, place = slot_place(slot)
            for blk in range(2):
                q1, q2, q3 = thirds(qb[h, half, place, blk, 0] * SCALE)
                o1, o2 = halves(qb[h, half, place, blk, 1])
                rows = pl.ds(pl.multiple_of(place * (2 * CELLS) + blk * CELLS, CELLS), CELLS)
                for i, part in enumerate((q1, q1, q2, q2, q3, q1)):
                    rq[h, half, rows, i * DIM:(i + 1) * DIM] = part
                for i, part in enumerate((o1, o1, o2, o2)):
                    ro[h, half, rows, i * DIM:(i + 1) * DIM] = part
            return c

        lax.fori_loop(low, low + 2, one, 0)

    def prepare_keys(h, line):
        for unit in range(3):
            rows = slice(unit * CELLS, (unit + 1) * CELLS)
            k1, k2, k3 = thirds(kvb[h, line, unit, 0])
            v1, v2 = halves(kvb[h, line, unit, 1])
            for i, part in enumerate((k1, k2, k1, k2, k1, k3)):
                kp[2 * h + line, rows, i * DIM:(i + 1) * DIM] = part
            for i, part in enumerate((v1, v2, v1, v2)):
                lv[rows, i * DIM:(i + 1) * DIM] = part

    far_keys = lax.broadcasted_iota(jnp.int32, (KEYS, 1), 0) >= CELLS
    bias = jnp.where(far_keys, jnp.where(side_in, 0.0, LOW), 0.0)

    def forward_block(h, k, line, half):
        index = 3 * h + k
        scores = dot(kp[2 * h + line], rq[h, half], ((1,), (1,))) + bias
        dprobs = dot(lv[...], ro[h, half], ((1,), (1,)))
        peak = jnp.max(scores, axis=0, keepdims=True)
        weights = jnp.exp(scores - peak)
        wbuf[index] = weights
        dbuf[index] = dprobs
        st[index, 0:1] = peak
        st[index, 1:2] = jnp.sum(weights, axis=0, keepdims=True)
        st[index, 2:3] = jnp.sum(weights * dprobs, axis=0, keepdims=True)

    def forward(h, before):
        def one(step, c):
            for i in range(3):
                @pl.when(step == i)
                def _():
                    before[i]()

            half = jnp.where(step == 0, xl, 1 - xl)
            line = step // 2
            here = (step < 2) | y_in

            @pl.when(here & (step != 1))
            def _():
                @pl.when(step == 2)
                def _():
                    for kv in range(2):
                        y_copy(h, 0, kv).wait_recv()

                        @pl.when(side_in)
                        def _():
                            y_copy(h, 1, kv).wait_recv()
                            y_copy(h, 2, kv).wait_recv()

                prepare_keys(h, line)

            @pl.when(here)
            def _():
                forward_block(h, step, line, half)

            @pl.when(jnp.logical_not(here))
            def _():
                st[3 * h + 2, 0:1] = jnp.full((1, HALF), LOW, F32)
                st[3 * h + 2, 1:3] = jnp.zeros((2, HALF), F32)

            return c

        lax.fori_loop(0, 3, one, 0)

    me = 4 * xl + 2 * zp + core

    def merge(triples):
        peak = triples[0][0]
        for p, _, _ in triples[1:]:
            peak = jnp.maximum(peak, p)
        total = jnp.zeros_like(peak)
        center = jnp.zeros_like(peak)
        for p, s, c in triples:
            factor = jnp.exp(p - peak)
            total += s * factor
            center += c * factor
        return peak, total, center

    def triple(ref, base):
        return tuple(ref[base + i:base + i + 1] for i in range(3))

    def stat_copy(h, which):
        place = sall.at[h, me]
        return remote(place, place, stat_sem, (h, which), group[which])

    def start_stats(h):
        merged = (triple(st.at[3 * h], 0), merge([triple(st.at[3 * h + 1], 0), triple(st.at[3 * h + 2], 0)]))
        for half in range(2):
            for i in range(3):
                value = jnp.where(half == xl, merged[0][i], merged[1][i])
                sall[h, me, 3 * half + i:3 * half + i + 1] = value
        sall[h, me, 6:8] = jnp.zeros((2, HALF), F32)
        for which in range(7):
            stat_copy(h, which).start()

    def end_stats(h):
        for which in range(7):
            stat_copy(h, which).wait_recv()
        for half in range(2):
            peak, total, center = merge([triple(sall.at[h, i], 3 * half) for i in range(8)])
            inverse = 1.0 / total
            gst[h, half, 0:1] = peak
            gst[h, half, 1:2] = inverse
            gst[h, half, 2:3] = center * inverse

    def backward_block(h, k, line, half, give):
        index = 3 * h + k
        alpha = jnp.exp(st[index, 0:1] - gst[h, half, 0:1]) * gst[h, half, 1:2]
        probs = wbuf[index] * alpha
        dscores = probs * (dbuf[index] - gst[h, half, 2:3])
        p1, p2 = halves(probs)
        s1, s2 = halves(dscores)
        o12 = ro[h, half, :, DIM:3 * DIM]
        q12 = rq[h, half, :, DIM:3 * DIM]
        k12 = kp[2 * h + line, :, 0:2 * DIM].T
        dv = dot(p1, o12, ((1,), (0,))) + dot(p2, o12, ((1,), (0,)))
        dk = dot(s1, q12, ((1,), (0,))) + dot(s2, q12, ((1,), (0,)))
        dq = dot(jnp.concatenate([k12, k12], axis=1), jnp.concatenate([s1, s2], axis=0), ((1,), (0,)))
        dq = dq[:DIM] + dq[DIM:]
        for place in range(2):
            for blk in range(2):
                at = (2 * place + blk) * CELLS
                dqt[h, half, place, blk] += dq[:, at:at + CELLS]
        give(1, dv[:, :DIM] + dv[:, DIM:])
        give(0, dk[:, :DIM] + dk[:, DIM:])

    def yr_copy(h, unit, kind):
        return remote(halo.at[h, unit, kind], yret.at[h, unit, kind], yr_sem, (h, unit, kind), y_from)

    def dqs_copy(h):
        return remote(dqt.at[h, :, :, 1 - core], dqs.at[h], dqs_sem, (h,), sib_id)

    def backward(h):
        def one(turn, c):
            step = 2 - turn

            @pl.when((step < 2) | y_in)
            def _():
                half = jnp.where(step == 0, xl, 1 - xl)

                def give(kind, value):
                    @pl.when(step == 2)
                    def _():
                        for unit in range(3):
                            halo[h, unit, kind] = value[unit * CELLS:(unit + 1) * CELLS]

                        @pl.when(side_in)
                        def _():
                            yr_copy(h, 2, kind).start()
                            yr_copy(h, 1, kind).start()

                        if kind == 0:
                            yr_copy(h, 0, 0).start()
                            yr_copy(h, 0, 1).start()

                    @pl.when(step < 2)
                    def _():
                        for unit in range(3):
                            own[h, unit, kind] += value[unit * CELLS:(unit + 1) * CELLS]

                backward_block(h, step, step // 2, half, give)

            return c

        lax.fori_loop(0, 3, one, 0)
        dqs_copy(h).start()

    def dq_copy(h, which):
        device = (xpair, zpair, diag)[which]
        half, place = ((1 - xl, zp), (xl, 1 - zp), (1 - xl, 1 - zp))[which]
        return remote(dqt.at[h, half, place, core], dqr.at[h, which], dq_sem, (h, which), device)

    def share_dq(h):
        dqs_copy(h).wait_recv()
        for half in range(2):
            for place in range(2):
                dqt[h, half, place, core] += dqs[h, half, place]
        for which in range(3):
            dq_copy(h, which).start()

    def zr_copy(h, which, kind):
        device = (near_id, far_from)[which]
        return remote(own.at[h, 1 + which, kind], zret.at[h, which, kind], zr_sem, (h, which, kind), device)

    def pass_back(h):
        for kind in (1, 0):
            for which in (1, 0):
                @pl.when(side_in)
                def _():
                    @pl.when(y_out)
                    def _():
                        yr_copy(h, 1 + which, kind).wait_recv()
                        own[h, 1 + which, kind] += yret[h, 1 + which, kind]

                    zr_copy(h, which, kind).start()

    def finish(h):
        lanes = slice(h * DIM, (h + 1) * DIM)
        for which in range(3):
            dq_copy(h, which).wait_recv()
        dq = dqt[h, xl, zp, core] + dqr[h, 0] + dqr[h, 1] + dqr[h, 2]
        dq_out[:, :, lanes] = (dq.T * SCALE).reshape(32, 4, DIM)

        @pl.when(y_out)
        def _():
            yr_copy(h, 0, 0).wait_recv()
            yr_copy(h, 0, 1).wait_recv()
            own[h, 0] += yret[h, 0]

        @pl.when(far_out)
        def _():
            zr_copy(h, 1, 0).wait_recv()
            zr_copy(h, 1, 1).wait_recv()
            own[h, 0] += zret[h, 1]

        @pl.when(side_in)
        def _():
            zr_copy(h, 0, 0).wait_recv()
            zr_copy(h, 0, 1).wait_recv()
            own[h, 0] += zret[h, 0]

        dk_out[:, :, lanes] = own[h, 0, 0].reshape(32, 4, DIM)
        dv_out[:, :, lanes] = own[h, 0, 1].reshape(32, 4, DIM)

    def all_left(h):
        for part in range(2):
            @pl.when(y_out)
            def _():
                y_copy(h, 0, part).wait_send()

                @pl.when(side_in)
                def _():
                    y_copy(h, 1, part).wait_send()
                    y_copy(h, 2, part).wait_send()

            @pl.when(side_in)
            def _():
                near_copy(h, part).wait_send()
                zr_copy(h, 0, part).wait_send()
                zr_copy(h, 1, part).wait_send()

            @pl.when(to_relay)
            def _():
                relay_copy(h, part).wait_send()

            @pl.when((far_out & jnp.logical_not(to_relay)) | relay)
            def _():
                far_copy(h, part).wait_send()

            zq_copy(h, part).wait_send()
            xq_copy(h, part).wait_send()
            diag_by_z(h, part).wait_send()

        @pl.when(y_in)
        def _():
            for kind in range(2):
                yr_copy(h, 0, kind).wait_send()

                @pl.when(side_in)
                def _():
                    yr_copy(h, 1, kind).wait_send()
                    yr_copy(h, 2, kind).wait_send()

        for slot in range(4):
            sib_copy(h, slot).wait_send()
        dqs_copy(h).wait_send()
        for which in range(3):
            dq_copy(h, which).wait_send()
        for which in range(7):
            stat_copy(h, which).wait_send()

    y_sends(0)
    z_sends(0)
    x_sends(0)
    arrange(1, range(4))
    dqt[...] = jnp.zeros(dqt.shape, F32)
    own[...] = jnp.zeros(own.shape, F32)

    @pl.when(jnp.logical_not(side_in))
    def _():
        for h in range(2):
            for line in range(2):
                kvb[h, line, 1:3] = jnp.zeros((2, 2, CELLS, DIM), F32)

    def head0_start():
        pass_keys(0, 0)
        pass_queries(0)
        last_pass(0)
        z_sends(1)
        prepare_queries(0, 0)

    def head0_other():
        y_sends(1)
        x_sends(1)
        last_queries(0)
        prepare_queries(0, 2)

    def head0_halo():
        pass_keys(1, 0)

    def head1_start():
        prepare_queries(1, 0)

    def head1_other():
        end_stats(0)
        backward(0)
        last_queries(1)
        share_dq(0)
        prepare_queries(1, 2)

    def head1_halo():
        pass

    forward(0, (head0_start, head0_other, head0_halo))
    start_stats(0)
    pass_queries(1)
    last_pass(1)
    forward(1, (head1_start, head1_other, head1_halo))
    start_stats(1)
    pass_back(0)
    end_stats(1)
    backward(1)
    share_dq(1)
    finish(0)
    pass_back(1)
    finish(1)
    all_left(0)
    all_left(1)


def copy_kernel(*refs):
    held, sems = refs[6:]
    pieces = [(i, pl.ds(8 * j, 8)) for j in range(4) for i in range(3)]
    ins = [
        pltpu.make_async_copy(refs[i].at[at], held.at[i, at], sems.at[0, n]) for n, (i, at) in enumerate(pieces)
    ]
    outs = [
        pltpu.make_async_copy(held.at[i, at], refs[3 + i].at[at], sems.at[1, n]) for n, (i, at) in enumerate(pieces)
    ]
    for copy in ins:
        copy.start()
    for first, second in zip(ins, outs):
        first.wait()
        second.start()
    for copy in outs:
        copy.wait()


def body(query_field, key_field, value_field, output_grad):
    frames, rows, cols, channels = query_field.shape
    flat = (frames * rows, cols, channels)

    def sems(*shape):
        return pltpu.SemaphoreType.DMA((2, 2) + shape)

    outs = pl.pallas_call(
        kernel,
        out_shape=[jax.ShapeDtypeStruct(flat, F32)] * 3,
        in_specs=[pl.BlockSpec(memory_space=pl.ANY)] * 4,
        out_specs=[pl.BlockSpec(memory_space=pltpu.VMEM)] * 3,
        scratch_shapes=[
            pltpu.VMEM((4,) + flat, F32),
            pltpu.VMEM((2, 2, 3, 2, CELLS, DIM), F32),
            pltpu.VMEM((2, 2, 2, 2, 2, CELLS, DIM), F32),
            pltpu.VMEM((4, KEYS, 6 * DIM), BF16),
            pltpu.VMEM((KEYS, 4 * DIM), BF16),
            pltpu.VMEM((2, 2, HALF, 6 * DIM), BF16),
            pltpu.VMEM((2, 2, HALF, 4 * DIM), BF16),
            pltpu.VMEM((6, KEYS, HALF), F32),
            pltpu.VMEM((6, KEYS, HALF), F32),
            pltpu.VMEM((2, 2, CELLS, DIM), F32),
            pltpu.VMEM((6, 8, HALF), F32),
            pltpu.VMEM((2, 8, 8, HALF), F32),
            pltpu.VMEM((2, 2, 8, HALF), F32),
            pltpu.VMEM((2, 2, 2, 2, DIM, CELLS), F32),
            pltpu.VMEM((2, 2, 2, DIM, CELLS), F32),
            pltpu.VMEM((2, 3, DIM, CELLS), F32),
            pltpu.VMEM((2, 3, 2, CELLS, DIM), F32),
            pltpu.VMEM((2, 3, 2, CELLS, DIM), F32),
            pltpu.VMEM((2, 3, 2, CELLS, DIM), F32),
            pltpu.VMEM((2, 2, 2, CELLS, DIM), F32),
            pltpu.SemaphoreType.DMA((4,)),
            sems(2), sems(2), sems(3, 2), sems(2), sems(2), sems(2), sems(4), sems(2), sems(7),
            sems(3, 2), sems(2, 2), sems(), sems(3),
        ],
        compiler_params=pltpu.CompilerParams(
            collective_id=0, has_side_effects=True, vmem_limit_bytes=56 * 1024 * 1024
        ),
    )(*(x.reshape(flat) for x in (query_field, key_field, value_field, output_grad)))
    outs = pl.pallas_call(
        copy_kernel,
        out_shape=[jax.ShapeDtypeStruct(flat, F32)] * 3,
        in_specs=[pl.BlockSpec(memory_space=pl.ANY)] * 3,
        out_specs=[pl.BlockSpec(memory_space=pl.ANY)] * 3,
        scratch_shapes=[pltpu.VMEM((3,) + flat, F32), pltpu.SemaphoreType.DMA((2, 12))],
    )(*outs)
    return tuple(x.reshape(frames, rows, cols, channels) for x in outs)


def solution(mesh):
    spec = P(None, "ha", "wa", None)
    return jax.shard_map(
        body, mesh=mesh, in_specs=(spec,) * 4, out_specs=(spec,) * 3, check_vma=False,
    )
```
